256 devices in a mesh: dp: 32 (over y, x, core), mp: 8 (over z).
Axes of the slice: x: 4, y: 4, z: 8, core: 2. Of those that a mesh axis runs over, the one named last changes fastest.
Arguments:
- feats: bfloat16 [32768, 2048], P('dp', 'mp'), may hold values from -6 to 6
- parent: int32 [32768], P('dp'), may hold values from 0 to 1022, as said below
- counts: int32 [32], replicated, may hold values from 1 to 1024, 16384 in all
- accepted: int32 [32768], P('dp'), may hold values 0 or 1
- cand_ids: int32 [32768, 8], P('dp'), may hold values from 0 to 128255, as said below
- target_probs: bfloat16 [32768, 8], P('dp'), may hold values from 0 to 1, as said below
- gain: bfloat16 [2048], P('mp'), may hold values from 0.5 to 2
- embed: bfloat16 [128256, 2048], P('dp', 'mp'), may hold values from -0.125 to 0.125
- proj: bfloat16 [2048, 2048], P(None, 'mp'), may hold values from -6 to 6
Outputs:
- new_proj: bfloat16 [2048, 2048], P(None, 'mp')
- loss: float32 [], replicated
The draws below stay inside these ranges and needn't reach their ends.
Inputs may be any that keep to these rules, and one draw needn't show every extreme that they name: parent of a row with local index i is a local index below i; the row of local index 0 names 0, and the row of local index 1023 names 1022. `cand_ids`: among the 8192 candidates of one group, at most 384 lie in any one block of 4008 consecutive ids starting at a multiple of 4008, and in every group some block holds exactly 384. `target_probs`: positive.
All inputs are finite; a program needn't handle non-finite values. No bound on the sum of `accepted` on one device may be relied on, other than what follows from the above.
Results may differ from the reference program's by a relative error of at most 0.008.
Values may be sent and summed in bfloat16 or wider, within the bound.
A program may use at most 128 MiB of HBM per device.

```python
import math
import jax
import jax.numpy as jnp
import numpy as np
from jax import lax

D = 2048
VOCAB = 128256
K = 8
NODE_DEV = 1024
NODES = 32768
GROUPS = 32
V_SHARD = 4008
N_DP = 32


def draw_parent(key, part):
    key = jax.random.fold_in(key, 5)
    local = jnp.arange(NODES, dtype=jnp.int32) % NODE_DEV
    picked = jax.random.randint(key, (NODES,), 0, jnp.maximum(local, 1)).astype(jnp.int32)
    return jnp.where(local == NODE_DEV - 1, NODE_DEV - 2, picked).astype(jnp.int32)


def draw_cand_ids(key, part):
    key = jax.random.fold_in(key, 11)
    per_group = NODE_DEV * K
    mean_load = per_group // N_DP
    half_load = mean_load // 2
    quarter = N_DP // 4

    def one_group(group_key):
        key_rank, key_shuffle, key_offset = jax.random.split(group_key, 3)
        ranking = jax.random.permutation(key_rank, N_DP)
        load = mean_load + jnp.where(ranking < quarter, half_load, jnp.where(ranking < 2 * quarter, -half_load, 0))
        bounds = jnp.cumsum(load)
        places = jnp.arange(per_group, dtype=jnp.int32)
        owners = jnp.sum((places[:, None] >= bounds[None, :]).astype(jnp.int32), axis=1)
        owners = jax.random.permutation(key_shuffle, owners)
        offsets = jax.random.randint(key_offset, (per_group,), 0, V_SHARD)
        return (owners * V_SHARD + offsets).reshape(NODE_DEV, K)
    group_keys = jax.random.split(key, N_DP)
    return jax.vmap(one_group)(group_keys).reshape(NODES, K).astype(jnp.int32)


def sharpness(low, high):
    row_group = (jnp.arange(NODES, dtype=jnp.int32) // NODE_DEV).astype(jnp.float32)
    frac = row_group / jnp.float32(max(GROUPS - 1, 1))
    return low * jnp.exp(frac * jnp.log(jnp.float32(high / low)))


def draw_target_probs(key, part):
    key = jax.random.fold_in(key, 17)
    spread = sharpness(0.7, 9.0)
    level = jax.random.uniform(key, (NODES, K), jnp.float32, 0.0, 1.0)
    return jnp.exp(-level * spread[:, None]).astype(jnp.bfloat16)


def touch_ends(values, own_key, least, largest):
    dims = values.shape
    index_at = [jax.random.randint(jax.random.fold_in(own_key, axis), (), 0, dims[axis]) for axis in range(len(dims))]
    values = values.at[tuple(index_at)].set(least)
    longest = dims.index(max(dims))
    index_at[longest] = (index_at[longest] + 1) % dims[longest]
    return values.at[tuple(index_at)].set(largest)


def block_scale(stream_key, dims, cuts, low, high):
    level = 1.0
    for dim, shards_of in cuts:
        steps = jax.random.uniform(jax.random.fold_in(jax.random.fold_in(stream_key, 6), dim), (shards_of,), jnp.float32, low / len(cuts), high / len(cuts))
        level = level * jnp.repeat(jnp.exp(steps), dims[dim] // shards_of).reshape((-1,) + (1,) * (len(dims) - 1 - dim))
    return level


def length_profile(amount, total, most, slope):
    loads = [(1 << 20) // math.isqrt(grade ** slope) + 1 for grade in range(2, amount + 1)]
    spare, holding = total - most - (amount - 1), [1] * (amount - 1)
    while spare > 0:
        candidates = [i for i in range(amount - 1) if holding[i] < most]
        mass, budget = sum([loads[i] for i in candidates]), spare
        for i in candidates:
            more = min(most - holding[i], max(1, budget * loads[i] // mass), spare)
            holding[i] = holding[i] + more
            spare = spare - more
    return np.array([most] + holding)


def uneven_parts(own_key, amount, total, bound, lean):
    if amount == 2:
        one = jax.random.randint(own_key, (), max(1, total - bound), min(bound, total - 1) + 1)
        return jnp.stack([one, total - one])
    tallies = jnp.asarray(length_profile(amount, total, bound, lean), jnp.int32)
    twos = (amount - 1) // 2
    giver, taker = tallies[1:1 + 2 * twos:2], tallies[2:2 + 2 * twos:2]
    room = jnp.minimum(giver - 1, bound - taker)
    passed = jax.random.randint(jax.random.fold_in(own_key, 1), (twos,), 0, 1 << 20) % (room + 1)
    tallies = tallies.at[1:1 + 2 * twos:2].set(giver - passed).at[2:2 + 2 * twos:2].set(taker + passed)
    return tallies[jax.random.permutation(jax.random.fold_in(own_key, 2), amount)]


def centred(rng, shape, width, limit, cuts=(), kind=jnp.bfloat16):
    drawn = jax.random.normal(rng, shape, jnp.float32) * width
    if len(cuts) > 0:
        drawn = block_scale(rng, shape, cuts, -0.22, 0.18) * drawn
    return jnp.clip(drawn, min=-limit, max=limit).astype(kind)


def setup_inputs(seed: int = 0) -> dict:
    key_of = jax.random.split(jax.random.key(seed), 10)
    return {
        "feats": centred(key_of[0], (NODES, D), 1.0, 6.0, ((0, 32), (1, 8))),
        "parent": draw_parent(jax.random.fold_in(key_of[9], 71), 0),
        "counts": uneven_parts(key_of[2], GROUPS, NODE_DEV * N_DP // 2, NODE_DEV, 2).astype(jnp.int32),
        "accepted": touch_ends((jax.random.randint(key_of[3], (NODES,), 0, 2) < 1).astype(jnp.int32), jax.random.fold_in(key_of[3], 1), 0, 1),
        "cand_ids": draw_cand_ids(jax.random.fold_in(key_of[9], 71), 0),
        "target_probs": draw_target_probs(jax.random.fold_in(key_of[9], 71), 0),
        "gain": jnp.clip(jnp.exp(math.log(2.0) - 1.3862944 * jax.random.uniform(key_of[6], (D,), jnp.float32) ** block_scale(key_of[6], (D,), ((0, 8),), -0.2, 0.2)), 0.5, 2.0).astype(jnp.bfloat16),
        "embed": centred(key_of[7], (VOCAB, D), D ** -0.5, 0.125, ((0, 32), (1, 8))),
        "proj": centred(key_of[8], (D, D), 1.0, 6.0, ((1, 8),)),
    }


def reference(feats, parent, counts, accepted, cand_ids, target_probs, gain, embed, proj):
    scale_in = 1.0 / jnp.sqrt(jnp.float32(D))
    gain_f = gain.astype(jnp.float32)

    def one_group(carry, index):
        grad_sum, num_sum, den_sum = carry
        start = (index * NODE_DEV).astype(jnp.int32)
        rows_x = lax.dynamic_slice_in_dim(feats, start, NODE_DEV, 0)
        parents = lax.dynamic_slice_in_dim(parent, start, NODE_DEV, 0)
        accept = lax.dynamic_slice_in_dim(accepted, start, NODE_DEV, 0)
        ids = lax.dynamic_slice_in_dim(cand_ids, start, NODE_DEV, 0)
        probs = lax.dynamic_slice_in_dim(target_probs, start, NODE_DEV, 0).astype(jnp.float32)
        mixed = (rows_x.astype(jnp.float32) + rows_x[parents].astype(jnp.float32)).astype(jnp.bfloat16)
        hidden = jnp.dot(mixed, proj, preferred_element_type=jnp.float32) * scale_in
        recip = lax.rsqrt(lax.optimization_barrier(jnp.mean(hidden * hidden, axis=1)) + 1e-05)
        normed = (hidden * recip[:, None] * gain_f).astype(jnp.bfloat16)
        cand_rows = embed[ids].astype(jnp.float32)
        scores = jnp.einsum('nkd,nd->nk', cand_rows, normed.astype(jnp.float32))
        logp = scores - jnp.log(lax.optimization_barrier(jnp.sum(jnp.exp(scores), axis=1, keepdims=True)))
        prob = jnp.exp(logp)
        target = probs / lax.optimization_barrier(jnp.sum(probs, axis=1, keepdims=True))
        kl_node = lax.optimization_barrier(jnp.sum(target * (jnp.log(target) - logp), axis=1))
        live = jnp.arange(NODE_DEV, dtype=jnp.int32) < counts[index]
        weight = jnp.where(live, 1 + accept, 0).astype(jnp.float32)
        grad_scores = weight[:, None] * (prob - target)
        dnormed = jnp.einsum('nk,nkd->nd', grad_scores, cand_rows)
        inner = lax.optimization_barrier(jnp.sum(dnormed * gain_f * hidden, axis=1))
        dhidden = (recip[:, None] * gain_f * dnormed - hidden * (recip ** 3 * inner / D)[:, None]).astype(jnp.bfloat16)
        grad_part = lax.dot_general(mixed, dhidden, (((0,), (0,)), ((), ())), preferred_element_type=jnp.float32) * scale_in
        return ((grad_sum + grad_part, num_sum + jnp.sum(weight * kl_node), den_sum + jnp.sum(weight)), None)
    init = (jnp.zeros((D, D), jnp.float32), jnp.float32(0.0), jnp.float32(0.0))
    (grad, num, den), _ = lax.scan(one_group, init, jnp.arange(GROUPS, dtype=jnp.int32))
    factor = lax.rsqrt(jnp.mean(grad * grad) + 1e-06)
    new_proj = (proj.astype(jnp.float32) - 0.5 * grad * factor).astype(jnp.bfloat16)
    return (new_proj, num / den)
```

```python
import functools
import jax
import jax.numpy as jnp
from jax import lax
from jax.experimental import pallas as pl
from jax.experimental.pallas import tpu as pltpu
from jax.sharding import PartitionSpec as P

MESH = pl.DeviceIdType.MESH
F32 = jnp.float32
BF16 = jnp.bfloat16
I32 = jnp.int32

CAP = 224
CAPL = 256


def dot(a, b):
    return jnp.dot(a, b, preferred_element_type=F32)


def dot_nt(a, b):
    return lax.dot_general(a, b, (((1,), (1,)), ((), ())), preferred_element_type=F32)


def one_hot(hit):
    return jnp.where(hit, 1.0, 0.0).astype(BF16)


def iota(shape, axis):
    return lax.broadcasted_iota(I32, shape, axis)


def step_kernel(
    nd, nz, full_rows,
    rowi, meta, feats, gain, embed, proj,
    out, stat,
    perm, mixed, metap, metar, mixp, mixr, live, metat,
    sendid, idr, rows_out, rows_in, whole, whole_t, hidden, ng,
    pick, pick_t, kmat, sc, zsend, zr, scaled, dn, dh,
    pair_out, pair_in, gown, rs_out, rs_in, gfull, ez_out, ez, dt_out, dt,
    meta_s, meta_r, mix_s, mix_r, id_s, id_r, row_s, row_r,
    zr_s, zr_r, zl_s, zl_r, zx_s, zx_r, pair_s, pair_r,
    rs_s, rs_r, ag_s, ag_r, fw_s, fw_r, ez_s, ez_r, dt_s, dt_r,
):
    me = lax.axis_index("dp")
    z = lax.axis_index("mp")
    nodes = feats.shape[0]
    width = feats.shape[1]
    slots = live.shape[0]
    share = nodes // nd
    core = lax.rem(me, 2)
    chip = lax.div(me, 2)
    chips = nd // 2
    sibling = me + 1 - 2 * core
    vocab = embed.shape[0]

    def copy(src, dst, ss, rs, d, zz):
        return pltpu.make_async_remote_copy(
            src_ref=src, dst_ref=dst, send_sem=ss, recv_sem=rs,
            device_id=(d, zz), device_id_type=MESH,
        )

    def nxt(i):
        return lax.rem(me + i, nd)

    def prv(i):
        return lax.rem(me - i + nd, nd)

    def loop(lo, hi, body):
        def wrapped(i, carry):
            body(i)
            return carry
        lax.fori_loop(lo, hi, wrapped, 0)

    def dp_copy(src, dst, ss, rs, d):
        return copy(src.at[d], dst.at[me], ss.at[d], rs.at[me], d, z)

    def dp_wait(src, dst, ss, rs, h):
        copy(src.at[h], dst.at[h], ss.at[h], rs.at[h], h, z).wait_recv()

    def dp_send_all(src, dst, ss, rs):
        loop(1, nd, lambda i: dp_copy(src, dst, ss, rs, nxt(i)).start())

    def dp_wait_all(src, dst, ss, rs):
        loop(1, nd, lambda i: dp_wait(src, dst, ss, rs, prv(i)))

    def dp_sent_all(src, dst, ss, rs):
        loop(1, nd, lambda i: dp_copy(src, dst, ss, rs, nxt(i)).wait_send())

    barrier = pltpu.get_barrier_semaphore()
    loop(1, nd, lambda i: pl.semaphore_signal(barrier, inc=1, device_id=(nxt(i), z), device_id_type=MESH))
    loop(1, nz, lambda i: pl.semaphore_signal(barrier, inc=1, device_id=(me, lax.rem(z + i, nz)), device_id_type=MESH))

    step = 128

    def perm_block(b):
        rows = pl.ds(b * step, step)
        e = one_hot(iota((step, nodes), 0) + b * step == rowi[0:1, :])
        perm[rows, :] = e
        metap[pl.ds(b * (step // share), step // share)] = (
            dot(e, meta[...]).astype(BF16).reshape(step // share, share, metap.shape[2])
        )

    loop(0, nodes // step, perm_block)
    pl.semaphore_wait(barrier, nd - 1 + nz - 1)
    dp_send_all(metap, metar, meta_s, meta_r)
    metar[me] = metap[me]

    def mix_block(b):
        rows = pl.ds(b * step, step)
        at = meta[rows, 33:34].astype(F32) * 32.0 + meta[rows, 34:35].astype(F32)
        p = one_hot(iota((step, nodes), 1) == at.astype(I32))
        mixed[rows, :] = (feats[rows, :].astype(F32) + dot(p, feats[...])).astype(BF16)

    loop(0, nodes // step, mix_block)

    def mixp_block(b):
        e = perm[pl.ds(b * step, step), :]
        mixp[pl.ds(b * (step // share), step // share)] = (
            dot(e, mixed[...]).astype(BF16).reshape(step // share, share, width)
        )

    loop(0, nodes // step, mixp_block)
    dp_send_all(mixp, mixr, mix_s, mix_r)
    mixr[me] = mixp[me]

    def live_block(b):
        live[pl.ds(b * step, step), :] = one_hot(iota((step, nodes), 0) + b * step == rowi[1:2, :])

    loop(0, slots // step, live_block)

    dp_wait_all(metap, metar, meta_s, meta_r)
    for b in range(slots // step):
        part = dot(live[b * step:(b + 1) * step, :], metar[...].reshape(nodes, metar.shape[2]))
        metat[:, b * step:(b + 1) * step] = part.T

    owner = metat[0:8, :].astype(I32)
    upper = one_hot(iota((slots, slots), 0) < iota((slots, slots), 1))
    own_iota = iota((nd, slots), 0)
    member = jnp.concatenate(
        [jnp.where(own_iota == owner[k:k + 1, :], 1.0, 0.0) for k in range(8)], axis=0
    )
    before = dot(member.astype(BF16), upper)
    carry = jnp.zeros((nd, 1), F32)
    lists = jnp.zeros((nd * 8, CAPL), F32)
    node_row = iota((1, slots), 1)
    for k in range(8):
        mk = member[k * nd:(k + 1) * nd, :]
        rank = jnp.sum(mk * (before[k * nd:(k + 1) * nd, :] + carry), axis=0, keepdims=True)
        carry = carry + jnp.sum(mk, axis=1, keepdims=True)
        fields = jnp.concatenate(
            [
                metat[8 + k:9 + k, :],
                metat[16 + k:17 + k, :],
                (node_row // 2).astype(F32),
                ((node_row % 2) * 8 + (k + 1)).astype(F32),
                jnp.zeros((4, slots), F32),
            ],
            axis=0,
        )
        here = iota((nd, 8, slots), 0) == owner[k:k + 1, :][None]
        f = jnp.where(here, fields[None], 0.0).reshape(nd * 8, slots).astype(BF16)
        at = one_hot(iota((CAPL, slots), 0) == rank.astype(I32))
        lists = lists + dot_nt(f, at)
    sendid[...] = lists.reshape(nd, 8, CAPL)
    over = jnp.max(jnp.where(carry > float(CAP), 1.0, 0.0), axis=0, keepdims=True)
    dp_send_all(sendid, idr, id_s, id_r)
    idr[me] = sendid[me]

    dp_wait_all(mixp, mixr, mix_s, mix_r)
    for b in range(slots // step):
        part = dot(live[b * step:(b + 1) * step, :], mixr[...].reshape(nodes, width))
        whole[z, b * step:(b + 1) * step, :] = part.astype(BF16)
    zright = lax.rem(z + 1, nz)
    zleft = lax.rem(z + nz - 1, nz)

    def ring_right(s):
        b = lax.rem(z - s + nz, nz)
        return copy(whole.at[b], whole.at[b], zr_s.at[s], zr_r.at[s], me, zright)

    def ring_left(s):
        b = lax.rem(z + s, nz)
        return copy(whole.at[b], whole.at[b], zl_s.at[s], zl_r.at[s], me, zleft)

    def got_right(s):
        b = lax.rem(z - s - 1 + nz, nz)
        copy(whole.at[b], whole.at[b], zr_s.at[s], zr_r.at[s], me, zright).wait_recv()
        return b

    def got_left(s):
        b = lax.rem(z + s + 1, nz)
        copy(whole.at[b], whole.at[b], zl_s.at[s], zl_r.at[s], me, zleft).wait_recv()
        return b

    n_right = nz // 2
    n_left = nz - 1 - n_right
    ring_right(0).start()
    ring_left(0).start()

    scale = 1.0 / (float(full_rows) ** 0.5)

    def use_block(b, first=False):
        blk = whole[b]
        whole_t[b] = blk.T
        h = dot(blk, proj[pl.ds(pl.multiple_of(b * width, width), width), :])
        if first:
            hidden[...] = h
        else:
            hidden[...] += h

    chunk = 256

    def serve(i):
        h = nxt(i)
        cols = idr[h].T
        hi = cols[:CAP, 0:1]
        lo = cols[:CAP, 1:2]
        acc = jnp.zeros((CAP, width), F32)
        for c in range(0, vocab, chunk):
            n = min(chunk, vocab - c)
            key = jnp.where(hi == float(c // chunk + 1), lo, -1.0)
            oh = one_hot(iota((CAP, n), 1).astype(F32) == key)
            acc = acc + dot(oh, embed[c:c + n, :])
        rows_out[h] = acc.astype(BF16)

    def serve_far(i):
        h = nxt(i)
        dp_wait(sendid, idr, id_s, id_r, h)
        serve(i)
        dp_copy(rows_out, rows_in, row_s, row_r, h).start()

    use_block(z, True)
    done = 1
    plan = [(4, 0), (8, 1), (12, 2), (16, 3)]
    for upto, s in plan:
        loop(done, upto, serve_far)
        done = upto
        if s < n_right:
            b = got_right(s)
            if s + 1 < n_right:
                ring_right(s + 1).start()
            use_block(b)
        if s < n_left:
            b = got_left(s)
            if s + 1 < n_left:
                ring_left(s + 1).start()
            use_block(b)
    loop(done, nd, serve_far)
    serve(0)
    rows_in[me] = rows_out[me]

    hid = hidden[...] * scale
    hidden[...] = hid
    square = jnp.sum(hid * hid, axis=1, keepdims=True)
    ng[...] = (hid * gain[...]).astype(BF16)
    lane = iota((slots, 128), 1)
    sc[...] = jnp.where(lane == 16, square, 0.0)
    kmat[...] = jnp.zeros(kmat.shape, BF16)
    scaled[...] = jnp.zeros(scaled.shape, BF16)

    def unpack(a, b):
        bm = b - 1.0
        odd = jnp.where(bm >= 8.0, 1.0, 0.0)
        k = jnp.where(b > 0.0, bm - 8.0 * odd, -1.0)
        node = jnp.where(b > 0.0, 2.0 * a + odd, -1.0)
        return node.astype(I32), k.astype(I32)

    def score(o):
        ids = sendid[o]
        cols = ids.T
        node_c, k_c = unpack(cols[:CAP, 2:3], cols[:CAP, 3:4])
        node_r, _ = unpack(ids[2:3, :], ids[3:4, :])
        p = one_hot(iota((CAP, slots), 1) == node_c)
        pt = one_hot(iota((slots, CAPL), 0) == node_r)
        pick[o] = p
        pick_t[o] = pt
        s = jnp.sum(rows_in[o].astype(F32) * dot(p, ng[...]), axis=1, keepdims=True)
        s_hi = s.astype(BF16).astype(F32)
        s_lo = s - s_hi
        ln = iota((CAP, 128), 1)
        val = jnp.where(ln == k_c, s_hi, jnp.where(ln == k_c + 8, s_lo, 0.0))
        val = jnp.where(k_c >= 0, val, 0.0)
        kmat[0:CAP, :] = val.astype(BF16)
        sc[...] += dot(pt, kmat[...])

    score(me)

    def score_far(i):
        o = prv(i)
        dp_wait(rows_out, rows_in, row_s, row_r, o)
        score(o)

    loop(1, nd, score_far)

    sct = sc[...].T
    zsend[0:8, :] = sct[0:8, :] + sct[8:16, :]
    zsend[8:16, :] = sct[16:24, :]

    def zx(i):
        zz = lax.rem(z + i, nz)
        return copy(zsend, zr.at[z], zx_s.at[zz], zx_r.at[z], me, zz)

    def zx_wait(i):
        zz = lax.rem(z + i, nz)
        copy(zsend, zr.at[zz], zx_s.at[zz], zx_r.at[zz], me, zz).wait_recv()

    loop(1, nz, lambda i: zx(i).start())
    zr[z] = zsend[...]
    loop(1, nz, zx_wait)
    tot = zr[0]
    for i in range(1, nz):
        tot = tot + zr[i]
    raw = tot[0:8, :]
    recip = lax.rsqrt(tot[8:9, :] / float(full_rows) + 1e-05)
    scores = raw * recip
    logp = scores - jnp.log(jnp.sum(jnp.exp(scores), axis=0, keepdims=True))
    prob = jnp.exp(logp)
    probs = metat[24:32, :]
    target = probs / jnp.sum(probs, axis=0, keepdims=True)
    kl = jnp.sum(target * (jnp.log(target) - logp), axis=0, keepdims=True)
    weight = 1.0 + metat[32:33, :]
    num = jnp.sum(weight * kl, axis=1, keepdims=True)
    den = jnp.sum(weight, axis=1, keepdims=True)
    gs = weight * (prob - target)
    inner = jnp.sum(gs * raw, axis=0, keepdims=True)
    back = recip * recip * recip * inner * (1.0 / float(full_rows))
    gs_hi = gs.astype(BF16).astype(F32)
    gs16 = jnp.concatenate([gs_hi, gs - gs_hi], axis=0).astype(BF16)
    coef = jnp.concatenate([recip, back, jnp.zeros((6, slots), F32)], axis=0).T
    dn[...] = jnp.zeros(dn.shape, F32)

    def spread(o):
        cols = sendid[o].T
        _, k_c = unpack(cols[:CAP, 2:3], cols[:CAP, 3:4])
        g16 = dot_nt(pick[o], gs16)
        ln = iota((CAP, 16), 1)
        g = jnp.sum(jnp.where(ln % 8 == k_c, g16, 0.0), axis=1, keepdims=True)
        scaled[0:CAP, :] = (rows_in[o].astype(F32) * g).astype(BF16)
        dn[...] += dot(pick_t[o], scaled[...])

    loop(0, nd, spread)
    dh[...] = (coef[:, 0:1] * gain[...] * dn[...] - hidden[...] * coef[:, 1:2]).astype(BF16)

    quarter = nz // 2

    def pair(q):
        return copy(pair_out.at[q], pair_in.at[q], pair_s.at[q], pair_r.at[q], sibling, z)

    for q in range(quarter):
        pair_out[q] = (dot(whole_t[(1 - core) * quarter + q], dh[...]) * scale).astype(BF16)
        pair(q).start()
    for q in range(quarter):
        gown[q] = dot(whole_t[core * quarter + q], dh[...]) * scale
    per = chips // quarter
    for q in range(quarter):
        pair(q).wait_recv()
        both = gown[q] + pair_in[q].astype(F32)
        rs_out[q * per:(q + 1) * per] = both.astype(BF16).reshape(per, width // per, width)

    def chip_at(i):
        return lax.rem(chip + i, chips)

    def rs(i):
        p = chip_at(i)
        return copy(rs_out.at[p], rs_in.at[chip], rs_s.at[p], rs_r.at[chip], p * 2 + core, z)

    def rs_wait(i):
        p = chip_at(i)
        copy(rs_out.at[p], rs_in.at[p], rs_s.at[p], rs_r.at[p], p * 2 + core, z).wait_recv()

    loop(1, chips, lambda i: rs(i).start())
    rs_in[chip] = rs_out[chip]
    loop(1, chips, rs_wait)
    shard = rs_in[0].astype(F32)
    for p in range(1, chips):
        shard = shard + rs_in[p].astype(F32)
    gfull[core, chip] = shard.astype(BF16)
    energy = jnp.sum(jnp.sum(shard * shard, axis=1, keepdims=True), axis=0, keepdims=True)
    ez_out[...] = jnp.broadcast_to(energy, (8, 128))

    def ezc(i):
        zz = lax.rem(z + i, nz)
        return copy(ez_out, ez.at[z], ez_s.at[zz], ez_r.at[z], me, zz)

    def ezc_wait(i):
        zz = lax.rem(z + i, nz)
        copy(ez_out, ez.at[zz], ez_s.at[zz], ez_r.at[zz], me, zz).wait_recv()

    def ag(i):
        p = chip_at(i)
        return copy(gfull.at[core, chip], gfull.at[core, chip], ag_s.at[p], ag_r.at[chip], p * 2 + core, z)

    def ag_wait(i):
        p = lax.rem(chip - i + chips, chips)
        copy(gfull.at[core, p], gfull.at[core, p], ag_s.at[p], ag_r.at[p], p * 2 + core, z).wait_recv()
        return p

    def forward(p):
        return copy(gfull.at[core, p], gfull.at[core, p], fw_s.at[p], fw_r.at[p], sibling, z)

    def forward_wait(p):
        copy(gfull.at[1 - core, p], gfull.at[1 - core, p], fw_s.at[p], fw_r.at[p], sibling, z).wait_recv()

    loop(1, nz, lambda i: ezc(i).start())
    loop(1, chips, lambda i: ag(i).start())
    forward(chip).start()
    ez[z] = ez_out[...]
    loop(1, nz, ezc_wait)
    etot = ez[0]
    for i in range(1, nz):
        etot = etot + ez[i]
    row = iota((8, 128), 0)
    tile = jnp.where(row == 0, etot, jnp.where(row == 1, num, jnp.where(row == 2, den, over)))

    def dtc(i):
        d = nxt(i)
        return copy(dt_out, dt.at[me], dt_s.at[d], dt_r.at[me], d, z)

    def dtc_wait(i):
        h = prv(i)
        copy(dt_out, dt.at[h], dt_s.at[h], dt_r.at[h], h, z).wait_recv()

    dt_out[...] = tile
    loop(1, nd, lambda i: dtc(i).start())
    dt[me] = tile

    def ag_pass(i):
        p = ag_wait(i)
        forward(p).start()

    loop(1, chips, ag_pass)
    loop(1, nd, dtc_wait)
    total = dt[0]
    for i in range(1, nd):
        total = total + dt[i]
    entries = float(full_rows) * float(full_rows)
    factor = 0.5 * lax.rsqrt(total[0:1, 0:1] / entries + 1e-06)
    loss = total[1:2, :] / total[2:3, :]
    stat[...] = jnp.where(row == 0, loss, total[3:4, :])

    blk_rows = width // per

    def finish(h, p):
        r = pl.ds(pl.multiple_of((h * chips + p) * blk_rows, blk_rows), blk_rows)
        out[r, :] = (proj[r, :].astype(F32) - gfull[h, p].astype(F32) * factor).astype(BF16)

    loop(0, chips, lambda p: finish(core, p))

    def finish_far(p):
        forward_wait(p)
        finish(1 - core, p)

    loop(0, chips, finish_far)

    dp_sent_all(metap, metar, meta_s, meta_r)
    dp_sent_all(mixp, mixr, mix_s, mix_r)
    dp_sent_all(sendid, idr, id_s, id_r)
    dp_sent_all(rows_out, rows_in, row_s, row_r)
    for s in range(n_right):
        ring_right(s).wait_send()
    for s in range(n_left):
        ring_left(s).wait_send()
    for q in range(quarter):
        pair(q).wait_send()
    loop(1, nz, lambda i: zx(i).wait_send())
    loop(1, chips, lambda i: rs(i).wait_send())
    loop(1, nz, lambda i: ezc(i).wait_send())
    loop(1, chips, lambda i: ag(i).wait_send())
    loop(0, chips, lambda p: forward(p).wait_send())
    loop(1, nd, lambda i: dtc(i).wait_send())


def fast_step(nd, nz, feats, parent, counts, accepted, cand_ids, target_probs, gain, embed, proj):
    me = lax.axis_index("dp")
    nodes, width = feats.shape
    full_rows = proj.shape[0]
    vocab = embed.shape[0]
    share = nodes // nd
    slots = nodes // 2
    chips = nd // 2
    quarter = nz // 2
    per = chips // quarter
    groups = jnp.arange(nd, dtype=I32)
    off = jnp.sum(jnp.where(groups[None, :] < groups[:, None], counts[None, :], 0), axis=1)
    first = (me - off) & (nd - 1)
    j = jnp.arange(share, dtype=I32)
    alive = j[None, :] * nd + first[:, None] < counts[:, None]
    into = jnp.where(alive, ((off + first) // nd)[:, None] + j[None, :], -1).reshape(1, nodes)
    rot = jnp.sum(jnp.where(groups < me, counts, 0))
    n = jnp.arange(nodes, dtype=I32)
    to = (((n + rot) & (nd - 1)) * share + n // nd).reshape(1, nodes)
    rowi = jnp.concatenate([to, into, jnp.zeros((6, nodes), I32)], axis=0)
    owner = cand_ids // vocab
    local = cand_ids - owner * vocab
    meta = jnp.concatenate(
        [
            owner.astype(BF16),
            (local // 256 + 1).astype(BF16),
            (local % 256).astype(BF16),
            target_probs,
            accepted[:, None].astype(BF16),
            (parent // 32)[:, None].astype(BF16),
            (parent % 32)[:, None].astype(BF16),
            jnp.zeros((nodes, 128 - 35), BF16),
        ],
        axis=1,
    )
    vm = pltpu.VMEM
    scratch = [
        vm((nodes, nodes), BF16),
        vm((nodes, width), BF16),
        vm((nd, share, 128), BF16),
        vm((nd, share, 128), BF16),
        vm((nd, share, width), BF16),
        vm((nd, share, width), BF16),
        vm((slots, nodes), BF16),
        vm((128, slots), F32),
        vm((nd, 8, CAPL), F32),
        vm((nd, 8, CAPL), F32),
        vm((nd, CAP, width), BF16),
        vm((nd, CAP, width), BF16),
        vm((nz, slots, width), BF16),
        vm((nz, width, slots), BF16),
        vm((slots, width), F32),
        vm((slots, width), BF16),
        vm((nd, CAP, slots), BF16),
        vm((nd, slots, CAPL), BF16),
        vm((CAPL, 128), BF16),
        vm((slots, 128), F32),
        vm((16, slots), F32),
        vm((nz, 16, slots), F32),
        vm((CAPL, width), BF16),
        vm((slots, width), F32),
        vm((slots, width), BF16),
        vm((quarter, width, width), BF16),
        vm((quarter, width, width), BF16),
        vm((quarter, width, width), F32),
        vm((chips, width // per, width), BF16),
        vm((chips, width // per, width), BF16),
        vm((2, chips, width // per, width), BF16),
        vm((8, 128), F32),
        vm((nz, 8, 128), F32),
        vm((8, 128), F32),
        vm((nd, 8, 128), F32),
    ]
    dma = pltpu.SemaphoreType.DMA
    for count in (
        nd, nd, nd, nd, nd, nd, nd, nd,
        nz, nz, nz, nz, nz, nz, quarter, quarter,
        chips, chips, chips, chips, chips, chips, nz, nz, nd, nd,
    ):
        scratch.append(dma((count,)))
    in_vmem = pl.BlockSpec(memory_space=pltpu.VMEM)
    out, stat = pl.pallas_call(
        functools.partial(step_kernel, nd, nz, full_rows),
        out_shape=(
            jax.ShapeDtypeStruct(proj.shape, BF16),
            jax.ShapeDtypeStruct((8, 128), F32),
        ),
        in_specs=[in_vmem] * 6,
        out_specs=(in_vmem, in_vmem),
        scratch_shapes=scratch,
        compiler_params=pltpu.CompilerParams(
            collective_id=0, has_side_effects=True, vmem_limit_bytes=60 * 1024 * 1024
        ),
        name="step",
    )(rowi, meta, feats, gain.astype(F32).reshape(1, width), embed, proj)
    return out, stat


def wide_step(feats, parent, counts, accepted, cand_ids, target_probs, gain, embed, proj):
    node_rows, width_part = feats.shape
    full_width = proj.shape[0]
    group = lax.axis_index("dp")
    groups = lax.axis_size("dp")
    shard_rows = embed.shape[0]
    cand_count = cand_ids.shape[1]
    scale_in = 1.0 / jnp.sqrt(jnp.float32(full_width))
    gain_f = gain.astype(jnp.float32)
    flat_ids = cand_ids.reshape(-1)
    requests = flat_ids.shape[0]
    capacity = 3 * requests // (2 * groups)
    owners = flat_ids // shard_rows
    local_ids = flat_ids - owners * shard_rows
    member = owners[:, None] == jnp.arange(groups, dtype=jnp.int32)[None, :]
    per_owner = jnp.sum(member.astype(jnp.int32), axis=0)
    starts = jnp.cumsum(per_owner) - per_owner
    my_start = jnp.sum(jnp.where(member, starts[None, :], 0), axis=1)
    order = jnp.argsort(owners, stable=True)
    ranks = jnp.arange(requests, dtype=jnp.int32) - my_start[order]
    slots = owners[order] * capacity + ranks
    outgoing = jnp.zeros((groups * capacity,), jnp.int32).at[slots].set(local_ids[order])
    placed = jnp.zeros((requests,), jnp.int32).at[order].set(slots)
    mixed = (feats.astype(jnp.float32) + feats[parent].astype(jnp.float32)).astype(jnp.bfloat16)
    piece = lax.all_gather(mixed, "mp", axis=1, tiled=True)
    partial_value = jnp.dot(piece, proj, preferred_element_type=jnp.float32)
    whole = piece
    partial_value, whole = (partial_value, whole)
    hidden = partial_value * scale_in
    squares = lax.psum(jnp.sum(hidden * hidden, axis=1), "mp")
    recip = lax.rsqrt(squares / full_width + 1e-05)
    normed = (hidden * recip[:, None] * gain_f).astype(jnp.bfloat16)
    found = embed[
        lax.all_to_all(
            outgoing.reshape(groups, capacity), "dp", split_axis=0, concat_axis=0, tiled=True
        )
    ]
    fetched = lax.all_to_all(found, "dp", split_axis=0, concat_axis=0, tiled=True)
    cand_rows = fetched.reshape(groups * capacity, width_part)[placed].reshape(
        node_rows, cand_count, width_part
    )
    part_scores = jnp.einsum("nkd,nd->nk", cand_rows, normed, preferred_element_type=jnp.float32)
    scores = lax.psum(part_scores, "mp")
    logp = scores - jnp.log(jnp.sum(jnp.exp(scores), axis=1, keepdims=True))
    prob = jnp.exp(logp)
    probs = target_probs.astype(jnp.float32)
    target = probs / jnp.sum(probs, axis=1, keepdims=True)
    kl_node = jnp.sum(target * (jnp.log(target) - logp), axis=1)
    live_count = lax.dynamic_index_in_dim(counts, group, 0, keepdims=False)
    live = jnp.arange(node_rows, dtype=jnp.int32) < live_count
    weight = jnp.where(live, 1 + accepted, 0).astype(jnp.float32)
    num, den = lax.psum((jnp.sum(weight * kl_node), jnp.sum(weight)), "dp")
    grad_scores = weight[:, None] * (prob - target)
    dnormed = jnp.einsum("nk,nkd->nd", grad_scores, cand_rows, preferred_element_type=jnp.float32)
    inner = lax.psum(jnp.sum(dnormed * gain_f * hidden, axis=1), "mp")
    dhidden = (
        recip[:, None] * gain_f * dnormed - hidden * (recip**3 * inner / full_width)[:, None]
    ).astype(jnp.bfloat16)
    grad_part = (
        lax.dot_general(
            whole, dhidden, (((0,), (0,)), ((), ())), preferred_element_type=jnp.float32
        )
        * scale_in
    )
    grad = lax.psum(grad_part, "dp")
    energy = lax.psum(jnp.sum(grad * grad), "mp")
    factor = lax.rsqrt(energy / (full_width * full_width) + 1e-06)
    new_proj = (proj.astype(jnp.float32) - 0.5 * grad * factor).astype(jnp.bfloat16)
    return (new_proj, num / den)


def solution(mesh):
    nd = mesh.shape["dp"]
    nz = mesh.shape["mp"]

    def per_device(*args):
        out, stat = fast_step(nd, nz, *args)
        return lax.cond(
            stat[1, 0] > 0.0,
            lambda: wide_step(*args),
            lambda: (out, stat[0, 0]),
        )

    placed = (
        P("dp", "mp"),
        P("dp"),
        P(),
        P("dp"),
        P("dp", None),
        P("dp", None),
        P("mp"),
        P("dp", "mp"),
        P(None, "mp"),
    )
    return jax.shard_map(
        per_device, mesh=mesh, in_specs=placed, out_specs=(P(None, "mp"), P()), check_vma=False
    )
```

```python
import functools
import jax
import jax.numpy as jnp
from jax import lax
from jax.experimental import pallas as pl
from jax.experimental.pallas import tpu as pltpu
from jax.sharding import PartitionSpec as P

MESH = pl.DeviceIdType.MESH
F32 = jnp.float32
BF16 = jnp.bfloat16
I32 = jnp.int32

GROUP = 4
CAP = 352
CAPL = 384
HALF = 224


def dot(a, b):
    return jnp.dot(a, b, preferred_element_type=F32)


def dot_nt(a, b):
    return lax.dot_general(a, b, (((1,), (1,)), ((), ())), preferred_element_type=F32)


def one_hot(hit):
    return jnp.where(hit, 1.0, 0.0).astype(BF16)


def iota(shape, axis):
    return lax.broadcasted_iota(I32, shape, axis)


def step_kernel(
    nd, nz, full_rows,
    counts, ids, odds, parent, accepted, feats, gain, embed, proj,
    out, stat,
    emb, perm, meta, metap, metar, mixp, mixr, live, metat,
    sendid, idr, rows_out, rows_in, whole, whole_t, hidden, ng,
    pick, pick_t, kmat, ksel, sc, zsend, zr, scaled, dn, dh,
    pair_out, pair_in, gown, rs_out, rs_in, gfull, ez_out, ez, dt_out, dt,
    emb_s, emb_r, meta_s, meta_r, mix_s, mix_r, id_s, id_r, row_s, row_r,
    zr_s, zr_r, zl_s, zl_r, zx_s, zx_r, pair_s, pair_r,
    rs_s, rs_r, ag_s, ag_r, fw_s, fw_r, ez_s, ez_r, dt_s, dt_r,
):
    me = lax.axis_index("dp")
    z = lax.axis_index("mp")
    nodes = feats.shape[0]
    width = feats.shape[1]
    slots = live.shape[0]
    share = nodes // nd
    core = lax.rem(me, 2)
    chip = lax.div(me, 2)
    chips = nd // 2
    sibling = me + 1 - 2 * core
    vocab = embed.shape[0]

    sent = []

    def copy(src, dst, ss, rs, d, zz):
        return pltpu.make_async_remote_copy(
            src_ref=src, dst_ref=dst, send_sem=ss, recv_sem=rs,
            device_id=(d, zz), device_id_type=MESH,
        )

    def nxt(i):
        return lax.rem(me + i, nd)

    def prv(i):
        return lax.rem(me - i + nd, nd)

    def loop(lo, hi, body):
        def wrapped(i, carry):
            body(i)
            return carry
        lax.fori_loop(lo, hi, wrapped, 0)

    def dp_copy(src, dst, ss, rs, d):
        return copy(src.at[d], dst.at[me], ss.at[d], rs.at[me], d, z)

    def dp_wait(src, dst, ss, rs, h):
        copy(src.at[h], dst.at[h], ss.at[h], rs.at[h], h, z).wait_recv()

    def dp_send_all(src, dst, ss, rs):
        loop(1, nd, lambda i: dp_copy(src, dst, ss, rs, nxt(i)).start())
        sent.append(lambda: dp_sent_all(src, dst, ss, rs))

    def dp_wait_all(src, dst, ss, rs):
        loop(1, nd, lambda i: dp_wait(src, dst, ss, rs, prv(i)))

    def dp_sent_all(src, dst, ss, rs):
        loop(1, nd, lambda i: dp_copy(src, dst, ss, rs, nxt(i)).wait_send())

    side = int(chips ** 0.5)
    chip_x = lax.rem(chip, side)
    chip_y = lax.div(chip, side)

    def offset(i):
        dx = lax.rem(i, side)
        dy = lax.rem(lax.div(i, side) + i, side)
        return dx + core * (dy - dx), dy + core * (dx - dy)

    def to_chip(i):
        dx, dy = offset(i)
        return lax.rem(chip_y + dy, side) * side + lax.rem(chip_x + dx, side)

    def from_chip(i):
        dx, dy = offset(i)
        return lax.rem(chip_y - dy + side, side) * side + lax.rem(chip_x - dx + side, side)

    def chip_copy(src, dst, ss, rs, p):
        return copy(src.at[p], dst.at[chip], ss.at[p], rs.at[chip], p * 2 + core, z)

    def chip_wait(src, dst, ss, rs, p):
        copy(src.at[p], dst.at[p], ss.at[p], rs.at[p], p * 2 + core, z).wait_recv()

    def chip_sent_all(src, dst, ss, rs):
        loop(1, chips, lambda i: chip_copy(src, dst, ss, rs, to_chip(i)).wait_send())

    barrier = pltpu.get_barrier_semaphore()
    loop(1, nd, lambda i: pl.semaphore_signal(barrier, inc=1, device_id=(nxt(i), z), device_id_type=MESH))
    loop(1, nz, lambda i: pl.semaphore_signal(barrier, inc=1, device_id=(me, lax.rem(z + i, nz)), device_id_type=MESH))

    node_lane = iota((1, nodes), 1)
    lane_h = lax.div(node_lane, share)
    lane_j = node_lane - lane_h * share

    def deal(h, state):
        off, mine, into = state
        count = counts[h]
        first = (me - off) & (nd - 1)
        base = (off + first) // nd
        row = jnp.where(lane_j * nd + first < count, base + lane_j, -1)
        return off + count, jnp.where(h == me, off, mine), jnp.where(lane_h == h, row, into)

    _, mine, into = lax.fori_loop(
        0, nd, deal, (jnp.int32(0), jnp.int32(0), jnp.full((1, nodes), -1, I32))
    )
    dealt = ((node_lane + mine) & (nd - 1)) * share + lax.div(node_lane, nd)

    def in_row(ref):
        return jnp.concatenate([ref[r:r + 1, :] for r in range(ref.shape[0])], axis=1)

    idf = ids[...].astype(F32)
    own_f = jnp.floor((idf + 0.5) * (1.0 / float(vocab)))
    at_f = idf - own_f * float(vocab)
    hi_f = jnp.floor(at_f * (1.0 / 256.0))
    par = in_row(parent)
    extra = jnp.concatenate(
        [
            in_row(accepted).astype(F32),
            (par // 32).astype(F32),
            (par % 32).astype(F32),
            jnp.zeros((5, nodes), F32),
        ],
        axis=0,
    )
    table = jnp.concatenate(
        [own_f, hi_f + 1.0, at_f - 256.0 * hi_f, odds[...].astype(F32), extra, jnp.zeros((88, nodes), F32)],
        axis=0,
    )
    meta[...] = table.T.astype(BF16)

    step = 128

    def perm_block(b):
        rows = pl.ds(b * step, step)
        e = one_hot(iota((step, nodes), 0) + b * step == dealt)
        perm[rows, :] = e
        metap[pl.ds(b * (step // share), step // share)] = (
            dot(e, meta[...]).astype(BF16).reshape(step // share, share, metap.shape[2])
        )

    loop(0, nodes // step, perm_block)

    block = emb.shape[1]
    even = vocab // 32 * 32
    emb[core, 0:even, :] = embed[0:even, :]
    emb[core, even:block, :] = jnp.concatenate(
        [embed[even:vocab, :].astype(F32), jnp.zeros((block - vocab, width), F32)], axis=0
    ).astype(BF16)
    pl.semaphore_wait(barrier, nd - 1 + nz - 1)

    def emb_copy(c):
        return copy(emb.at[c], emb.at[c], emb_s.at[c], emb_r.at[c], sibling, z)

    emb_copy(core).start()
    sent.append(lambda: emb_copy(core).wait_send())
    dp_send_all(metap, metar, meta_s, meta_r)
    metar[me] = metap[me]

    def mixp_block(b):
        mine_b = metap[pl.ds(b * (step // share), step // share)].reshape(step, metap.shape[2]).astype(F32)
        at = mine_b[:, 33:34] * 32.0 + mine_b[:, 34:35]
        p = one_hot(iota((step, nodes), 1) == at.astype(I32))
        mixp[pl.ds(b * (step // share), step // share)] = (
            dot(perm[pl.ds(b * step, step), :] + p, feats[...])
            .astype(BF16)
            .reshape(step // share, share, width)
        )

    loop(0, nodes // step, mixp_block)
    dp_send_all(mixp, mixr, mix_s, mix_r)
    mixr[me] = mixp[me]

    def live_block(b):
        live[pl.ds(b * step, step), :] = one_hot(iota((step, nodes), 0) + b * step == into)

    loop(0, slots // step, live_block)

    dp_wait_all(metap, metar, meta_s, meta_r)
    for b in range(slots // step):
        part = dot(live[b * step:(b + 1) * step, :], metar[...].reshape(nodes, metar.shape[2]))
        metat[:, b * step:(b + 1) * step] = part.T

    owner = metat[0:8, :].astype(I32)
    upper = one_hot(iota((slots, slots), 0) < iota((slots, slots), 1))
    own_iota = iota((nd, slots), 0)
    member = jnp.concatenate(
        [jnp.where(own_iota == owner[k:k + 1, :], 1.0, 0.0) for k in range(8)], axis=0
    )
    before = dot(member.astype(BF16), upper)
    carry = jnp.zeros((nd, 1), F32)
    lists = jnp.zeros((chips * 8, CAPL), F32)
    asks = jnp.zeros((chips, 1), F32)
    at_chip = owner // 2
    odd_core = owner - 2 * at_chip
    chip_iota = iota((chips, slots), 0)
    node_row = iota((1, slots), 1)
    for k in range(8):
        mk = member[k * nd:(k + 1) * nd, :]
        rank = jnp.sum(mk * (before[k * nd:(k + 1) * nd, :] + carry), axis=0, keepdims=True)
        carry = carry + jnp.sum(mk, axis=1, keepdims=True)
        odd_k = odd_core[k:k + 1, :].astype(F32)
        place = rank + odd_k * (float(CAP - 1) - 2.0 * rank)
        asks = asks + jnp.sum(jnp.where(chip_iota == at_chip[k:k + 1, :], 1.0, 0.0), axis=1, keepdims=True)
        fields = jnp.concatenate(
            [
                metat[8 + k:9 + k, :] + float(block // 256) * odd_k,
                metat[16 + k:17 + k, :],
                (node_row // 2).astype(F32),
                ((node_row % 2) * 8 + (k + 1)).astype(F32),
                jnp.zeros((4, slots), F32),
            ],
            axis=0,
        )
        here = iota((chips, 8, slots), 0) == at_chip[k:k + 1, :][None]
        f = jnp.where(here, fields[None], 0.0).reshape(chips * 8, slots).astype(BF16)
        at = one_hot(iota((CAPL, slots), 0) == place.astype(I32))
        lists = lists + dot_nt(f, at)
    sendid[...] = lists.reshape(chips, 8, CAPL)
    over = jnp.maximum(
        jnp.max(jnp.where(carry > float(HALF), 1.0, 0.0), axis=0, keepdims=True),
        jnp.max(jnp.where(asks > float(CAP), 1.0, 0.0), axis=0, keepdims=True),
    )
    loop(1, chips, lambda i: chip_copy(sendid, idr, id_s, id_r, to_chip(i)).start())
    sent.append(lambda: chip_sent_all(sendid, idr, id_s, id_r))
    idr[chip] = sendid[chip]

    dp_wait_all(mixp, mixr, mix_s, mix_r)
    for b in range(slots // step):
        part = dot(live[b * step:(b + 1) * step, :], mixr[...].reshape(nodes, width))
        whole[z, b * step:(b + 1) * step, :] = part.astype(BF16)
    zright = lax.rem(z + 1, nz)
    zleft = lax.rem(z + nz - 1, nz)

    def ring_right(s):
        b = lax.rem(z - s + nz, nz)
        return copy(whole.at[b], whole.at[b], zr_s.at[s], zr_r.at[s], me, zright)

    def ring_left(s):
        b = lax.rem(z + s, nz)
        return copy(whole.at[b], whole.at[b], zl_s.at[s], zl_r.at[s], me, zleft)

    def got_right(s):
        b = lax.rem(z - s - 1 + nz, nz)
        copy(whole.at[b], whole.at[b], zr_s.at[s], zr_r.at[s], me, zright).wait_recv()
        return b

    def got_left(s):
        b = lax.rem(z + s + 1, nz)
        copy(whole.at[b], whole.at[b], zl_s.at[s], zl_r.at[s], me, zleft).wait_recv()
        return b

    n_right = nz // 2
    n_left = nz - 1 - n_right
    ring_right(0).start()
    ring_left(0).start()

    scale = 1.0 / (float(full_rows) ** 0.5)

    def use_block(b, first=False):
        blk = whole[b]
        whole_t[b] = blk.T
        h = dot(blk, proj[pl.ds(pl.multiple_of(b * width, width), width), :])
        if first:
            hidden[...] = h
        else:
            hidden[...] += h

    chunk = 256

    low = CAP - HALF

    def serve(h):
        cols = idr[h].T
        hi = jnp.broadcast_to(cols[:CAP, 0:1], (CAP, chunk)).astype(BF16)
        lo = one_hot(iota((CAP, chunk), 1) == cols[:CAP, 1:2].astype(I32))
        halves = []
        for c in range(2):
            first = c * low
            parts = [
                jnp.where(
                    hi[first:first + HALF, :] == jnp.bfloat16(c * (block // chunk) + i + 1),
                    lo[first:first + HALF, :],
                    jnp.bfloat16(0),
                )
                for i in range(block // chunk)
            ]
            halves.append(dot(jnp.concatenate(parts, axis=1), emb[c]))
        front, rear = halves
        rows_out[h, 0:low, :] = front[0:low, :].astype(BF16)
        rows_out[h, low:HALF, :] = (front[low:, :] + rear[:HALF - low, :]).astype(BF16)
        rows_out[h, HALF:CAP, :] = rear[HALF - low:, :].astype(BF16)

    def serve_far(i):
        h = to_chip(i)
        chip_wait(sendid, idr, id_s, id_r, h)
        serve(h)
        chip_copy(rows_out, rows_in, row_s, row_r, h).start()

    emb_copy(1 - core).wait_recv()
    use_block(z, True)
    done = 1
    plan = [(4, 0), (7, 1), (10, 2), (13, 3)]
    for upto, s in plan:
        loop(done, upto, serve_far)
        done = upto
        if s < n_right:
            b = got_right(s)
            if s + 1 < n_right:
                ring_right(s + 1).start()
            use_block(b)
        if s < n_left:
            b = got_left(s)
            if s + 1 < n_left:
                ring_left(s + 1).start()
            use_block(b)
    loop(done, chips, serve_far)
    serve(chip)
    rows_in[chip] = rows_out[chip]
    sent.append(lambda: chip_sent_all(rows_out, rows_in, row_s, row_r))
    for s in range(n_right):
        sent.append(functools.partial(lambda s: ring_right(s).wait_send(), s))
    for s in range(n_left):
        sent.append(functools.partial(lambda s: ring_left(s).wait_send(), s))

    hid = hidden[...] * scale
    hidden[...] = hid
    square = jnp.sum(hid * hid, axis=1, keepdims=True)
    ng[...] = (hid * gain[...].astype(F32)).astype(BF16)
    lane = iota((slots, 128), 1)
    sc[...] = jnp.where(lane == 16, square, 0.0)
    kmat[...] = jnp.zeros(kmat.shape, BF16)
    scaled[...] = jnp.zeros(scaled.shape, BF16)

    def unpack(a, b):
        bm = b - 1.0
        odd = jnp.where(bm >= 8.0, 1.0, 0.0)
        k = jnp.where(b > 0.0, bm - 8.0 * odd, -1.0)
        node = jnp.where(b > 0.0, 2.0 * a + odd, -1.0)
        return node.astype(I32), k.astype(I32)

    def owner_at(j, q):
        return from_chip(j * GROUP + q + 1)

    def score(j):
        for q in range(GROUP):
            lists_o = sendid[owner_at(j, q)]
            cols = lists_o.T
            node_c, k_c = unpack(cols[:CAP, 2:3], cols[:CAP, 3:4])
            node_r, _ = unpack(lists_o[2:3, :], lists_o[3:4, :])
            pick[j, q * CAP:(q + 1) * CAP, :] = one_hot(iota((CAP, slots), 1) == node_c)
            pick_t[j, :, q * CAPL:(q + 1) * CAPL] = one_hot(iota((slots, CAPL), 0) == node_r)
            ln = iota((CAP, 128), 1)
            ksel[j, q * CAP:(q + 1) * CAP, :] = one_hot(ln == k_c) + one_hot((ln == k_c + 8) & (k_c >= 0))
        for q in range(GROUP):
            wait_rows(j, q)
        asked = dot(pick[j], ng[...])
        for q in range(GROUP):
            got = rows_in[owner_at(j, q)].astype(F32)
            s = jnp.sum(got * asked[q * CAP:(q + 1) * CAP, :], axis=1, keepdims=True)
            s_hi = s.astype(BF16).astype(F32)
            ln = iota((CAP, 128), 1)
            val = jnp.where(ln < 8, s_hi, s - s_hi) * ksel[j, q * CAP:(q + 1) * CAP, :].astype(F32)
            kmat[q * CAPL:q * CAPL + CAP, :] = val.astype(BF16)
        sc[...] += dot(pick_t[j], kmat[...])

    def wait_rows(j, q):
        chip_wait(rows_out, rows_in, row_s, row_r, owner_at(j, q))

    groups = chips // GROUP
    loop(0, groups - 1, score)
    last = groups - 1

    def wait_rows(j, q):
        if q + 1 < GROUP:
            chip_wait(rows_out, rows_in, row_s, row_r, owner_at(j, q))

    score(last)

    sct = sc[...].T
    zsend[0:8, :] = sct[0:8, :] + sct[8:16, :]
    zsend[8:16, :] = sct[16:24, :]

    def zx(i):
        zz = lax.rem(z + i, nz)
        return copy(zsend, zr.at[z], zx_s.at[zz], zx_r.at[z], me, zz)

    def zx_wait(i):
        zz = lax.rem(z + i, nz)
        copy(zsend, zr.at[zz], zx_s.at[zz], zx_r.at[zz], me, zz).wait_recv()

    loop(1, nz, lambda i: zx(i).start())
    sent.append(lambda: loop(1, nz, lambda i: zx(i).wait_send()))
    zr[z] = zsend[...]
    loop(1, nz, zx_wait)
    tot = zr[0]
    for i in range(1, nz):
        tot = tot + zr[i]
    raw = tot[0:8, :]
    recip = lax.rsqrt(tot[8:9, :] / float(full_rows) + 1e-05)
    scores = raw * recip
    logp = scores - jnp.log(jnp.sum(jnp.exp(scores), axis=0, keepdims=True))
    prob = jnp.exp(logp)
    probs = metat[24:32, :]
    target = probs / jnp.sum(probs, axis=0, keepdims=True)
    kl = jnp.sum(target * (jnp.log(target) - logp), axis=0, keepdims=True)
    weight = 1.0 + metat[32:33, :]
    num = jnp.sum(weight * kl, axis=1, keepdims=True)
    den = jnp.sum(weight, axis=1, keepdims=True)
    gs = weight * (prob - target)
    inner = jnp.sum(gs * raw, axis=0, keepdims=True)
    back = recip * recip * recip * inner * (1.0 / float(full_rows))
    gs_hi = gs.astype(BF16).astype(F32)
    gs16 = jnp.concatenate([gs_hi, gs - gs_hi], axis=0).astype(BF16)
    coef = jnp.concatenate([recip, back, jnp.zeros((6, slots), F32)], axis=0).T
    dn[...] = jnp.zeros(dn.shape, F32)

    def spread(j):
        g16 = dot_nt(pick[j], gs16)
        g = jnp.sum(g16 * ksel[j][:, 0:16].astype(F32), axis=1, keepdims=True)
        for q in range(GROUP):
            got = rows_in[owner_at(j, q)].astype(F32)
            scaled[q * CAPL:q * CAPL + CAP, :] = (got * g[q * CAP:(q + 1) * CAP, :]).astype(BF16)
        dn[...] += dot(pick_t[j], scaled[...])

    loop(0, groups, spread)
    dh[...] = (coef[:, 0:1] * gain[...].astype(F32) * dn[...] - hidden[...] * coef[:, 1:2]).astype(BF16)

    quarter = nz // 2

    def pair(q):
        return copy(pair_out.at[q], pair_in.at[q], pair_s.at[q], pair_r.at[q], sibling, z)

    for q in range(quarter):
        pair_out[q] = (dot(whole_t[(1 - core) * quarter + q], dh[...]) * scale).astype(BF16)
        pair(q).start()
    for q in range(quarter):
        gown[q] = dot(whole_t[core * quarter + q], dh[...]) * scale
    per = chips // quarter
    for q in range(quarter):
        pair(q).wait_recv()
        both = gown[q] + pair_in[q].astype(F32)
        rs_out[q * per:(q + 1) * per] = both.astype(BF16).reshape(per, width // per, width)

    for q in range(quarter):
        sent.append(functools.partial(lambda q: pair(q).wait_send(), q))

    def chip_at(i):
        return lax.rem(chip + i, chips)

    def rs(i):
        p = chip_at(i)
        return copy(rs_out.at[p], rs_in.at[chip], rs_s.at[p], rs_r.at[chip], p * 2 + core, z)

    def rs_wait(i):
        p = chip_at(i)
        copy(rs_out.at[p], rs_in.at[p], rs_s.at[p], rs_r.at[p], p * 2 + core, z).wait_recv()

    loop(1, chips, lambda i: rs(i).start())
    rs_in[chip] = rs_out[chip]
    loop(1, chips, rs_wait)
    sent.append(lambda: loop(1, chips, lambda i: rs(i).wait_send()))
    shard = rs_in[0].astype(F32)
    for p in range(1, chips):
        shard = shard + rs_in[p].astype(F32)
    gfull[core, chip] = shard.astype(BF16)
    energy = jnp.sum(jnp.sum(shard * shard, axis=1, keepdims=True), axis=0, keepdims=True)
    ez_out[...] = jnp.broadcast_to(energy, (8, 128))

    def ezc(i):
        zz = lax.rem(z + i, nz)
        return copy(ez_out, ez.at[z], ez_s.at[zz], ez_r.at[z], me, zz)

    def ezc_wait(i):
        zz = lax.rem(z + i, nz)
        copy(ez_out, ez.at[zz], ez_s.at[zz], ez_r.at[zz], me, zz).wait_recv()

    def ag(i):
        p = chip_at(i)
        return copy(gfull.at[core, chip], gfull.at[core, chip], ag_s.at[p], ag_r.at[chip], p * 2 + core, z)

    def ag_wait(i):
        p = lax.rem(chip - i + chips, chips)
        copy(gfull.at[core, p], gfull.at[core, p], ag_s.at[p], ag_r.at[p], p * 2 + core, z).wait_recv()
        return p

    def forward(p):
        return copy(gfull.at[core, p], gfull.at[core, p], fw_s.at[p], fw_r.at[p], sibling, z)

    def forward_wait(p):
        copy(gfull.at[1 - core, p], gfull.at[1 - core, p], fw_s.at[p], fw_r.at[p], sibling, z).wait_recv()

    loop(1, nz, lambda i: ezc(i).start())
    loop(1, chips, lambda i: ag(i).start())
    forward(chip).start()
    ez[z] = ez_out[...]
    loop(1, nz, ezc_wait)
    etot = ez[0]
    for i in range(1, nz):
        etot = etot + ez[i]
    row = iota((8, 128), 0)
    sent.append(lambda: loop(1, nz, lambda i: ezc(i).wait_send()))
    sent.append(lambda: loop(1, chips, lambda i: ag(i).wait_send()))
    sent.append(lambda: loop(0, chips, lambda p: forward(p).wait_send()))
    tile = jnp.where(row == 0, etot, jnp.where(row == 1, num, jnp.where(row == 2, den, over)))

    def dtc(i):
        d = nxt(i)
        return copy(dt_out, dt.at[me], dt_s.at[d], dt_r.at[me], d, z)

    def dtc_wait(i):
        h = prv(i)
        copy(dt_out, dt.at[h], dt_s.at[h], dt_r.at[h], h, z).wait_recv()

    dt_out[...] = tile
    loop(1, nd, lambda i: dtc(i).start())
    dt[me] = tile
    sent.append(lambda: loop(1, nd, lambda i: dtc(i).wait_send()))

    def ag_pass(i):
        p = ag_wait(i)
        forward(p).start()

    loop(1, chips, ag_pass)
    loop(1, nd, dtc_wait)
    total = dt[0]
    for i in range(1, nd):
        total = total + dt[i]
    entries = float(full_rows) * float(full_rows)
    factor = 0.5 * lax.rsqrt(total[0:1, 0:1] / entries + 1e-06)
    loss = total[1:2, :] / total[2:3, :]
    stat[...] = jnp.where(row == 0, loss, total[3:4, :])

    blk_rows = width // per

    def finish(h, p):
        r = pl.ds(pl.multiple_of((h * chips + p) * blk_rows, blk_rows), blk_rows)
        out[r, :] = (proj[r, :].astype(F32) - gfull[h, p].astype(F32) * factor).astype(BF16)

    loop(0, chips, lambda p: finish(core, p))

    def finish_far(p):
        forward_wait(p)
        finish(1 - core, p)

    loop(0, chips, finish_far)

    for wait in sent:
        wait()


def fast_step(nd, nz, feats, parent, counts, accepted, cand_ids, target_probs, gain, embed, proj):
    nodes, width = feats.shape
    full_rows = proj.shape[0]
    share = nodes // nd
    vocab = embed.shape[0]
    slots = nodes // 2
    chips = nd // 2
    quarter = nz // 2
    per = chips // quarter
    vm = pltpu.VMEM
    scratch = [
        vm((2, -(-vocab // 256) * 256, width), BF16),
        vm((nodes, nodes), BF16),
        vm((nodes, 128), BF16),
        vm((nd, share, 128), BF16),
        vm((nd, share, 128), BF16),
        vm((nd, share, width), BF16),
        vm((nd, share, width), BF16),
        vm((slots, nodes), BF16),
        vm((128, slots), F32),
        vm((chips, 8, CAPL), F32),
        vm((chips, 8, CAPL), F32),
        vm((chips, CAP, width), BF16),
        vm((chips, CAP, width), BF16),
        vm((nz, slots, width), BF16),
        vm((nz, width, slots), BF16),
        vm((slots, width), F32),
        vm((slots, width), BF16),
        vm((chips // GROUP, GROUP * CAP, slots), BF16),
        vm((chips // GROUP, slots, GROUP * CAPL), BF16),
        vm((GROUP * CAPL, 128), BF16),
        vm((chips // GROUP, GROUP * CAP, 128), BF16),
        vm((slots, 128), F32),
        vm((16, slots), F32),
        vm((nz, 16, slots), F32),
        vm((GROUP * CAPL, width), BF16),
        vm((slots, width), F32),
        vm((slots, width), BF16),
        vm((quarter, width, width), BF16),
        vm((quarter, width, width), BF16),
        vm((quarter, width, width), F32),
        vm((chips, width // per, width), BF16),
        vm((chips, width // per, width), BF16),
        vm((2, chips, width // per, width), BF16),
        vm((8, 128), F32),
        vm((nz, 8, 128), F32),
        vm((8, 128), F32),
        vm((nd, 8, 128), F32),
    ]
    dma = pltpu.SemaphoreType.DMA
    for count in (
        2, 2, nd, nd, nd, nd, chips, chips, chips, chips,
        nz, nz, nz, nz, nz, nz, quarter, quarter,
        chips, chips, chips, chips, chips, chips, nz, nz, nd, nd,
    ):
        scratch.append(dma((count,)))
    in_vmem = pl.BlockSpec(memory_space=pltpu.VMEM)
    out, stat = pl.pallas_call(
        functools.partial(step_kernel, nd, nz, full_rows),
        out_shape=(
            jax.ShapeDtypeStruct(proj.shape, BF16),
            jax.ShapeDtypeStruct((8, 128), F32),
        ),
        in_specs=[pl.BlockSpec(memory_space=pltpu.SMEM)] + [in_vmem] * 8,
        out_specs=(in_vmem, in_vmem),
        scratch_shapes=scratch,
        compiler_params=pltpu.CompilerParams(
            collective_id=0, has_side_effects=True, vmem_limit_bytes=60 * 1024 * 1024
        ),
        name="step",
    )(
        counts, cand_ids.T, target_probs.T, parent.reshape(8, nodes // 8), accepted.reshape(8, nodes // 8),
        feats, gain.reshape(1, width), embed, proj,
    )
    return out, stat


def every(x, axis):
    n = lax.axis_size(axis)
    return lax.all_to_all(jnp.broadcast_to(x[None], (n,) + x.shape), axis, 0, 0, tiled=True)


def total(x, axis):
    return jnp.sum(every(jnp.atleast_1d(x), axis), axis=0).reshape(x.shape)


def wide_step(feats, parent, counts, accepted, cand_ids, target_probs, gain, embed, proj):
    node_rows, width_part = feats.shape
    full_width = proj.shape[0]
    group = lax.axis_index("dp")
    groups = lax.axis_size("dp")
    shard_rows = embed.shape[0]
    cand_count = cand_ids.shape[1]
    scale_in = 1.0 / jnp.sqrt(jnp.float32(full_width))
    gain_f = gain.astype(jnp.float32)
    flat_ids = cand_ids.reshape(-1)
    requests = flat_ids.shape[0]
    capacity = 3 * requests // (2 * groups)
    owners = flat_ids // shard_rows
    local_ids = flat_ids - owners * shard_rows
    member = owners[:, None] == jnp.arange(groups, dtype=jnp.int32)[None, :]
    per_owner = jnp.sum(member.astype(jnp.int32), axis=0)
    starts = jnp.cumsum(per_owner) - per_owner
    my_start = jnp.sum(jnp.where(member, starts[None, :], 0), axis=1)
    order = jnp.argsort(owners, stable=True)
    ranks = jnp.arange(requests, dtype=jnp.int32) - my_start[order]
    slots = owners[order] * capacity + ranks
    outgoing = jnp.zeros((groups * capacity,), jnp.int32).at[slots].set(local_ids[order])
    placed = jnp.zeros((requests,), jnp.int32).at[order].set(slots)
    mixed = (feats.astype(jnp.float32) + feats[parent].astype(jnp.float32)).astype(jnp.bfloat16)
    piece = every(mixed, "mp").transpose(1, 0, 2).reshape(node_rows, full_width)
    partial_value = jnp.dot(piece, proj, preferred_element_type=jnp.float32)
    whole = piece
    partial_value, whole = (partial_value, whole)
    hidden = partial_value * scale_in
    squares = total(jnp.sum(hidden * hidden, axis=1), "mp")
    recip = lax.rsqrt(squares / full_width + 1e-05)
    normed = (hidden * recip[:, None] * gain_f).astype(jnp.bfloat16)
    found = embed[
        lax.all_to_all(
            outgoing.reshape(groups, capacity), "dp", split_axis=0, concat_axis=0, tiled=True
        )
    ]
    fetched = lax.all_to_all(found, "dp", split_axis=0, concat_axis=0, tiled=True)
    cand_rows = fetched.reshape(groups * capacity, width_part)[placed].reshape(
        node_rows, cand_count, width_part
    )
    part_scores = jnp.einsum("nkd,nd->nk", cand_rows, normed, preferred_element_type=jnp.float32)
    scores = total(part_scores, "mp")
    logp = scores - jnp.log(jnp.sum(jnp.exp(scores), axis=1, keepdims=True))
    prob = jnp.exp(logp)
    probs = target_probs.astype(jnp.float32)
    target = probs / jnp.sum(probs, axis=1, keepdims=True)
    kl_node = jnp.sum(target * (jnp.log(target) - logp), axis=1)
    live_count = lax.dynamic_index_in_dim(counts, group, 0, keepdims=False)
    live = jnp.arange(node_rows, dtype=jnp.int32) < live_count
    weight = jnp.where(live, 1 + accepted, 0).astype(jnp.float32)
    num, den = total(jnp.stack([jnp.sum(weight * kl_node), jnp.sum(weight)]), "dp")
    grad_scores = weight[:, None] * (prob - target)
    dnormed = jnp.einsum("nk,nkd->nd", grad_scores, cand_rows, preferred_element_type=jnp.float32)
    inner = total(jnp.sum(dnormed * gain_f * hidden, axis=1), "mp")
    dhidden = (
        recip[:, None] * gain_f * dnormed - hidden * (recip**3 * inner / full_width)[:, None]
    ).astype(jnp.bfloat16)
    grad_part = (
        lax.dot_general(
            whole, dhidden, (((0,), (0,)), ((), ())), preferred_element_type=jnp.float32
        )
        * scale_in
    )
    shares = lax.all_to_all(grad_part.reshape(groups, -1, width_part), "dp", 0, 0, tiled=True)
    grad = every(jnp.sum(shares, axis=0), "dp").reshape(full_width, width_part)
    energy = total(jnp.sum(grad * grad), "mp")
    factor = lax.rsqrt(energy / (full_width * full_width) + 1e-06)
    new_proj = (proj.astype(jnp.float32) - 0.5 * grad * factor).astype(jnp.bfloat16)
    return (new_proj, num / den)


def solution(mesh):
    nd = mesh.shape["dp"]
    nz = mesh.shape["mp"]

    def per_device(*args):
        out, stat = fast_step(nd, nz, *args)
        return lax.cond(
            stat[1, 0] > 0.0,
            lambda: wide_step(*args),
            lambda: (out, stat[0, 0]),
        )

    placed = (
        P("dp", "mp"),
        P("dp"),
        P(),
        P("dp"),
        P("dp", None),
        P("dp", None),
        P("mp"),
        P("dp", "mp"),
        P(None, "mp"),
    )
    return jax.shard_map(
        per_device, mesh=mesh, in_specs=placed, out_specs=(P(None, "mp"), P()), check_vma=False
    )
```

```python
import functools
import jax
import jax.numpy as jnp
from jax import lax
from jax.experimental import pallas as pl
from jax.experimental.pallas import tpu as pltpu
from jax.sharding import PartitionSpec as P

MESH = pl.DeviceIdType.MESH
F32 = jnp.float32
BF16 = jnp.bfloat16
I32 = jnp.int32

GROUP = 4
MIXLATE = 1
CAP = 352
CAPL = 384
HALF = 224


def dot(a, b):
    return jnp.dot(a, b, preferred_element_type=F32)


def dot_nt(a, b):
    return lax.dot_general(a, b, (((1,), (1,)), ((), ())), preferred_element_type=F32)


def one_hot(hit):
    return jnp.where(hit, 1.0, 0.0).astype(BF16)


def iota(shape, axis):
    return lax.broadcasted_iota(I32, shape, axis)


def step_kernel(
    nd, nz, full_rows,
    counts, ids, odds, parent, accepted, gain2, feats_in, embed_in, proj_in,
    out, loss_out, flag_out,
    feats, embed, proj, in_s, emb, perm, meta, mixat, metap, metar, mixp, mixr, live, metat,
    lists, sendid, idr, rows_out, rows_in, whole, whole_t, hidden, ng,
    pick_t, ksel_t, asked, sct, zsend, zr, dh,
    pair_out, pair_in, gown, rs_out, rs_in, gfull, sb_out, sb, ez_out, ez, dt_out, dt,
    emb_s, emb_r, meta_s, meta_r, mix_s, mix_r, id_s, id_r, row_s, row_r,
    zr_s, zr_r, zl_s, zl_r, zx_s, zx_r, pair_s, pair_r,
    rs_s, rs_r, ag_s, ag_r, fw_s, fw_r, sb_s, sb_r, ez_s, ez_r, dt_s, dt_r,
):
    me = lax.axis_index("dp")
    z = lax.axis_index("mp")
    nodes = feats.shape[0]
    width = feats.shape[1]
    slots = live.shape[1]
    share = nodes // nd
    core = lax.rem(me, 2)
    chip = lax.div(me, 2)
    chips = nd // 2
    sibling = me + 1 - 2 * core
    vocab = embed.shape[0]

    sent = []

    fetch = [
        pltpu.make_async_copy(src, dst, in_s.at[i])
        for i, (src, dst) in enumerate(((feats_in, feats), (embed_in, embed), (proj_in, proj)))
    ]
    for f in fetch:
        f.start()

    def copy(src, dst, ss, rs, d, zz):
        return pltpu.make_async_remote_copy(
            src_ref=src, dst_ref=dst, send_sem=ss, recv_sem=rs,
            device_id=(d, zz), device_id_type=MESH,
        )

    def nxt(i):
        return lax.rem(me + i, nd)

    def prv(i):
        return lax.rem(me - i + nd, nd)

    def loop(lo, hi, body):
        def wrapped(i, carry):
            body(i)
            return carry
        lax.fori_loop(lo, hi, wrapped, 0)

    side = int(chips ** 0.5)
    chip_x = lax.rem(chip, side)
    chip_y = lax.div(chip, side)

    def offset(i):
        dx = lax.rem(i, side)
        dy = lax.rem(lax.div(i, side) + i, side)
        return dx + core * (dy - dx), dy + core * (dx - dy)

    def to_chip(i):
        dx, dy = offset(i)
        return lax.rem(chip_y + dy, side) * side + lax.rem(chip_x + dx, side)

    def from_chip(i):
        dx, dy = offset(i)
        return lax.rem(chip_y - dy + side, side) * side + lax.rem(chip_x - dx + side, side)

    def chip_copy(src, dst, ss, rs, p):
        return copy(src.at[p], dst.at[chip], ss.at[p], rs.at[chip], p * 2 + core, z)

    def chip_wait(src, dst, ss, rs, p):
        copy(src.at[p], dst.at[p], ss.at[p], rs.at[p], p * 2 + core, z).wait_recv()

    def chip_sent_all(src, dst, ss, rs):
        loop(1, chips, lambda i: chip_copy(src, dst, ss, rs, to_chip(i)).wait_send())

    def dp_copy(src, dst, ss, rs, d):
        return copy(src.at[d], dst.at[me], ss.at[d], rs.at[me], d, z)

    def dp_wait(src, dst, ss, rs, h):
        copy(src.at[h], dst.at[h], ss.at[h], rs.at[h], h, z).wait_recv()

    def each_device(act):
        act(sibling)

        def both(i):
            act(to_chip(i) * 2 + core)
            act(to_chip(i) * 2 + 1 - core)

        loop(1, chips, both)

    def each_source(act):
        act(sibling)

        def both(i):
            act(from_chip(i) * 2 + core)
            act(from_chip(i) * 2 + 1 - core)

        loop(1, chips, both)

    def dp_send_all(src, dst, ss, rs):
        each_device(lambda d: dp_copy(src, dst, ss, rs, d).start())
        sent.append(lambda: dp_sent_all(src, dst, ss, rs))

    def dp_wait_all(src, dst, ss, rs):
        each_source(lambda h: dp_wait(src, dst, ss, rs, h))

    def dp_sent_all(src, dst, ss, rs):
        each_device(lambda d: dp_copy(src, dst, ss, rs, d).wait_send())

    barrier = pltpu.get_barrier_semaphore()
    loop(1, nd, lambda i: pl.semaphore_signal(barrier, inc=1, device_id=(nxt(i), z), device_id_type=MESH))
    loop(1, nz, lambda i: pl.semaphore_signal(barrier, inc=1, device_id=(me, lax.rem(z + i, nz)), device_id_type=MESH))

    pair_rows = share // 2
    node_lane = iota((1, nodes), 1)
    src_lane = iota((1, slots), 1)
    lane_h = lax.div(src_lane, pair_rows)
    lane_j = 2 * (src_lane - lane_h * pair_rows)

    def deal(h, state):
        off, mine, into0, into1 = state
        count = counts[h]
        first = (me - off) & (nd - 1)
        base = (off + first) // nd
        row0 = jnp.where(lane_j * nd + first < count, base + lane_j, -1)
        row1 = jnp.where((lane_j + 1) * nd + first < count, base + lane_j + 1, -1)
        here = lane_h == h
        return (
            off + count, jnp.where(h == me, off, mine),
            jnp.where(here, row0, into0), jnp.where(here, row1, into1),
        )

    none = jnp.full((1, slots), -1, I32)
    _, mine, into0, into1 = lax.fori_loop(0, nd, deal, (jnp.int32(0), jnp.int32(0), none, none))
    place_j = lax.div(node_lane, nd)
    dealt = (
        ((node_lane + mine) & (nd - 1)) * share
        + (place_j & 1) * pair_rows + lax.div(place_j, 2)
    )
    gain = jnp.concatenate([gain2[0:1, :], gain2[1:2, :]], axis=1).astype(F32)

    def in_row(ref):
        return jnp.concatenate([ref[r:r + 1, :] for r in range(ref.shape[0])], axis=1)

    idf = ids[...].astype(F32)
    own_f = jnp.floor((idf + 0.5) * (1.0 / float(vocab)))
    at_f = idf - own_f * float(vocab)
    hi_f = jnp.floor(at_f * (1.0 / 256.0))
    par = in_row(parent)
    extra = jnp.concatenate(
        [
            in_row(accepted).astype(F32),
            (par // 32).astype(F32),
            (par % 32).astype(F32),
            jnp.zeros((5, nodes), F32),
        ],
        axis=0,
    )
    table = jnp.concatenate(
        [own_f, hi_f + 1.0, at_f - 256.0 * hi_f, odds[...].astype(F32), extra, jnp.zeros((88, nodes), F32)],
        axis=0,
    )
    meta[...] = table.T.astype(BF16)

    step = 128

    def perm_block(b):
        rows = pl.ds(b * step, step)
        e = one_hot(iota((step, nodes), 0) + b * step == dealt)
        perm[rows, :] = e
        m = dot(e, meta[...])
        mixat[rows, :] = m
        m = m.astype(BF16).reshape(step // share, 2, pair_rows, 128)
        metap[pl.ds(b * (step // share), step // share)] = jnp.concatenate(
            [m[:, 0, :, 0:64], m[:, 1, :, 0:64]], axis=-1
        )

    loop(0, nodes // step, perm_block)

    fetch[1].wait()
    block = emb.shape[1]
    even = vocab // 32 * 32
    emb[core, 0:even, :] = embed[0:even, :]
    emb[core, even:block, :] = jnp.concatenate(
        [embed[even:vocab, :].astype(F32), jnp.zeros((block - vocab, width), F32)], axis=0
    ).astype(BF16)
    pl.semaphore_wait(barrier, nd - 1 + nz - 1)

    def emb_copy(c):
        return copy(emb.at[c], emb.at[c], emb_s.at[c], emb_r.at[c], sibling, z)

    emb_copy(core).start()
    sent.append(lambda: emb_copy(core).wait_send())
    dp_send_all(metap, metar, meta_s, meta_r)
    metar[me] = metap[me]

    def mixp_block(b):
        rows = pl.ds(b * step, step)
        at = mixat[rows, 33:34] * 32.0 + mixat[rows, 34:35]
        p = one_hot(iota((step, nodes), 1) == at.astype(I32))
        mixp[pl.ds(b * (step // share), step // share)] = (
            dot(perm[rows, :] + p, feats[...])
            .astype(BF16)
            .reshape(step // share, share, width)
        )

    fetch[0].wait()
    loop(0, nodes // step, mixp_block)
    if not MIXLATE:
        dp_send_all(mixp, mixr, mix_s, mix_r)
    mixr[me] = mixp[me]

    def live_block(b):
        at = iota((step, slots), 0) + b * step
        live[0, pl.ds(b * step, step), :] = one_hot(at == into0)
        live[1, pl.ds(b * step, step), :] = one_hot(at == into1)

    loop(0, slots // step, live_block)

    dp_wait_all(metap, metar, meta_s, meta_r)
    for b in range(slots // step):
        rows = slice(b * step, (b + 1) * step)
        got = metar[...].reshape(slots, metar.shape[2])
        part = dot(live[0, rows, :], got)[:, 0:64] + dot(live[1, rows, :], got)[:, 64:128]
        metat[:, rows] = part.T

    owner = metat[0:8, :].astype(I32)
    upper = one_hot(iota((slots, slots), 0) < iota((slots, slots), 1))
    own_iota = iota((nd, slots), 0)
    member = jnp.concatenate(
        [jnp.where(own_iota == owner[k:k + 1, :], 1.0, 0.0) for k in range(8)], axis=0
    )
    before = dot(member.astype(BF16), upper)
    carry = jnp.zeros((nd, 1), F32)
    found = jnp.zeros((chips * 8, CAPL), F32)
    asks = jnp.zeros((chips, 1), F32)
    at_chip = owner // 2
    odd_core = owner - 2 * at_chip
    chip_iota = iota((chips, slots), 0)
    node_row = iota((1, slots), 1)
    for k in range(8):
        mk = member[k * nd:(k + 1) * nd, :]
        rank = jnp.sum(mk * (before[k * nd:(k + 1) * nd, :] + carry), axis=0, keepdims=True)
        carry = carry + jnp.sum(mk, axis=1, keepdims=True)
        odd_k = odd_core[k:k + 1, :].astype(F32)
        place = rank + odd_k * (float(CAP - 1) - 2.0 * rank)
        asks = asks + jnp.sum(jnp.where(chip_iota == at_chip[k:k + 1, :], 1.0, 0.0), axis=1, keepdims=True)
        fields = jnp.concatenate(
            [
                metat[8 + k:9 + k, :] + float(block // 256) * odd_k,
                metat[16 + k:17 + k, :],
                (node_row // 2).astype(F32),
                ((node_row % 2) * 8 + (k + 1)).astype(F32),
                jnp.zeros((4, slots), F32),
            ],
            axis=0,
        )
        here = iota((chips, 8, slots), 0) == at_chip[k:k + 1, :][None]
        f = jnp.where(here, fields[None], 0.0).reshape(chips * 8, slots).astype(BF16)
        at = one_hot(iota((CAPL, slots), 0) == place.astype(I32))
        found = found + dot_nt(f, at)
    found = found.reshape(chips, 8, CAPL)
    lists[...] = found
    tiles = CAPL // 128
    sendid[...] = jnp.concatenate(
        [found[:, f:f + 1, t * 128:(t + 1) * 128] for f in range(2) for t in range(tiles)]
        + [jnp.zeros((chips, 8 - 2 * tiles, 128), F32)],
        axis=1,
    )
    over = jnp.maximum(
        jnp.max(jnp.where(carry > float(HALF), 1.0, 0.0), axis=0, keepdims=True),
        jnp.max(jnp.where(asks > float(CAP), 1.0, 0.0), axis=0, keepdims=True),
    )
    loop(1, chips, lambda i: chip_copy(sendid, idr, id_s, id_r, to_chip(i)).start())
    sent.append(lambda: chip_sent_all(sendid, idr, id_s, id_r))
    idr[chip] = sendid[chip]
    if MIXLATE:
        dp_send_all(mixp, mixr, mix_s, mix_r)

    def owner_at(j, q):
        return from_chip(j * GROUP + q + 1)

    groups = chips // GROUP

    def pick_group(j):
        for q in range(GROUP):
            a = lists[owner_at(j, q), 2:3, :]
            b = lists[owner_at(j, q), 3:4, :]
            odd = jnp.where(b - 1.0 >= 8.0, 1.0, 0.0)
            node = jnp.where(b > 0.0, 2.0 * a + odd, -1.0).astype(I32)
            k = jnp.where(b > 0.0, b - 1.0 - 8.0 * odd, -1.0).astype(I32)
            pick_t[j, :, q * CAPL:(q + 1) * CAPL] = one_hot(iota((slots, CAPL), 0) == node)
            ksel_t[j, :, q * CAPL:(q + 1) * CAPL] = jnp.where(iota((8, CAPL), 0) == k, 1.0, 0.0)

    def ask_group(j):
        got = lax.dot_general(pick_t[j], ng[...], (((0,), (0,)), ((), ())), preferred_element_type=F32)
        asked[j] = got.astype(BF16)

    def score(j, arrivals):
        for q in range(arrivals):
            wait_row(j * GROUP + q + 1)
        got = rows_in[j * GROUP:(j + 1) * GROUP].reshape(GROUP * CAPL, width).astype(F32)
        s = jnp.sum(got * asked[j].astype(F32), axis=1, keepdims=True)
        s = jnp.broadcast_to(s, (GROUP * CAPL, 128)).T[0:8, :]
        s_hi = s.astype(BF16).astype(F32)
        by_k = jnp.concatenate([s_hi * ksel_t[j], (s - s_hi) * ksel_t[j]], axis=0).astype(BF16)
        return dot_nt(by_k, pick_t[j])

    def mix_in():
        dp_wait_all(mixp, mixr, mix_s, mix_r)
        for b in range(slots // step):
            rows = slice(b * step, (b + 1) * step)
            part = dot(live[0, rows, :], mixr[:, 0:pair_rows, :].reshape(slots, width)) + dot(
                live[1, rows, :], mixr[:, pair_rows:share, :].reshape(slots, width)
            )
            whole[z, rows, :] = part.astype(BF16)

    if not MIXLATE:
        mix_in()
    zright = lax.rem(z + 1, nz)
    zleft = lax.rem(z + nz - 1, nz)

    def ring_part(s, first):
        if s + 1 < nz // 2:
            return pl.ds(0, slots)
        return pl.ds(first * (slots // 2), slots // 2)

    def ring_copy(s, b, side_r):
        rows = ring_part(s, 0 if side_r else 1)
        ss, rs = (zr_s, zr_r) if side_r else (zl_s, zl_r)
        return copy(
            whole.at[b, rows], whole.at[b, rows], ss.at[s], rs.at[s], me, zright if side_r else zleft
        )

    def ring_right(s):
        return ring_copy(s, lax.rem(z - s + nz, nz), True)

    def ring_left(s):
        return ring_copy(s, lax.rem(z + s, nz), False)

    def got_right(s):
        b = lax.rem(z - s - 1 + nz, nz)
        ring_copy(s, b, True).wait_recv()
        return b

    def got_left(s):
        b = lax.rem(z + s + 1, nz)
        ring_copy(s, b, False).wait_recv()
        return b

    hops = nz // 2
    if not MIXLATE:
        ring_right(0).start()
        ring_left(0).start()
    for j in range(groups):
        pick_group(j)
    scale = 1.0 / (float(full_rows) ** 0.5)

    def use_block(b, first=False):
        blk = whole[b]
        whole_t[b] = blk.T
        h = dot(blk, proj[pl.ds(pl.multiple_of(b * width, width), width), :])
        if first:
            hidden[...] = h
        else:
            hidden[...] += h

    chunk = 256

    low = CAP - HALF

    def serve(h):
        cols = idr[h].T
        hi = jnp.concatenate([cols[:, t:t + 1] for t in range(tiles)], axis=0)[:CAP]
        lo = jnp.concatenate([cols[:, tiles + t:tiles + t + 1] for t in range(tiles)], axis=0)[:CAP]
        hi = jnp.broadcast_to(hi, (CAP, chunk)).astype(BF16)
        lo = one_hot(iota((CAP, chunk), 1) == lo.astype(I32))
        halves = []
        for c in range(2):
            first = c * low
            parts = [
                jnp.where(
                    hi[first:first + HALF, :] == jnp.bfloat16(c * (block // chunk) + i + 1),
                    lo[first:first + HALF, :],
                    jnp.bfloat16(0),
                )
                for i in range(block // chunk)
            ]
            halves.append(dot(jnp.concatenate(parts, axis=1), emb[c]))
        front, rear = halves
        rows_out[h, 0:low, :] = front[0:low, :].astype(BF16)
        rows_out[h, low:HALF, :] = (front[low:, :] + rear[:HALF - low, :]).astype(BF16)
        rows_out[h, HALF:CAP, :] = rear[HALF - low:, :].astype(BF16)

    def row_copy(i):
        p = to_chip(i)
        used = pl.ds(0, CAP)
        return copy(
            rows_out.at[p, used], rows_in.at[i - 1, used], row_s.at[p], row_r.at[i - 1], p * 2 + core, z
        )

    def wait_row(i):
        p = from_chip(i)
        used = pl.ds(0, CAP)
        copy(
            rows_out.at[p, used], rows_in.at[i - 1, used], row_s.at[p], row_r.at[i - 1], p * 2 + core, z
        ).wait_recv()

    def serve_far(i):
        h = to_chip(i)
        chip_wait(sendid, idr, id_s, id_r, h)
        serve(h)
        row_copy(i).start()

    emb_copy(1 - core).wait_recv()
    fetch[2].wait()
    done = 1
    if MIXLATE:
        loop(done, 4, serve_far)
        done = 4
        mix_in()
        ring_right(0).start()
        ring_left(0).start()
    use_block(z, True)
    for s in range(hops):
        upto = min(done + 5, chips)
        loop(done, upto, serve_far)
        done = upto
        if s + 2 == hops:
            loop(done, chips, serve_far)
            done = chips
            serve(chip)
        b = got_right(s)
        if s + 1 < hops:
            ring_right(s + 1).start()
            use_block(b)
        b = got_left(s)
        if s + 1 < hops:
            ring_left(s + 1).start()
        use_block(b)
    rows_in[chips - 1, 0:CAP, :] = rows_out[chip, 0:CAP, :]
    rows_in[:, CAP:CAPL, :] = jnp.zeros((chips, CAPL - CAP, width), BF16)
    sent.append(lambda: loop(1, chips, lambda i: row_copy(i).wait_send()))
    for s in range(hops):
        sent.append(functools.partial(lambda s: ring_right(s).wait_send(), s))
        sent.append(functools.partial(lambda s: ring_left(s).wait_send(), s))

    hid = hidden[...] * scale
    hidden[...] = hid
    square = jnp.sum(hid * hid, axis=1, keepdims=True)
    ng[...] = (hid * gain).astype(BF16)
    square = jnp.broadcast_to(square, (slots, 128)).T[0:1, :]
    for j in range(groups):
        ask_group(j)
    got = score(0, GROUP)
    for j in range(1, groups):
        got = got + score(j, GROUP - (j + 1) // groups)

    zsend[:, 0:slots] = got[0:8, :] + got[8:16, :]
    folds = slots // 128
    zsend[:, slots:slots + 128] = jnp.concatenate(
        [square[:, f * 128:(f + 1) * 128] for f in range(folds)] + [jnp.zeros((8 - folds, 128), F32)], axis=0
    )

    def zx(i):
        zz = lax.rem(z + i, nz)
        return copy(zsend, zr.at[z], zx_s.at[zz], zx_r.at[z], me, zz)

    def zx_wait(i):
        zz = lax.rem(z + i, nz)
        copy(zsend, zr.at[zz], zx_s.at[zz], zx_r.at[zz], me, zz).wait_recv()

    loop(1, nz, lambda i: zx(i).start())
    sent.append(lambda: loop(1, nz, lambda i: zx(i).wait_send()))
    zr[z] = zsend[...]
    loop(1, nz, zx_wait)
    tot = zr[0]
    for i in range(1, nz):
        tot = tot + zr[i]
    raw = tot[:, 0:slots]
    squares = jnp.concatenate([tot[f:f + 1, slots:slots + 128] for f in range(folds)], axis=1)
    recip = lax.rsqrt(squares / float(full_rows) + 1e-05)
    scores = raw * recip
    logp = scores - jnp.log(jnp.sum(jnp.exp(scores), axis=0, keepdims=True))
    prob = jnp.exp(logp)
    probs = metat[24:32, :]
    target = probs / jnp.sum(probs, axis=0, keepdims=True)
    kl = jnp.sum(target * (jnp.log(target) - logp), axis=0, keepdims=True)
    weight = 1.0 + metat[32:33, :]
    num = jnp.sum(weight * kl, axis=1, keepdims=True)
    den = jnp.sum(weight, axis=1, keepdims=True)
    gs = weight * (prob - target)
    inner = jnp.sum(gs * raw, axis=0, keepdims=True)
    back = recip * recip * recip * inner * (1.0 / float(full_rows))
    gs_hi = gs.astype(BF16).astype(F32)
    gs16 = jnp.concatenate([gs_hi, gs - gs_hi], axis=0).astype(BF16)
    coef = jnp.concatenate([recip, back, jnp.zeros((6, slots), F32)], axis=0).T

    for j in range(groups):
        g16 = dot(gs16, pick_t[j])
        g = jnp.sum((g16[0:8, :] + g16[8:16, :]) * ksel_t[j], axis=0, keepdims=True)
        scaled = pick_t[j] * g.astype(BF16)
        part = dot(scaled, rows_in[j * GROUP:(j + 1) * GROUP].reshape(GROUP * CAPL, width))
        dnormed = part if j == 0 else dnormed + part
    dh[...] = (coef[:, 0:1] * gain * dnormed - hidden[...] * coef[:, 1:2]).astype(BF16)

    quarter = nz // 2

    def pair(q):
        return copy(pair_out.at[q], pair_in.at[q], pair_s.at[q], pair_r.at[q], sibling, z)

    def turn(q):
        return lax.rem(chip_y + q, quarter)

    for q in range(quarter):
        pair_out[q] = (dot(whole_t[(1 - core) * quarter + turn(q)], dh[...]) * scale).astype(BF16)
        pair(q).start()
    for q in range(quarter):
        gown[q] = dot(whole_t[core * quarter + turn(q)], dh[...]) * scale
    per = chips // quarter

    def rs_copy(p):
        return chip_copy(rs_out, rs_in, rs_s, rs_r, p)

    for q in range(quarter):
        pair(q).wait_recv()
        both = gown[q] + pair_in[q].astype(F32)
        first = turn(q) * per
        rs_out[pl.ds(first, per)] = both.astype(BF16).reshape(per, width // per, width)
        for i in range(1 if q == 0 else 0, per):
            rs_copy(first + lax.rem(chip_x + i, per)).start()
    for q in range(quarter):
        sent.append(functools.partial(lambda q: pair(q).wait_send(), q))

    def chip_got(src, dst, ss, rs):
        loop(1, chips, lambda i: chip_wait(src, dst, ss, rs, from_chip(i)))

    sent.append(lambda: chip_sent_all(rs_out, rs_in, rs_s, rs_r))
    rs_in[chip] = rs_out[chip]
    chip_got(rs_out, rs_in, rs_s, rs_r)
    shard = rs_in[0].astype(F32)
    for p in range(1, chips):
        shard = shard + rs_in[p].astype(F32)
    gfull[core, chip] = shard.astype(BF16)
    energy = jnp.sum(jnp.sum(shard * shard, axis=1, keepdims=True), axis=0, keepdims=True)
    row = iota((8, 128), 0)
    tile = jnp.where(row == 0, energy, jnp.where(row == 1, num, jnp.where(row == 2, den, over)))

    sb_out[...] = tile
    both_cores = copy(sb_out, sb, sb_s.at[0], sb_r.at[0], sibling, z)
    both_cores.start()

    def ezc(i):
        zz = lax.rem(z + i, nz)
        return copy(ez_out, ez.at[z], ez_s.at[zz], ez_r.at[z], me, zz)

    def ezc_wait(i):
        zz = lax.rem(z + i, nz)
        copy(ez_out, ez.at[zz], ez_s.at[zz], ez_r.at[zz], me, zz).wait_recv()

    def ag(i):
        p = to_chip(i)
        return copy(gfull.at[core, chip], gfull.at[core, chip], ag_s.at[p], ag_r.at[chip], p * 2 + core, z)

    def ag_wait(i):
        p = from_chip(i)
        copy(gfull.at[core, p], gfull.at[core, p], ag_s.at[p], ag_r.at[p], p * 2 + core, z).wait_recv()
        return p

    def forward(p):
        return copy(gfull.at[core, p], gfull.at[core, p], fw_s.at[p], fw_r.at[p], sibling, z)

    def forward_wait(p):
        copy(gfull.at[1 - core, p], gfull.at[1 - core, p], fw_s.at[p], fw_r.at[p], sibling, z).wait_recv()

    sent.append(both_cores.wait_send)
    sent.append(lambda: loop(1, nz, lambda i: ezc(i).wait_send()))
    sent.append(lambda: loop(1, chips, lambda i: ag(i).wait_send()))
    sent.append(lambda: loop(0, chips, lambda p: forward(p).wait_send()))

    loop(1, chips, lambda i: ag(i).start())
    forward(chip).start()
    both_cores.wait_recv()
    tile = tile + sb[...]
    ez_out[...] = tile
    loop(1, nz, lambda i: ezc(i).start())
    ez[z] = tile
    loop(1, nz, ezc_wait)
    etot = ez[0]
    for i in range(1, nz):
        etot = etot + ez[i]
    tile = jnp.where(row == 0, etot, tile)
    dt_out[...] = tile

    def dtc(i):
        p = to_chip(i)
        return copy(dt_out, dt.at[chip], dt_s.at[p], dt_r.at[chip], p * 2 + core, z)

    def dtc_wait(i):
        p = from_chip(i)
        copy(dt_out, dt.at[p], dt_s.at[p], dt_r.at[p], p * 2 + core, z).wait_recv()

    loop(1, chips, lambda i: dtc(i).start())
    sent.append(lambda: loop(1, chips, lambda i: dtc(i).wait_send()))
    dt[chip] = tile

    def ag_pass(i):
        p = ag_wait(i)
        forward(p).start()

    loop(1, chips, ag_pass)
    loop(1, chips, dtc_wait)
    total = dt[0]
    for i in range(1, chips):
        total = total + dt[i]
    entries = float(full_rows) * float(full_rows)
    factor = 0.5 * lax.rsqrt(total[0:1, 0:1] / entries + 1e-06)
    loss_out[...] = total[1:2, 0:1] / total[2:3, 0:1]
    flag_out[...] = total[3:4, 0:1]

    blk_rows = width // per

    def finish(h, p):
        r = pl.ds(pl.multiple_of((h * chips + p) * blk_rows, blk_rows), blk_rows)
        out[r, :] = (proj[r, :].astype(F32) - gfull[h, p].astype(F32) * factor).astype(BF16)

    loop(0, chips, lambda p: finish(core, p))

    def finish_far(p):
        forward_wait(p)
        finish(1 - core, p)

    loop(0, chips, finish_far)

    for wait in sent:
        wait()


def fast_step(nd, nz, feats, parent, counts, accepted, cand_ids, target_probs, gain, embed, proj):
    nodes, width = feats.shape
    full_rows = proj.shape[0]
    share = nodes // nd
    vocab = embed.shape[0]
    slots = nodes // 2
    chips = nd // 2
    quarter = nz // 2
    per = chips // quarter
    vm = pltpu.VMEM
    scratch = [
        vm(feats.shape, BF16),
        vm(embed.shape, BF16),
        vm(proj.shape, BF16),
        pltpu.SemaphoreType.DMA((3,)),
        vm((2, -(-vocab // 256) * 256, width), BF16),
        vm((nodes, nodes), BF16),
        vm((nodes, 128), BF16),
        vm((nodes, 128), F32),
        vm((nd, share // 2, 128), BF16),
        vm((nd, share // 2, 128), BF16),
        vm((nd, share, width), BF16),
        vm((nd, share, width), BF16),
        vm((2, slots, slots), BF16),
        vm((64, slots), F32),
        vm((chips, 8, CAPL), F32),
        vm((chips, 8, 128), F32),
        vm((chips, 8, 128), F32),
        vm((chips, CAPL, width), BF16),
        vm((chips, CAPL, width), BF16),
        vm((nz, slots, width), BF16),
        vm((nz, width, slots), BF16),
        vm((slots, width), F32),
        vm((slots, width), BF16),
        vm((chips // GROUP, slots, GROUP * CAPL), BF16),
        vm((chips // GROUP, 8, GROUP * CAPL), F32),
        vm((chips // GROUP, GROUP * CAPL, width), BF16),
        vm((16, slots), F32),
        vm((8, slots + 128), F32),
        vm((nz, 8, slots + 128), F32),
        vm((slots, width), BF16),
        vm((quarter, width, width), BF16),
        vm((quarter, width, width), BF16),
        vm((quarter, width, width), F32),
        vm((chips, width // per, width), BF16),
        vm((chips, width // per, width), BF16),
        vm((2, chips, width // per, width), BF16),
        vm((8, 128), F32),
        vm((8, 128), F32),
        vm((8, 128), F32),
        vm((nz, 8, 128), F32),
        vm((8, 128), F32),
        vm((chips, 8, 128), F32),
    ]
    dma = pltpu.SemaphoreType.DMA
    for count in (
        2, 2, nd, nd, nd, nd, chips, chips, chips, chips,
        nz, nz, nz, nz, nz, nz, quarter, quarter,
        chips, chips, chips, chips, chips, chips, 1, 1, nz, nz, chips, chips,
    ):
        scratch.append(dma((count,)))
    in_vmem = pl.BlockSpec(memory_space=pltpu.VMEM)
    return pl.pallas_call(
        functools.partial(step_kernel, nd, nz, full_rows),
        out_shape=(
            jax.ShapeDtypeStruct(proj.shape, BF16),
            jax.ShapeDtypeStruct((1, 1), F32),
            jax.ShapeDtypeStruct((1, 1), F32),
        ),
        in_specs=[pl.BlockSpec(memory_space=pltpu.SMEM)] + [in_vmem] * 5 + [pl.BlockSpec(memory_space=pl.ANY)] * 3,
        out_specs=(in_vmem, in_vmem, in_vmem),
        scratch_shapes=scratch,
        compiler_params=pltpu.CompilerParams(
            collective_id=0, has_side_effects=True, vmem_limit_bytes=60 * 1024 * 1024
        ),
        name="step",
    )(
        counts, cand_ids.T, target_probs.T, parent.reshape(8, nodes // 8), accepted.reshape(8, nodes // 8),
        gain.reshape(2, width // 2), feats, embed, proj,
    )


def every(x, axis):
    n = lax.axis_size(axis)
    return lax.all_to_all(jnp.broadcast_to(x[None], (n,) + x.shape), axis, 0, 0, tiled=True)


def total(x, axis):
    return jnp.sum(every(jnp.atleast_1d(x), axis), axis=0).reshape(x.shape)


def wide_step(feats, parent, counts, accepted, cand_ids, target_probs, gain, embed, proj):
    node_rows, width_part = feats.shape
    full_width = proj.shape[0]
    group = lax.axis_index("dp")
    groups = lax.axis_size("dp")
    shard_rows = embed.shape[0]
    cand_count = cand_ids.shape[1]
    scale_in = 1.0 / jnp.sqrt(jnp.float32(full_width))
    gain_f = gain.astype(jnp.float32)
    flat_ids = cand_ids.reshape(-1)
    requests = flat_ids.shape[0]
    capacity = 3 * requests // (2 * groups)
    owners = flat_ids // shard_rows
    local_ids = flat_ids - owners * shard_rows
    member = owners[:, None] == jnp.arange(groups, dtype=jnp.int32)[None, :]
    per_owner = jnp.sum(member.astype(jnp.int32), axis=0)
    starts = jnp.cumsum(per_owner) - per_owner
    my_start = jnp.sum(jnp.where(member, starts[None, :], 0), axis=1)
    order = jnp.argsort(owners, stable=True)
    ranks = jnp.arange(requests, dtype=jnp.int32) - my_start[order]
    slots = owners[order] * capacity + ranks
    outgoing = jnp.zeros((groups * capacity,), jnp.int32).at[slots].set(local_ids[order])
    placed = jnp.zeros((requests,), jnp.int32).at[order].set(slots)
    mixed = (feats.astype(jnp.float32) + feats[parent].astype(jnp.float32)).astype(jnp.bfloat16)
    piece = every(mixed, "mp").transpose(1, 0, 2).reshape(node_rows, full_width)
    partial_value = jnp.dot(piece, proj, preferred_element_type=jnp.float32)
    whole = piece
    partial_value, whole = (partial_value, whole)
    hidden = partial_value * scale_in
    squares = total(jnp.sum(hidden * hidden, axis=1), "mp")
    recip = lax.rsqrt(squares / full_width + 1e-05)
    normed = (hidden * recip[:, None] * gain_f).astype(jnp.bfloat16)
    found = embed[
        lax.all_to_all(
            outgoing.reshape(groups, capacity), "dp", split_axis=0, concat_axis=0, tiled=True
        )
    ]
    fetched = lax.all_to_all(found, "dp", split_axis=0, concat_axis=0, tiled=True)
    cand_rows = fetched.reshape(groups * capacity, width_part)[placed].reshape(
        node_rows, cand_count, width_part
    )
    part_scores = jnp.einsum("nkd,nd->nk", cand_rows, normed, preferred_element_type=jnp.float32)
    scores = total(part_scores, "mp")
    logp = scores - jnp.log(jnp.sum(jnp.exp(scores), axis=1, keepdims=True))
    prob = jnp.exp(logp)
    probs = target_probs.astype(jnp.float32)
    target = probs / jnp.sum(probs, axis=1, keepdims=True)
    kl_node = jnp.sum(target * (jnp.log(target) - logp), axis=1)
    live_count = lax.dynamic_index_in_dim(counts, group, 0, keepdims=False)
    live = jnp.arange(node_rows, dtype=jnp.int32) < live_count
    weight = jnp.where(live, 1 + accepted, 0).astype(jnp.float32)
    num, den = total(jnp.stack([jnp.sum(weight * kl_node), jnp.sum(weight)]), "dp")
    grad_scores = weight[:, None] * (prob - target)
    dnormed = jnp.einsum("nk,nkd->nd", grad_scores, cand_rows, preferred_element_type=jnp.float32)
    inner = total(jnp.sum(dnormed * gain_f * hidden, axis=1), "mp")
    dhidden = (
        recip[:, None] * gain_f * dnormed - hidden * (recip**3 * inner / full_width)[:, None]
    ).astype(jnp.bfloat16)
    grad_part = (
        lax.dot_general(
            whole, dhidden, (((0,), (0,)), ((), ())), preferred_element_type=jnp.float32
        )
        * scale_in
    )
    shares = lax.all_to_all(grad_part.reshape(groups, -1, width_part), "dp", 0, 0, tiled=True)
    grad = every(jnp.sum(shares, axis=0), "dp").reshape(full_width, width_part)
    energy = total(jnp.sum(grad * grad), "mp")
    factor = lax.rsqrt(energy / (full_width * full_width) + 1e-06)
    new_proj = (proj.astype(jnp.float32) - 0.5 * grad * factor).astype(jnp.bfloat16)
    return (new_proj, num / den)


def solution(mesh):
    nd = mesh.shape["dp"]
    nz = mesh.shape["mp"]

    def per_device(*args):
        out, loss, flag = fast_step(nd, nz, *args)
        return lax.cond(
            flag[0, 0] > 0.0,
            lambda: wide_step(*args),
            lambda: (out, loss[0, 0]),
        )

    placed = (
        P("dp", "mp"),
        P("dp"),
        P(),
        P("dp"),
        P("dp", None),
        P("dp", None),
        P("mp"),
        P("dp", "mp"),
        P(None, "mp"),
    )
    return jax.shard_map(
        per_device, mesh=mesh, in_specs=placed, out_specs=(P(None, "mp"), P()), check_vma=False
    )
```

```python
import functools
import jax
import jax.numpy as jnp
from jax import lax
from jax.experimental import pallas as pl
from jax.experimental.pallas import tpu as pltpu
from jax.sharding import PartitionSpec as P

MESH = pl.DeviceIdType.MESH
F32 = jnp.float32
BF16 = jnp.bfloat16
I32 = jnp.int32

GROUP = 4
MIXFIRST = 1
CH = 1
CAP = 352
CAPL = 384
HALF = 224


def dot(a, b):
    return jnp.dot(a, b, preferred_element_type=F32)


def dot_nt(a, b):
    return lax.dot_general(a, b, (((1,), (1,)), ((), ())), preferred_element_type=F32)


def one_hot(hit):
    return jnp.where(hit, 1.0, 0.0).astype(BF16)


def iota(shape, axis):
    return lax.broadcasted_iota(I32, shape, axis)


def step_kernel(
    nd, nz, full_rows,
    counts, ids, odds, parent, accepted, gain2, feats_in, embed_in, proj_in,
    out, loss_out, flag_out,
    feats, embed, proj, in_s, emb, perm, meta, mixat, metap, metar, mixp, mixr, live, metat,
    lists, sendid, idr, rows_out, rows_in, whole, whole_t, hidden, ng,
    pick_t, ksel_t, asked, zq, zqr, zs, zsr, dh,
    pair_out, pair_in, gown, rs_out, rs_in, gfull, sb_out, sb, ez_out, ez, dt_out, dt,
    emb_s, emb_r, meta_s, meta_r, mix_s, mix_r, id_s, id_r, row_s, row_r,
    zr_s, zr_r, zl_s, zl_r, zx_s, zx_r, zq_s, zq_r, pair_s, pair_r,
    rs_s, rs_r, ag_s, ag_r, fw_s, fw_r, sb_s, sb_r, ez_s, ez_r, dt_s, dt_r,
):
    me = lax.axis_index("dp")
    z = lax.axis_index("mp")
    nodes = feats.shape[0]
    width = feats.shape[1]
    slots = live.shape[1]
    share = nodes // nd
    core = lax.rem(me, 2)
    chip = lax.div(me, 2)
    chips = nd // 2
    sibling = me + 1 - 2 * core
    vocab = embed.shape[0]

    sent = []

    fetch = [
        pltpu.make_async_copy(src, dst, in_s.at[i])
        for i, (src, dst) in enumerate(((feats_in, feats), (embed_in, embed), (proj_in, proj)))
    ]
    for f in fetch:
        f.start()

    def copy(src, dst, ss, rs, d, zz):
        return pltpu.make_async_remote_copy(
            src_ref=src, dst_ref=dst, send_sem=ss, recv_sem=rs,
            device_id=(d, zz), device_id_type=MESH,
        )

    def nxt(i):
        return lax.rem(me + i, nd)

    def prv(i):
        return lax.rem(me - i + nd, nd)

    def loop(lo, hi, body):
        def wrapped(i, carry):
            body(i)
            return carry
        lax.fori_loop(lo, hi, wrapped, 0)

    side = int(chips ** 0.5)
    chip_x = lax.rem(chip, side)
    chip_y = lax.div(chip, side)

    def offset(i):
        dx = lax.rem(i, side)
        dy = lax.rem(lax.div(i, side) + i, side)
        return dx + core * (dy - dx), dy + core * (dx - dy)

    def to_chip(i):
        dx, dy = offset(i)
        return lax.rem(chip_y + dy, side) * side + lax.rem(chip_x + dx, side)

    def from_chip(i, sibling_order=False):
        dx, dy = offset(i)
        if sibling_order:
            dx, dy = dy, dx
        return lax.rem(chip_y - dy + side, side) * side + lax.rem(chip_x - dx + side, side)

    others = chips - 1

    def round_got(dst, rs):
        copy(dst, dst, rs, rs, sibling, z).wait_recv()

    def round_sent(src, ss):
        copy(src, src, ss, ss, sibling, z).wait_send()

    def each_device(act):
        act(sibling)

        def both(i):
            act(to_chip(i) * 2 + core)
            act(to_chip(i) * 2 + 1 - core)

        loop(1, chips, both)

    def z_round(src, dst, ss, rs):
        def one(i):
            copy(src, dst.at[z], ss, rs, me, lax.rem(z + i, nz)).start()

        loop(1, nz, one)
        sent.append(lambda: round_sent(dst.at[pl.ds(0, nz - 1)], ss))

    def z_got(dst, rs):
        round_got(dst.at[pl.ds(0, nz - 1)], rs)

    def dp_round(src, dst, ss, rs):
        each_device(lambda d: copy(src.at[d], dst.at[me], ss.at[0], rs.at[0], d, z).start())
        sent.append(lambda: round_sent(src.at[pl.ds(0, nd - 1)], ss.at[0]))

    def dp_got(dst, rs):
        round_got(dst.at[pl.ds(0, nd - 1)], rs.at[0])

    barrier = pltpu.get_barrier_semaphore()
    loop(1, nd, lambda i: pl.semaphore_signal(barrier, inc=1, device_id=(nxt(i), z), device_id_type=MESH))
    loop(1, nz, lambda i: pl.semaphore_signal(barrier, inc=1, device_id=(me, lax.rem(z + i, nz)), device_id_type=MESH))

    pair_rows = share // 2
    node_lane = iota((1, nodes), 1)
    src_lane = iota((1, slots), 1)
    lane_h = lax.div(src_lane, pair_rows)
    lane_j = 2 * (src_lane - lane_h * pair_rows)

    def deal(h, state):
        off, mine, into0, into1 = state
        count = counts[h]
        first = (me - off) & (nd - 1)
        base = (off + first) // nd
        row0 = jnp.where(lane_j * nd + first < count, base + lane_j, -1)
        row1 = jnp.where((lane_j + 1) * nd + first < count, base + lane_j + 1, -1)
        here = lane_h == h
        return (
            off + count, jnp.where(h == me, off, mine),
            jnp.where(here, row0, into0), jnp.where(here, row1, into1),
        )

    none = jnp.full((1, slots), -1, I32)
    _, mine, into0, into1 = lax.fori_loop(0, nd, deal, (jnp.int32(0), jnp.int32(0), none, none))
    place_j = lax.div(node_lane, nd)
    dealt = (
        ((node_lane + mine) & (nd - 1)) * share
        + (place_j & 1) * pair_rows + lax.div(place_j, 2)
    )
    gain = jnp.concatenate([gain2[0:1, :], gain2[1:2, :]], axis=1).astype(F32)

    def in_row(ref):
        return jnp.concatenate([ref[r:r + 1, :] for r in range(ref.shape[0])], axis=1)

    idf = ids[...].astype(F32)
    own_f = jnp.floor((idf + 0.5) * (1.0 / float(vocab)))
    at_f = idf - own_f * float(vocab)
    hi_f = jnp.floor(at_f * (1.0 / 256.0))
    par = in_row(parent)
    extra = jnp.concatenate(
        [
            in_row(accepted).astype(F32),
            (par // 32).astype(F32),
            (par % 32).astype(F32),
            jnp.zeros((5, nodes), F32),
        ],
        axis=0,
    )
    table = jnp.concatenate(
        [own_f, hi_f + 1.0, at_f - 256.0 * hi_f, odds[...].astype(F32), extra, jnp.zeros((88, nodes), F32)],
        axis=0,
    )
    meta[...] = table.T.astype(BF16)

    step = 128

    def perm_block(b):
        rows = pl.ds(b * step, step)
        e = one_hot(iota((step, nodes), 0) + b * step == dealt)
        perm[rows, :] = e
        m = dot(e, meta[...])
        mixat[rows, :] = m
        m = m.astype(BF16).reshape(step // share, 2, pair_rows, 128)
        metap[pl.ds(b * (step // share), step // share)] = jnp.concatenate(
            [m[:, 0, :, 0:64], m[:, 1, :, 0:64]], axis=-1
        )

    loop(0, nodes // step, perm_block)

    fetch[1].wait()
    block = emb.shape[1]
    even = vocab // 32 * 32
    emb[core, 0:even, :] = embed[0:even, :]
    emb[core, even:block, :] = jnp.concatenate(
        [embed[even:vocab, :].astype(F32), jnp.zeros((block - vocab, width), F32)], axis=0
    ).astype(BF16)
    pl.semaphore_wait(barrier, nd - 1 + nz - 1)

    def emb_copy(c):
        return copy(emb.at[c], emb.at[c], emb_s.at[c], emb_r.at[c], sibling, z)

    emb_copy(core).start()
    sent.append(lambda: emb_copy(core).wait_send())
    dp_round(metap, metar, meta_s, meta_r)
    metar[me] = metap[me]

    def mixp_block(b):
        rows = pl.ds(b * step, step)
        at = mixat[rows, 33:34] * 32.0 + mixat[rows, 34:35]
        p = one_hot(iota((step, nodes), 1) == at.astype(I32))
        mixp[pl.ds(b * (step // share), step // share)] = (
            dot(perm[rows, :] + p, feats[...])
            .astype(BF16)
            .reshape(step // share, share, width)
        )

    fetch[0].wait()
    loop(0, nodes // step, mixp_block)
    if MIXFIRST:
        dp_round(mixp, mixr, mix_s, mix_r)
    mixr[me] = mixp[me]

    def live_block(b):
        at = iota((step, slots), 0) + b * step
        live[0, pl.ds(b * step, step), :] = one_hot(at == into0)
        live[1, pl.ds(b * step, step), :] = one_hot(at == into1)

    loop(0, slots // step, live_block)

    dp_got(metar, meta_r)
    for b in range(slots // step):
        rows = slice(b * step, (b + 1) * step)
        got = metar[...].reshape(slots, metar.shape[2])
        part = dot(live[0, rows, :], got)[:, 0:64] + dot(live[1, rows, :], got)[:, 64:128]
        metat[:, rows] = part.T

    owner = metat[0:8, :].astype(I32)
    upper = one_hot(iota((slots, slots), 0) < iota((slots, slots), 1))
    own_iota = iota((nd, slots), 0)
    member = jnp.concatenate(
        [jnp.where(own_iota == owner[k:k + 1, :], 1.0, 0.0) for k in range(8)], axis=0
    )
    before = dot(member.astype(BF16), upper)
    carry = jnp.zeros((nd, 1), F32)
    found = jnp.zeros((chips * 8, CAPL), F32)
    asks = jnp.zeros((chips, 1), F32)
    at_chip = owner // 2
    odd_core = owner - 2 * at_chip
    chip_iota = iota((chips, slots), 0)
    node_row = iota((1, slots), 1)
    for k in range(8):
        mk = member[k * nd:(k + 1) * nd, :]
        rank = jnp.sum(mk * (before[k * nd:(k + 1) * nd, :] + carry), axis=0, keepdims=True)
        carry = carry + jnp.sum(mk, axis=1, keepdims=True)
        odd_k = odd_core[k:k + 1, :].astype(F32)
        place = rank + odd_k * (float(CAP - 1) - 2.0 * rank)
        asks = asks + jnp.sum(jnp.where(chip_iota == at_chip[k:k + 1, :], 1.0, 0.0), axis=1, keepdims=True)
        fields = jnp.concatenate(
            [
                metat[8 + k:9 + k, :] + float(block // 256) * odd_k,
                metat[16 + k:17 + k, :],
                (node_row // 2).astype(F32),
                ((node_row % 2) * 8 + (k + 1)).astype(F32),
                jnp.zeros((4, slots), F32),
            ],
            axis=0,
        )
        here = iota((chips, 8, slots), 0) == at_chip[k:k + 1, :][None]
        f = jnp.where(here, fields[None], 0.0).reshape(chips * 8, slots).astype(BF16)
        at = one_hot(iota((CAPL, slots), 0) == place.astype(I32))
        found = found + dot_nt(f, at)
    found = found.reshape(chips, 8, CAPL)
    lists[...] = found
    tiles = CAPL // 128
    sendid[...] = jnp.concatenate(
        [found[:, f:f + 1, t * 128:(t + 1) * 128] for f in range(2) for t in range(tiles)]
        + [jnp.zeros((chips, 8 - 2 * tiles, 128), F32)],
        axis=1,
    )
    over = jnp.maximum(
        jnp.max(jnp.where(carry > float(HALF), 1.0, 0.0), axis=0, keepdims=True),
        jnp.max(jnp.where(asks > float(CAP), 1.0, 0.0), axis=0, keepdims=True),
    )

    def ask(i):
        p = to_chip(i)
        copy(sendid.at[p], idr.at[chip], id_s.at[0], id_r.at[chip], p * 2 + core, z).start()

    loop(1, chips, ask)
    sent.append(lambda: round_sent(sendid.at[pl.ds(0, others)], id_s.at[0]))
    idr[chip] = sendid[chip]
    if not MIXFIRST:
        dp_round(mixp, mixr, mix_s, mix_r)

    def owner_at(j, q):
        return from_chip(j * GROUP + q + 1)

    groups = chips // GROUP

    def pick_group(j):
        for q in range(GROUP):
            a = lists[owner_at(j, q), 2:3, :]
            b = lists[owner_at(j, q), 3:4, :]
            odd = jnp.where(b - 1.0 >= 8.0, 1.0, 0.0)
            node = jnp.where(b > 0.0, 2.0 * a + odd, -1.0).astype(I32)
            k = jnp.where(b > 0.0, b - 1.0 - 8.0 * odd, -1.0).astype(I32)
            pick_t[j, :, q * CAPL:(q + 1) * CAPL] = one_hot(iota((slots, CAPL), 0) == node)
            ksel_t[j, :, q * CAPL:(q + 1) * CAPL] = jnp.where(iota((8, CAPL), 0) == k, 1.0, 0.0)

    used = pl.ds(0, CAP)

    def ask_group(j):
        got = lax.dot_general(pick_t[j], ng[...], (((0,), (0,)), ((), ())), preferred_element_type=F32)
        asked[j] = got.astype(BF16)

    def score(j, arrivals):
        round_got(rows_in.at[pl.ds(j * GROUP, arrivals), used], row_r.at[j])
        got = rows_in[j * GROUP:(j + 1) * GROUP].reshape(GROUP * CAPL, width).astype(F32)
        s = jnp.sum(got * asked[j].astype(F32), axis=1, keepdims=True)
        s = jnp.broadcast_to(s, (GROUP * CAPL, 128)).T[0:8, :]
        zs[j] = s[0:1, :]
        z_round(zs.at[j], zsr.at[j], zx_s.at[j], zx_r.at[j])
        zsr[j, z] = zs[j]

    def node_scores(j):
        z_got(zsr.at[j], zx_r.at[j])
        s = zsr[j, 0]
        for i in range(1, nz):
            s = s + zsr[j, i]
        s_hi = s.astype(BF16).astype(F32)
        by_k = jnp.concatenate([s_hi * ksel_t[j], (s - s_hi) * ksel_t[j]], axis=0).astype(BF16)
        return dot_nt(by_k, pick_t[j])

    def mix_in():
        dp_got(mixr, mix_r)
        for b in range(slots // step):
            rows = slice(b * step, (b + 1) * step)
            part = dot(live[0, rows, :], mixr[:, 0:pair_rows, :].reshape(slots, width)) + dot(
                live[1, rows, :], mixr[:, pair_rows:share, :].reshape(slots, width)
            )
            whole[z, rows, :] = part.astype(BF16)

    zright = lax.rem(z + 1, nz)
    zleft = lax.rem(z + nz - 1, nz)

    def ring_part(s, first):
        if s + 1 < nz // 2:
            return pl.ds(0, slots)
        return pl.ds(first * (slots // 2), slots // 2)

    def ring_copy(s, b, side_r):
        rows = ring_part(s, 0 if side_r else 1)
        ss, rs = (zr_s, zr_r) if side_r else (zl_s, zl_r)
        return copy(
            whole.at[b, rows], whole.at[b, rows], ss.at[s], rs.at[s], me, zright if side_r else zleft
        )

    def ring_right(s):
        return ring_copy(s, lax.rem(z - s + nz, nz), True)

    def ring_left(s):
        return ring_copy(s, lax.rem(z + s, nz), False)

    def got_right(s):
        b = lax.rem(z - s - 1 + nz, nz)
        ring_copy(s, b, True).wait_recv()
        return b

    def got_left(s):
        b = lax.rem(z + s + 1, nz)
        ring_copy(s, b, False).wait_recv()
        return b

    hops = nz // 2
    for j in range(groups):
        pick_group(j)
    scale = 1.0 / (float(full_rows) ** 0.5)

    def use_block(b, first=False):
        blk = whole[b]
        whole_t[b] = blk.T
        h = dot(blk, proj[pl.ds(pl.multiple_of(b * width, width), width), :])
        if first:
            hidden[...] = h
        else:
            hidden[...] += h

    chunk = 256

    low = CAP - HALF

    def serve(h):
        cols = idr[h].T
        hi = jnp.concatenate([cols[:, t:t + 1] for t in range(tiles)], axis=0)[:CAP]
        lo = jnp.concatenate([cols[:, tiles + t:tiles + t + 1] for t in range(tiles)], axis=0)[:CAP]
        hi = jnp.broadcast_to(hi, (CAP, chunk)).astype(BF16)
        lo = one_hot(iota((CAP, chunk), 1) == lo.astype(I32))
        halves = []
        for c in range(2):
            first = c * low
            parts = [
                jnp.where(
                    hi[first:first + HALF, :] == jnp.bfloat16(c * (block // chunk) + i + 1),
                    lo[first:first + HALF, :],
                    jnp.bfloat16(0),
                )
                for i in range(block // chunk)
            ]
            halves.append(dot(jnp.concatenate(parts, axis=1), emb[c]))
        front, rear = halves
        rows_out[h, 0:low, :] = front[0:low, :].astype(BF16)
        rows_out[h, low:HALF, :] = (front[low:, :] + rear[:HALF - low, :]).astype(BF16)
        rows_out[h, HALF:CAP, :] = rear[HALF - low:, :].astype(BF16)

    def row_send(i):
        p = to_chip(i)
        copy(
            rows_out.at[p, used], rows_in.at[i - 1, used],
            row_s.at[0], row_r.at[lax.div(i - 1, GROUP)], p * 2 + core, z,
        ).start()

    def serve_far(i):
        h = to_chip(i)
        round_got(idr.at[h], id_r.at[h])
        serve(h)
        row_send(i)

    emb_copy(1 - core).wait_recv()
    fetch[2].wait()
    done = 1
    loop(done, 4, serve_far)
    done = 4
    mix_in()
    ring_right(0).start()
    ring_left(0).start()
    use_block(z, True)
    for s in range(hops):
        upto = min(done + 5, chips)
        loop(done, upto, serve_far)
        done = upto
        if s + 2 == hops:
            loop(done, chips, serve_far)
            done = chips
            serve(chip)
        b = got_right(s)
        if s + 1 < hops:
            ring_right(s + 1).start()
            use_block(b)
        b = got_left(s)
        if s + 1 < hops:
            ring_left(s + 1).start()
        use_block(b)
    rows_in[chips - 1, 0:CAP, :] = rows_out[chip, 0:CAP, :]
    rows_in[:, CAP:CAPL, :] = jnp.zeros((chips, CAPL - CAP, width), BF16)
    sent.append(lambda: round_sent(rows_out.at[pl.ds(0, others), used], row_s.at[0]))
    for s in range(hops):
        sent.append(functools.partial(lambda s: ring_right(s).wait_send(), s))
        sent.append(functools.partial(lambda s: ring_left(s).wait_send(), s))

    hid = hidden[...] * scale
    hidden[...] = hid
    square = jnp.sum(hid * hid, axis=1, keepdims=True)
    ng[...] = (hid * gain).astype(BF16)
    square = jnp.broadcast_to(square, (slots, 128)).T[0:1, :]
    folds = slots // 128
    zq[...] = jnp.concatenate(
        [square[:, f * 128:(f + 1) * 128] for f in range(folds)] + [jnp.zeros((8 - folds, 128), F32)], axis=0
    )
    z_round(zq, zqr, zq_s.at[0], zq_r.at[0])
    zqr[z] = zq[...]
    for j in range(groups):
        ask_group(j)
    for j in range(groups):
        score(j, GROUP - (j + 1) // groups)

    z_got(zqr, zq_r.at[0])
    tot = zqr[0]
    for i in range(1, nz):
        tot = tot + zqr[i]
    squares = jnp.concatenate([tot[f:f + 1, :] for f in range(folds)], axis=1)
    recip = lax.rsqrt(squares / float(full_rows) + 1e-05)
    got = node_scores(0)
    for j in range(1, groups):
        got = got + node_scores(j)
    raw = got[0:8, :] + got[8:16, :]
    scores = raw * recip
    logp = scores - jnp.log(jnp.sum(jnp.exp(scores), axis=0, keepdims=True))
    prob = jnp.exp(logp)
    probs = metat[24:32, :]
    target = probs / jnp.sum(probs, axis=0, keepdims=True)
    kl = jnp.sum(target * (jnp.log(target) - logp), axis=0, keepdims=True)
    weight = 1.0 + metat[32:33, :]
    num = jnp.sum(weight * kl, axis=1, keepdims=True)
    den = jnp.sum(weight, axis=1, keepdims=True)
    gs = weight * (prob - target)
    inner = jnp.sum(gs * raw, axis=0, keepdims=True)
    back = recip * recip * recip * inner * (1.0 / float(full_rows))
    gs_hi = gs.astype(BF16).astype(F32)
    gs16 = jnp.concatenate([gs_hi, gs - gs_hi], axis=0).astype(BF16)
    coef = jnp.concatenate([recip, back, jnp.zeros((6, slots), F32)], axis=0).T

    for j in range(groups):
        g16 = dot(gs16, pick_t[j])
        g = jnp.sum((g16[0:8, :] + g16[8:16, :]) * ksel_t[j], axis=0, keepdims=True)
        scaled = pick_t[j] * g.astype(BF16)
        part = dot(scaled, rows_in[j * GROUP:(j + 1) * GROUP].reshape(GROUP * CAPL, width))
        dnormed = part if j == 0 else dnormed + part
    dh[...] = (coef[:, 0:1] * gain * dnormed - hidden[...] * coef[:, 1:2]).astype(BF16)

    quarter = nz // 2

    def pair(q):
        return copy(pair_out.at[q], pair_in.at[q], pair_s.at[q], pair_r.at[q], sibling, z)

    def turn(q):
        return lax.rem(chip_y + q, quarter)

    for q in range(quarter):
        pair_out[q] = (dot(whole_t[(1 - core) * quarter + turn(q)], dh[...]) * scale).astype(BF16)
        pair(q).start()
    for q in range(quarter):
        gown[q] = dot(whole_t[core * quarter + turn(q)], dh[...]) * scale
    per = chips // quarter

    part_rows = width // per // CH

    def rs_send(c, i, p):
        copy(rs_out.at[c, p], rs_in.at[c, i], rs_s.at[c], rs_r.at[c], p * 2 + core, z).start()

    batches = 3
    batch = others // batches

    def ag_send(c, i):
        p = to_chip(i)
        copy(
            gfull.at[core, c, 0], gfull.at[core, c, i],
            ag_s.at[c], ag_r.at[c * batches + lax.div(i - 1, batch)], p * 2 + core, z,
        ).start()

    def forward(c, b, side_core):
        at = pl.ds(0, 1) if b == batches else pl.ds(1 + b * batch, batch)
        ref = gfull.at[side_core, c, at]
        n = c * (batches + 1) + b
        return copy(ref, ref, fw_s.at[n], fw_r.at[n], sibling, z)

    for q in range(quarter):
        pair(q).wait_recv()
        both = (gown[q] + pair_in[q].astype(F32)).astype(BF16).reshape(per, CH, part_rows, width)
        first = turn(q) * per
        for c in range(CH):
            rs_out[c, pl.ds(first, per)] = both[:, c]
        for i in range(1 if q == 0 else 0, per):
            rs_send(0, q * per + i, first + lax.rem(chip_x + i, per))
    for c in range(1, CH):
        loop(1, chips, lambda i: rs_send(c, i, to_chip(i)))
    for q in range(quarter):
        sent.append(functools.partial(lambda q: pair(q).wait_send(), q))
    for c in range(CH):
        sent.append(functools.partial(lambda c: round_sent(rs_out.at[c, pl.ds(0, others)], rs_s.at[c]), c))
        sent.append(functools.partial(lambda c: round_sent(gfull.at[core, c, pl.ds(0, others)], ag_s.at[c]), c))
        for b in range(batches + 1):
            sent.append(functools.partial(lambda c, b: forward(c, b, core).wait_send(), c, b))
    energy = jnp.zeros((1, 1), F32)
    for c in range(CH):
        rs_in[c, 0] = rs_out[c, chip]
        round_got(rs_in.at[c, pl.ds(1, others)], rs_r.at[c])
        shard = rs_in[c, 0].astype(F32)
        for p in range(1, chips):
            shard = shard + rs_in[c, p].astype(F32)
        gfull[core, c, 0] = shard.astype(BF16)
        energy = energy + jnp.sum(jnp.sum(shard * shard, axis=1, keepdims=True), axis=0, keepdims=True)
        loop(1, chips, lambda i: ag_send(c, i))
        forward(c, batches, core).start()
    row = iota((8, 128), 0)
    tile = jnp.where(row == 0, energy, jnp.where(row == 1, num, jnp.where(row == 2, den, over)))

    sb_out[...] = tile
    both_cores = copy(sb_out, sb, sb_s.at[0], sb_r.at[0], sibling, z)
    both_cores.start()

    sent.append(both_cores.wait_send)

    def ag_pass(c, b):
        round_got(gfull.at[core, c, pl.ds(1 + b * batch, batch)], ag_r.at[c * batches + b])
        forward(c, b, core).start()

    both_cores.wait_recv()
    tile = tile + sb[...]
    ez_out[...] = tile
    z_round(ez_out, ez, ez_s.at[0], ez_r.at[0])
    ez[z] = tile
    z_got(ez, ez_r.at[0])
    etot = ez[0]
    for i in range(1, nz):
        etot = etot + ez[i]
    tile = jnp.where(row == 0, etot, tile)
    dt_out[...] = tile

    def tell(i):
        copy(dt_out, dt.at[i], dt_s.at[0], dt_r.at[0], to_chip(i) * 2 + core, z).start()

    loop(1, chips, tell)
    sent.append(lambda: round_sent(dt.at[pl.ds(1, others)], dt_s.at[0]))
    dt[0] = tile
    for c in range(CH):
        for b in range(batches):
            ag_pass(c, b)
    round_got(dt.at[pl.ds(1, others)], dt_r.at[0])
    total = dt[0]
    for i in range(1, chips):
        total = total + dt[i]
    entries = float(full_rows) * float(full_rows)
    factor = 0.5 * lax.rsqrt(total[0:1, 0:1] / entries + 1e-06)
    loss_out[...] = total[1:2, 0:1] / total[2:3, 0:1]
    flag_out[...] = total[3:4, 0:1]

    blk_rows = width // per

    def finish(h, c, i, p):
        at = (h * chips + p) * blk_rows + c * part_rows
        r = pl.ds(pl.multiple_of(at, part_rows), part_rows)
        out[r, :] = (proj[r, :].astype(F32) - gfull[h, c, i].astype(F32) * factor).astype(BF16)

    for c in range(CH):
        loop(0, chips, lambda i: finish(core, c, i, from_chip(i)))
    for c in range(CH):
        for b in range(batches, -1, -1):
            forward(c, b, 1 - core).wait_recv()
        loop(0, chips, lambda i: finish(1 - core, c, i, from_chip(i, True)))

    for wait in sent:
        wait()


def fast_step(nd, nz, feats, parent, counts, accepted, cand_ids, target_probs, gain, embed, proj):
    nodes, width = feats.shape
    full_rows = proj.shape[0]
    share = nodes // nd
    vocab = embed.shape[0]
    slots = nodes // 2
    chips = nd // 2
    quarter = nz // 2
    per = chips // quarter
    vm = pltpu.VMEM
    scratch = [
        vm(feats.shape, BF16),
        vm(embed.shape, BF16),
        vm(proj.shape, BF16),
        pltpu.SemaphoreType.DMA((3,)),
        vm((2, -(-vocab // 256) * 256, width), BF16),
        vm((nodes, nodes), BF16),
        vm((nodes, 128), BF16),
        vm((nodes, 128), F32),
        vm((nd, share // 2, 128), BF16),
        vm((nd, share // 2, 128), BF16),
        vm((nd, share, width), BF16),
        vm((nd, share, width), BF16),
        vm((2, slots, slots), BF16),
        vm((64, slots), F32),
        vm((chips, 8, CAPL), F32),
        vm((chips, 8, 128), F32),
        vm((chips, 8, 128), F32),
        vm((chips, CAPL, width), BF16),
        vm((chips, CAPL, width), BF16),
        vm((nz, slots, width), BF16),
        vm((nz, width, slots), BF16),
        vm((slots, width), F32),
        vm((slots, width), BF16),
        vm((chips // GROUP, slots, GROUP * CAPL), BF16),
        vm((chips // GROUP, 8, GROUP * CAPL), F32),
        vm((chips // GROUP, GROUP * CAPL, width), BF16),
        vm((8, 128), F32),
        vm((nz, 8, 128), F32),
        vm((chips // GROUP, 1, GROUP * CAPL), F32),
        vm((chips // GROUP, nz, 1, GROUP * CAPL), F32),
        vm((slots, width), BF16),
        vm((quarter, width, width), BF16),
        vm((quarter, width, width), BF16),
        vm((quarter, width, width), F32),
        vm((CH, chips, width // per // CH, width), BF16),
        vm((CH, chips, width // per // CH, width), BF16),
        vm((2, CH, chips, width // per // CH, width), BF16),
        vm((8, 128), F32),
        vm((8, 128), F32),
        vm((8, 128), F32),
        vm((nz, 8, 128), F32),
        vm((8, 128), F32),
        vm((chips, 8, 128), F32),
    ]
    dma = pltpu.SemaphoreType.DMA
    for count in (
        2, 2, 1, 1, 1, 1, 1, chips, 1, chips // GROUP,
        nz, nz, nz, nz, chips // GROUP, chips // GROUP, 1, 1, quarter, quarter,
        CH, CH, CH, 3 * CH, 4 * CH, 4 * CH, 1, 1, 1, 1, 1, 1,
    ):
        scratch.append(dma((count,)))
    in_vmem = pl.BlockSpec(memory_space=pltpu.VMEM)
    return pl.pallas_call(
        functools.partial(step_kernel, nd, nz, full_rows),
        out_shape=(
            jax.ShapeDtypeStruct(proj.shape, BF16),
            jax.ShapeDtypeStruct((1, 1), F32),
            jax.ShapeDtypeStruct((1, 1), F32),
        ),
        in_specs=[pl.BlockSpec(memory_space=pltpu.SMEM)] + [in_vmem] * 5 + [pl.BlockSpec(memory_space=pl.ANY)] * 3,
        out_specs=(in_vmem, in_vmem, in_vmem),
        scratch_shapes=scratch,
        compiler_params=pltpu.CompilerParams(
            collective_id=0, has_side_effects=True, vmem_limit_bytes=60 * 1024 * 1024
        ),
        name="step",
    )(
        counts, cand_ids.T, target_probs.T, parent.reshape(8, nodes // 8), accepted.reshape(8, nodes // 8),
        gain.reshape(2, width // 2), feats, embed, proj,
    )


def every(x, axis):
    n = lax.axis_size(axis)
    return lax.all_to_all(jnp.broadcast_to(x[None], (n,) + x.shape), axis, 0, 0, tiled=True)


def total(x, axis):
    return jnp.sum(every(jnp.atleast_1d(x), axis), axis=0).reshape(x.shape)


def wide_step(feats, parent, counts, accepted, cand_ids, target_probs, gain, embed, proj):
    node_rows, width_part = feats.shape
    full_width = proj.shape[0]
    group = lax.axis_index("dp")
    groups = lax.axis_size("dp")
    shard_rows = embed.shape[0]
    cand_count = cand_ids.shape[1]
    scale_in = 1.0 / jnp.sqrt(jnp.float32(full_width))
    gain_f = gain.astype(jnp.float32)
    flat_ids = cand_ids.reshape(-1)
    requests = flat_ids.shape[0]
    capacity = 3 * requests // (2 * groups)
    owners = flat_ids // shard_rows
    local_ids = flat_ids - owners * shard_rows
    member = owners[:, None] == jnp.arange(groups, dtype=jnp.int32)[None, :]
    per_owner = jnp.sum(member.astype(jnp.int32), axis=0)
    starts = jnp.cumsum(per_owner) - per_owner
    my_start = jnp.sum(jnp.where(member, starts[None, :], 0), axis=1)
    order = jnp.argsort(owners, stable=True)
    ranks = jnp.arange(requests, dtype=jnp.int32) - my_start[order]
    slots = owners[order] * capacity + ranks
    outgoing = jnp.zeros((groups * capacity,), jnp.int32).at[slots].set(local_ids[order])
    placed = jnp.zeros((requests,), jnp.int32).at[order].set(slots)
    mixed = (feats.astype(jnp.float32) + feats[parent].astype(jnp.float32)).astype(jnp.bfloat16)
    piece = every(mixed, "mp").transpose(1, 0, 2).reshape(node_rows, full_width)
    partial_value = jnp.dot(piece, proj, preferred_element_type=jnp.float32)
    whole = piece
    partial_value, whole = (partial_value, whole)
    hidden = partial_value * scale_in
    squares = total(jnp.sum(hidden * hidden, axis=1), "mp")
    recip = lax.rsqrt(squares / full_width + 1e-05)
    normed = (hidden * recip[:, None] * gain_f).astype(jnp.bfloat16)
    found = embed[
        lax.all_to_all(
            outgoing.reshape(groups, capacity), "dp", split_axis=0, concat_axis=0, tiled=True
        )
    ]
    fetched = lax.all_to_all(found, "dp", split_axis=0, concat_axis=0, tiled=True)
    cand_rows = fetched.reshape(groups * capacity, width_part)[placed].reshape(
        node_rows, cand_count, width_part
    )
    part_scores = jnp.einsum("nkd,nd->nk", cand_rows, normed, preferred_element_type=jnp.float32)
    scores = total(part_scores, "mp")
    logp = scores - jnp.log(jnp.sum(jnp.exp(scores), axis=1, keepdims=True))
    prob = jnp.exp(logp)
    probs = target_probs.astype(jnp.float32)
    target = probs / jnp.sum(probs, axis=1, keepdims=True)
    kl_node = jnp.sum(target * (jnp.log(target) - logp), axis=1)
    live_count = lax.dynamic_index_in_dim(counts, group, 0, keepdims=False)
    live = jnp.arange(node_rows, dtype=jnp.int32) < live_count
    weight = jnp.where(live, 1 + accepted, 0).astype(jnp.float32)
    num, den = total(jnp.stack([jnp.sum(weight * kl_node), jnp.sum(weight)]), "dp")
    grad_scores = weight[:, None] * (prob - target)
    dnormed = jnp.einsum("nk,nkd->nd", grad_scores, cand_rows, preferred_element_type=jnp.float32)
    inner = total(jnp.sum(dnormed * gain_f * hidden, axis=1), "mp")
    dhidden = (
        recip[:, None] * gain_f * dnormed - hidden * (recip**3 * inner / full_width)[:, None]
    ).astype(jnp.bfloat16)
    grad_part = (
        lax.dot_general(
            whole, dhidden, (((0,), (0,)), ((), ())), preferred_element_type=jnp.float32
        )
        * scale_in
    )
    shares = lax.all_to_all(grad_part.reshape(groups, -1, width_part), "dp", 0, 0, tiled=True)
    grad = every(jnp.sum(shares, axis=0), "dp").reshape(full_width, width_part)
    energy = total(jnp.sum(grad * grad), "mp")
    factor = lax.rsqrt(energy / (full_width * full_width) + 1e-06)
    new_proj = (proj.astype(jnp.float32) - 0.5 * grad * factor).astype(jnp.bfloat16)
    return (new_proj, num / den)


def solution(mesh):
    nd = mesh.shape["dp"]
    nz = mesh.shape["mp"]

    def per_device(*args):
        out, loss, flag = fast_step(nd, nz, *args)
        return lax.cond(
            flag[0, 0] > 0.0,
            lambda: wide_step(*args),
            lambda: (out, loss[0, 0]),
        )

    placed = (
        P("dp", "mp"),
        P("dp"),
        P(),
        P("dp"),
        P("dp", None),
        P("dp", None),
        P("mp"),
        P("dp", "mp"),
        P(None, "mp"),
    )
    return jax.shard_map(
        per_device, mesh=mesh, in_specs=placed, out_specs=(P(None, "mp"), P()), check_vma=False
    )
```

```python
import functools
import jax
import jax.numpy as jnp
from jax import lax
from jax.experimental import pallas as pl
from jax.experimental.pallas import tpu as pltpu
from jax.sharding import PartitionSpec as P

MESH = pl.DeviceIdType.MESH
F32 = jnp.float32
BF16 = jnp.bfloat16
I32 = jnp.int32

GROUP = 2
WIDE = 4
UNROLL = 1
CH = 1
BATCHES = 5
RING_AT = 2
CAP = 352
CAPL = 384
HALF = 224


def dot(a, b):
    return jnp.dot(a, b, preferred_element_type=F32)


def dot_nt(a, b):
    return lax.dot_general(a, b, (((1,), (1,)), ((), ())), preferred_element_type=F32)


def one_hot(hit):
    return jnp.where(hit, 1.0, 0.0).astype(BF16)


def iota(shape, axis):
    return lax.broadcasted_iota(I32, shape, axis)


def step_kernel(
    nd, nz, full_rows,
    counts, ids, odds, parent, accepted, gain2, feats_in, embed_in, proj_in,
    out, loss_out, flag_out,
    feats, embed, proj, in_s, emb, perm, meta, mixat, metap, metar, mixp, mixr, live, metat,
    lists, sendid, idr, rows_out, rows_in, whole, whole_t, hidden, ng,
    pick_t, ksel_t, asked, zq, zqr, zs, zsr, dh,
    pair_out, pair_in, gown, rs_out, rs_in, gfull, sb_out, sb, ez_out, ez, dt_out, dt,
    emb_s, emb_r, meta_s, meta_r, mix_s, mix_r, id_s, id_r, row_s, row_r,
    zr_s, zr_r, zl_s, zl_r, zx_s, zx_r, zq_s, zq_r, pair_s, pair_r,
    rs_s, rs_r, ag_s, ag_r, fw_s, fw_r, sb_s, sb_r, ez_s, ez_r, dt_s, dt_r,
):
    me = lax.axis_index("dp")
    z = lax.axis_index("mp")
    nodes = feats.shape[0]
    width = feats.shape[1]
    slots = live.shape[1]
    share = nodes // nd
    core = lax.rem(me, 2)
    chip = lax.div(me, 2)
    chips = nd // 2
    sibling = me + 1 - 2 * core
    vocab = embed.shape[0]

    sent = []

    fetch = [
        pltpu.make_async_copy(src, dst, in_s.at[i])
        for i, (src, dst) in enumerate(((feats_in, feats), (embed_in, embed), (proj_in, proj)))
    ]
    for f in fetch:
        f.start()

    def starts(lo, hi, body):
        if UNROLL:
            for i in range(lo, hi):
                body(i)
        else:
            loop(lo, hi, body)

    def copy(src, dst, ss, rs, d, zz):
        return pltpu.make_async_remote_copy(
            src_ref=src, dst_ref=dst, send_sem=ss, recv_sem=rs,
            device_id=(d, zz), device_id_type=MESH,
        )

    def nxt(i):
        return lax.rem(me + i, nd)

    def prv(i):
        return lax.rem(me - i + nd, nd)

    def loop(lo, hi, body):
        def wrapped(i, carry):
            body(i)
            return carry
        lax.fori_loop(lo, hi, wrapped, 0)

    side = int(chips ** 0.5)
    chip_x = lax.rem(chip, side)
    chip_y = lax.div(chip, side)

    def offset(i):
        if isinstance(i, int):
            dx = i % side
            dy = (i // side + i) % side
        else:
            dx = lax.rem(i, side)
            dy = lax.rem(lax.div(i, side) + i, side)
        return dx + core * (dy - dx), dy + core * (dx - dy)

    def to_chip(i):
        dx, dy = offset(i)
        return lax.rem(chip_y + dy, side) * side + lax.rem(chip_x + dx, side)

    def from_chip(i, sibling_order=False):
        dx, dy = offset(i)
        if sibling_order:
            dx, dy = dy, dx
        return lax.rem(chip_y - dy + side, side) * side + lax.rem(chip_x - dx + side, side)

    others = chips - 1

    def round_got(dst, rs):
        copy(dst, dst, rs, rs, sibling, z).wait_recv()

    def round_sent(src, ss):
        copy(src, src, ss, ss, sibling, z).wait_send()

    def each_device(act):
        act(sibling)

        def both(i):
            act(to_chip(i) * 2 + core)
            act(to_chip(i) * 2 + 1 - core)

        starts(1, chips, both)

    def z_round(src, dst, ss, rs):
        def one(i):
            copy(src, dst.at[z], ss, rs, me, lax.rem(z + i, nz)).start()

        starts(1, nz, one)
        sent.append(lambda: round_sent(dst.at[pl.ds(0, nz - 1)], ss))

    def z_got(dst, rs):
        round_got(dst.at[pl.ds(0, nz - 1)], rs)

    def dp_round(src, dst, ss, rs):
        each_device(lambda d: copy(src.at[d], dst.at[me], ss.at[0], rs.at[0], d, z).start())
        sent.append(lambda: round_sent(src.at[pl.ds(0, nd - 1)], ss.at[0]))

    def dp_got(dst, rs):
        round_got(dst.at[pl.ds(0, nd - 1)], rs.at[0])

    barrier = pltpu.get_barrier_semaphore()
    starts(1, nd, lambda i: pl.semaphore_signal(barrier, inc=1, device_id=(nxt(i), z), device_id_type=MESH))
    starts(1, nz, lambda i: pl.semaphore_signal(barrier, inc=1, device_id=(me, lax.rem(z + i, nz)), device_id_type=MESH))

    pair_rows = share // 2
    node_lane = iota((1, nodes), 1)
    src_lane = iota((1, slots), 1)
    lane_h = lax.div(src_lane, pair_rows)
    lane_j = 2 * (src_lane - lane_h * pair_rows)

    def deal(h, state):
        off, mine, into0, into1 = state
        count = counts[h]
        first = (me - off) & (nd - 1)
        base = (off + first) // nd
        row0 = jnp.where(lane_j * nd + first < count, base + lane_j, -1)
        row1 = jnp.where((lane_j + 1) * nd + first < count, base + lane_j + 1, -1)
        here = lane_h == h
        return (
            off + count, jnp.where(h == me, off, mine),
            jnp.where(here, row0, into0), jnp.where(here, row1, into1),
        )

    none = jnp.full((1, slots), -1, I32)
    _, mine, into0, into1 = lax.fori_loop(0, nd, deal, (jnp.int32(0), jnp.int32(0), none, none))
    place_j = lax.div(node_lane, nd)
    dealt = (
        ((node_lane + mine) & (nd - 1)) * share
        + (place_j & 1) * pair_rows + lax.div(place_j, 2)
    )
    gain = jnp.concatenate([gain2[0:1, :], gain2[1:2, :]], axis=1).astype(F32)

    def in_row(ref):
        return jnp.concatenate([ref[r:r + 1, :] for r in range(ref.shape[0])], axis=1)

    idf = ids[...].astype(F32)
    own_f = jnp.floor((idf + 0.5) * (1.0 / float(vocab)))
    at_f = idf - own_f * float(vocab)
    hi_f = jnp.floor(at_f * (1.0 / 256.0))
    par = in_row(parent)
    extra = jnp.concatenate(
        [
            in_row(accepted).astype(F32),
            (par // 32).astype(F32),
            (par % 32).astype(F32),
            jnp.zeros((5, nodes), F32),
        ],
        axis=0,
    )
    table = jnp.concatenate(
        [own_f, hi_f + 1.0, at_f - 256.0 * hi_f, odds[...].astype(F32), extra, jnp.zeros((88, nodes), F32)],
        axis=0,
    )
    meta[...] = table.T.astype(BF16)

    step = 128

    def perm_block(b):
        rows = pl.ds(b * step, step)
        e = one_hot(iota((step, nodes), 0) + b * step == dealt)
        perm[rows, :] = e
        m = dot(e, meta[...])
        mixat[rows, :] = m
        m = m.astype(BF16).reshape(step // share, 2, pair_rows, 128)
        metap[pl.ds(b * (step // share), step // share)] = jnp.concatenate(
            [m[:, 0, :, 0:64], m[:, 1, :, 0:64]], axis=-1
        )

    starts(0, nodes // step, perm_block)

    fetch[1].wait()
    block = emb.shape[1]
    even = vocab // 32 * 32
    emb[core, 0:even, :] = embed[0:even, :]
    emb[core, even:block, :] = jnp.concatenate(
        [embed[even:vocab, :].astype(F32), jnp.zeros((block - vocab, width), F32)], axis=0
    ).astype(BF16)
    pl.semaphore_wait(barrier, nd - 1 + nz - 1)

    def emb_copy(c):
        return copy(emb.at[c], emb.at[c], emb_s.at[c], emb_r.at[c], sibling, z)

    emb_copy(core).start()
    sent.append(lambda: emb_copy(core).wait_send())
    dp_round(metap, metar, meta_s, meta_r)
    metar[me] = metap[me]

    def mixp_block(b):
        rows = pl.ds(b * step, step)
        at = mixat[rows, 33:34] * 32.0 + mixat[rows, 34:35]
        p = one_hot(iota((step, nodes), 1) == at.astype(I32))
        mixp[pl.ds(b * (step // share), step // share)] = (
            dot(perm[rows, :] + p, feats[...])
            .astype(BF16)
            .reshape(step // share, share, width)
        )

    fetch[0].wait()
    starts(0, nodes // step, mixp_block)
    dp_round(mixp, mixr, mix_s, mix_r)
    mixr[me] = mixp[me]

    def live_block(b):
        at = iota((step, slots), 0) + b * step
        live[0, pl.ds(b * step, step), :] = one_hot(at == into0)
        live[1, pl.ds(b * step, step), :] = one_hot(at == into1)

    starts(0, slots // step, live_block)

    dp_got(metar, meta_r)
    for b in range(slots // step):
        rows = slice(b * step, (b + 1) * step)
        got = metar[...].reshape(slots, metar.shape[2])
        part = dot(live[0, rows, :], got)[:, 0:64] + dot(live[1, rows, :], got)[:, 64:128]
        metat[:, rows] = part.T

    owner = metat[0:8, :].astype(I32)
    upper = one_hot(iota((slots, slots), 0) < iota((slots, slots), 1))
    own_iota = iota((nd, slots), 0)
    member = jnp.concatenate(
        [jnp.where(own_iota == owner[k:k + 1, :], 1.0, 0.0) for k in range(8)], axis=0
    )
    before = dot(member.astype(BF16), upper)
    carry = jnp.zeros((nd, 1), F32)
    found = jnp.zeros((chips * 8, CAPL), F32)
    asks = jnp.zeros((chips, 1), F32)
    at_chip = owner // 2
    odd_core = owner - 2 * at_chip
    chip_iota = iota((chips, slots), 0)
    node_row = iota((1, slots), 1)
    for k in range(8):
        mk = member[k * nd:(k + 1) * nd, :]
        rank = jnp.sum(mk * (before[k * nd:(k + 1) * nd, :] + carry), axis=0, keepdims=True)
        carry = carry + jnp.sum(mk, axis=1, keepdims=True)
        odd_k = odd_core[k:k + 1, :].astype(F32)
        place = rank + odd_k * (float(CAP - 1) - 2.0 * rank)
        asks = asks + jnp.sum(jnp.where(chip_iota == at_chip[k:k + 1, :], 1.0, 0.0), axis=1, keepdims=True)
        fields = jnp.concatenate(
            [
                metat[8 + k:9 + k, :] + float(block // 256) * odd_k,
                metat[16 + k:17 + k, :],
                (node_row // 2).astype(F32),
                ((node_row % 2) * 8 + (k + 1)).astype(F32),
                jnp.zeros((4, slots), F32),
            ],
            axis=0,
        )
        here = iota((chips, 8, slots), 0) == at_chip[k:k + 1, :][None]
        f = jnp.where(here, fields[None], 0.0).reshape(chips * 8, slots).astype(BF16)
        at = one_hot(iota((CAPL, slots), 0) == place.astype(I32))
        found = found + dot_nt(f, at)
    found = found.reshape(chips, 8, CAPL)
    lists[...] = found
    tiles = CAPL // 128
    sendid[...] = jnp.concatenate(
        [found[:, f:f + 1, t * 128:(t + 1) * 128] for f in range(2) for t in range(tiles)]
        + [jnp.zeros((chips, 8 - 2 * tiles, 128), F32)],
        axis=1,
    )
    over = jnp.maximum(
        jnp.max(jnp.where(carry > float(HALF), 1.0, 0.0), axis=0, keepdims=True),
        jnp.max(jnp.where(asks > float(CAP), 1.0, 0.0), axis=0, keepdims=True),
    )

    def ask(i):
        p = to_chip(i)
        copy(sendid.at[p], idr.at[chip], id_s.at[0], id_r.at[chip], p * 2 + core, z).start()

    starts(1, chips, ask)
    sent.append(lambda: round_sent(sendid.at[pl.ds(0, others)], id_s.at[0]))
    idr[chip] = sendid[chip]

    def owner_at(j, q):
        return from_chip(j * GROUP + q + 1)

    groups = chips // GROUP

    def lanes(j, lo, hi):
        first = j * GROUP % WIDE
        return slice((first + lo) * CAPL, (first + hi) * CAPL)

    def picked(ref, j):
        return ref[j * GROUP // WIDE, :, lanes(j, 0, GROUP)]

    def pick_group(j):
        for q in range(GROUP):
            a = lists[owner_at(j, q), 2:3, :]
            b = lists[owner_at(j, q), 3:4, :]
            odd = jnp.where(b - 1.0 >= 8.0, 1.0, 0.0)
            node = jnp.where(b > 0.0, 2.0 * a + odd, -1.0).astype(I32)
            k = jnp.where(b > 0.0, b - 1.0 - 8.0 * odd, -1.0).astype(I32)
            at = lanes(j, q, q + 1)
            pick_t[j * GROUP // WIDE, :, at] = one_hot(iota((slots, CAPL), 0) == node)
            ksel_t[j * GROUP // WIDE, :, at] = jnp.where(iota((8, CAPL), 0) == k, 1.0, 0.0)

    used = pl.ds(0, CAP)

    def ask_group(j):
        got = lax.dot_general(picked(pick_t, j), ng[...], (((0,), (0,)), ((), ())), preferred_element_type=F32)
        asked[j] = got.astype(BF16)

    def score(j, arrivals):
        round_got(rows_in.at[pl.ds(j * GROUP, arrivals), used], row_r.at[j])
        got = rows_in[j * GROUP:(j + 1) * GROUP].reshape(GROUP * CAPL, width).astype(F32)
        s = jnp.sum(got * asked[j].astype(F32), axis=1, keepdims=True)
        s = jnp.broadcast_to(s, (GROUP * CAPL, 128)).T[0:8, :]
        zs[j] = s[0:1, :]
        z_round(zs.at[j], zsr.at[j], zx_s.at[j], zx_r.at[j])
        zsr[j, z] = zs[j]

    def node_scores(j):
        z_got(zsr.at[j], zx_r.at[j])
        s = zsr[j, 0]
        for i in range(1, nz):
            s = s + zsr[j, i]
        s_hi = s.astype(BF16).astype(F32)
        mask = picked(ksel_t, j)
        by_k = jnp.concatenate([s_hi * mask, (s - s_hi) * mask], axis=0).astype(BF16)
        return dot_nt(by_k, picked(pick_t, j))

    def mix_in():
        dp_got(mixr, mix_r)
        for b in range(slots // step):
            rows = slice(b * step, (b + 1) * step)
            part = dot(live[0, rows, :], mixr[:, 0:pair_rows, :].reshape(slots, width)) + dot(
                live[1, rows, :], mixr[:, pair_rows:share, :].reshape(slots, width)
            )
            whole[z, rows, :] = part.astype(BF16)

    zright = lax.rem(z + 1, nz)
    zleft = lax.rem(z + nz - 1, nz)

    def ring_part(s, first):
        if s + 1 < nz // 2:
            return pl.ds(0, slots)
        return pl.ds(first * (slots // 2), slots // 2)

    def ring_copy(s, b, side_r):
        rows = ring_part(s, 0 if side_r else 1)
        ss, rs = (zr_s, zr_r) if side_r else (zl_s, zl_r)
        return copy(
            whole.at[b, rows], whole.at[b, rows], ss.at[s], rs.at[s], me, zright if side_r else zleft
        )

    def ring_right(s):
        return ring_copy(s, lax.rem(z - s + nz, nz), True)

    def ring_left(s):
        return ring_copy(s, lax.rem(z + s, nz), False)

    def got_right(s):
        b = lax.rem(z - s - 1 + nz, nz)
        ring_copy(s, b, True).wait_recv()
        return b

    def got_left(s):
        b = lax.rem(z + s + 1, nz)
        ring_copy(s, b, False).wait_recv()
        return b

    hops = nz // 2
    for j in range(groups):
        pick_group(j)
    scale = 1.0 / (float(full_rows) ** 0.5)

    def use_block(b, first=False):
        blk = whole[b]
        whole_t[b] = blk.T
        h = dot(blk, proj[pl.ds(pl.multiple_of(b * width, width), width), :])
        if first:
            hidden[...] = h
        else:
            hidden[...] += h

    chunk = 256

    low = CAP - HALF

    def serve(h):
        cols = idr[h].T
        hi = jnp.concatenate([cols[:, t:t + 1] for t in range(tiles)], axis=0)[:CAP]
        lo = jnp.concatenate([cols[:, tiles + t:tiles + t + 1] for t in range(tiles)], axis=0)[:CAP]
        hi = jnp.broadcast_to(hi, (CAP, chunk)).astype(BF16)
        lo = one_hot(iota((CAP, chunk), 1) == lo.astype(I32))
        halves = []
        for c in range(2):
            first = c * low
            parts = [
                jnp.where(
                    hi[first:first + HALF, :] == jnp.bfloat16(c * (block // chunk) + i + 1),
                    lo[first:first + HALF, :],
                    jnp.bfloat16(0),
                )
                for i in range(block // chunk)
            ]
            halves.append(dot(jnp.concatenate(parts, axis=1), emb[c]))
        front, rear = halves
        rows_out[h, 0:low, :] = front[0:low, :].astype(BF16)
        rows_out[h, low:HALF, :] = (front[low:, :] + rear[:HALF - low, :]).astype(BF16)
        rows_out[h, HALF:CAP, :] = rear[HALF - low:, :].astype(BF16)

    def row_send(i):
        p = to_chip(i)
        copy(
            rows_out.at[p, used], rows_in.at[i - 1, used],
            row_s.at[0], row_r.at[lax.div(i - 1, GROUP)], p * 2 + core, z,
        ).start()

    def serve_far(i):
        h = to_chip(i)
        round_got(idr.at[h], id_r.at[h])
        serve(h)
        row_send(i)

    emb_copy(1 - core).wait_recv()
    fetch[2].wait()
    done = 1
    loop(done, 1 + RING_AT, serve_far)
    done = 1 + RING_AT
    mix_in()
    ring_right(0).start()
    ring_left(0).start()
    use_block(z, True)
    for s in range(hops):
        upto = min(done + 5, chips)
        loop(done, upto, serve_far)
        done = upto
        if s + 2 == hops:
            loop(done, chips, serve_far)
            done = chips
            serve(chip)
        b = got_right(s)
        if s + 1 < hops:
            ring_right(s + 1).start()
            use_block(b)
        b = got_left(s)
        if s + 1 < hops:
            ring_left(s + 1).start()
        use_block(b)
    rows_in[chips - 1, 0:CAP, :] = rows_out[chip, 0:CAP, :]
    rows_in[:, CAP:CAPL, :] = jnp.zeros((chips, CAPL - CAP, width), BF16)
    sent.append(lambda: round_sent(rows_out.at[pl.ds(0, others), used], row_s.at[0]))
    for s in range(hops):
        sent.append(functools.partial(lambda s: ring_right(s).wait_send(), s))
        sent.append(functools.partial(lambda s: ring_left(s).wait_send(), s))

    hid = hidden[...] * scale
    hidden[...] = hid
    square = jnp.sum(hid * hid, axis=1, keepdims=True)
    ng[...] = (hid * gain).astype(BF16)
    square = jnp.broadcast_to(square, (slots, 128)).T[0:1, :]
    folds = slots // 128
    zq[...] = jnp.concatenate(
        [square[:, f * 128:(f + 1) * 128] for f in range(folds)] + [jnp.zeros((8 - folds, 128), F32)], axis=0
    )
    z_round(zq, zqr, zq_s.at[0], zq_r.at[0])
    zqr[z] = zq[...]
    for j in range(groups):
        ask_group(j)
    for j in range(groups):
        score(j, GROUP - (j + 1) // groups)

    z_got(zqr, zq_r.at[0])
    tot = zqr[0]
    for i in range(1, nz):
        tot = tot + zqr[i]
    squares = jnp.concatenate([tot[f:f + 1, :] for f in range(folds)], axis=1)
    recip = lax.rsqrt(squares / float(full_rows) + 1e-05)
    got = node_scores(0)
    for j in range(1, groups):
        got = got + node_scores(j)
    raw = got[0:8, :] + got[8:16, :]
    scores = raw * recip
    logp = scores - jnp.log(jnp.sum(jnp.exp(scores), axis=0, keepdims=True))
    prob = jnp.exp(logp)
    probs = metat[24:32, :]
    target = probs / jnp.sum(probs, axis=0, keepdims=True)
    kl = jnp.sum(target * (jnp.log(target) - logp), axis=0, keepdims=True)
    weight = 1.0 + metat[32:33, :]
    num = jnp.sum(weight * kl, axis=1, keepdims=True)
    den = jnp.sum(weight, axis=1, keepdims=True)
    gs = weight * (prob - target)
    inner = jnp.sum(gs * raw, axis=0, keepdims=True)
    back = recip * recip * recip * inner * (1.0 / float(full_rows))
    gs_hi = gs.astype(BF16).astype(F32)
    gs16 = jnp.concatenate([gs_hi, gs - gs_hi], axis=0).astype(BF16)
    coef = jnp.concatenate([recip, back, jnp.zeros((6, slots), F32)], axis=0).T

    for j in range(chips // WIDE):
        g16 = dot(gs16, pick_t[j])
        g = jnp.sum((g16[0:8, :] + g16[8:16, :]) * ksel_t[j], axis=0, keepdims=True)
        scaled = pick_t[j] * g.astype(BF16)
        part = dot(scaled, rows_in[j * WIDE:(j + 1) * WIDE].reshape(WIDE * CAPL, width))
        dnormed = part if j == 0 else dnormed + part
    dh[...] = (coef[:, 0:1] * gain * dnormed - hidden[...] * coef[:, 1:2]).astype(BF16)

    quarter = nz // 2

    def pair(q):
        return copy(pair_out.at[q], pair_in.at[q], pair_s.at[q], pair_r.at[q], sibling, z)

    def turn(q, c):
        return lax.rem(chip_y + (1 - 2 * c) * q + quarter, quarter)

    for q in range(quarter):
        pair_out[q] = (dot(whole_t[(1 - core) * quarter + turn(q, 1 - core)], dh[...]) * scale).astype(BF16)
        pair(q).start()
    for q in range(quarter):
        gown[q] = dot(whole_t[core * quarter + turn(q, core)], dh[...]) * scale
    per = chips // quarter

    part_rows = width // per

    def rs_send(c, i, p):
        copy(rs_out.at[c, p], rs_in.at[c, i], rs_s.at[c], rs_r.at[c], p * 2 + core, z).start()

    batches = BATCHES
    batch = others // batches

    def ag_send(c, i):
        p = to_chip(i)
        copy(
            gfull.at[core, c, 0], gfull.at[core, c, i],
            ag_s.at[c], ag_r.at[c * batches + (i - 1) // batch], p * 2 + core, z,
        ).start()

    def forward(c, b, side_core):
        at = pl.ds(0, 1) if b == batches else pl.ds(1 + b * batch, batch)
        ref = gfull.at[side_core, c, at]
        n = c * (batches + 1) + b
        return copy(ref, ref, fw_s.at[n], fw_r.at[n], sibling, z)

    for q in range(quarter):
        pair(q).wait_recv()
        both = (gown[q] + pair_in[q].astype(F32)).astype(BF16).reshape(per, CH, part_rows, width)
        first = turn(q, core) * per
        for c in range(CH):
            rs_out[c, pl.ds(first, per)] = both[:, c]
        for i in range(1 if q == 0 else 0, per):
            rs_send(0, q * per + i, first + lax.rem(chip_x + (1 - 2 * core) * i + per, per))
    for c in range(1, CH):
        loop(1, chips, lambda i: rs_send(c, i, to_chip(i)))
    for q in range(quarter):
        sent.append(functools.partial(lambda q: pair(q).wait_send(), q))
    for c in range(CH):
        sent.append(functools.partial(lambda c: round_sent(rs_out.at[c, pl.ds(0, others)], rs_s.at[c]), c))
        sent.append(functools.partial(lambda c: round_sent(gfull.at[core, c, pl.ds(0, others)], ag_s.at[c]), c))
        for b in range(batches + 1):
            sent.append(functools.partial(lambda c, b: forward(c, b, core).wait_send(), c, b))
    def spread_shard(c):
        starts(1, chips, lambda i: ag_send(c, i))
        forward(c, batches, core).start()

    energy = jnp.zeros((1, 1), F32)
    for c in range(CH):
        rs_in[c, 0] = rs_out[c, chip]
        round_got(rs_in.at[c, pl.ds(1, others)], rs_r.at[c])
        shard = rs_in[c, 0].astype(F32)
        for p in range(1, chips):
            shard = shard + rs_in[c, p].astype(F32)
        gfull[core, c, 0] = shard.astype(BF16)
        energy = energy + jnp.sum(jnp.sum(shard * shard, axis=1, keepdims=True), axis=0, keepdims=True)
        if c + 1 < CH:
            spread_shard(c)
    row = iota((8, 128), 0)
    tile = jnp.where(row == 0, energy, jnp.where(row == 1, num, jnp.where(row == 2, den, over)))

    sb_out[...] = tile
    both_cores = copy(sb_out, sb, sb_s.at[0], sb_r.at[0], sibling, z)
    both_cores.start()
    spread_shard(CH - 1)

    sent.append(both_cores.wait_send)

    def ag_pass(c, b):
        round_got(gfull.at[core, c, pl.ds(1 + b * batch, batch)], ag_r.at[c * batches + b])
        forward(c, b, core).start()

    both_cores.wait_recv()
    tile = tile + sb[...]
    ez_out[...] = tile
    z_round(ez_out, ez, ez_s.at[0], ez_r.at[0])
    ez[z] = tile
    z_got(ez, ez_r.at[0])
    etot = ez[0]
    for i in range(1, nz):
        etot = etot + ez[i]
    tile = jnp.where(row == 0, etot, tile)
    dt_out[...] = tile

    def tell(i):
        copy(dt_out, dt.at[i], dt_s.at[0], dt_r.at[0], to_chip(i) * 2 + core, z).start()

    starts(1, chips, tell)
    sent.append(lambda: round_sent(dt.at[pl.ds(1, others)], dt_s.at[0]))
    dt[0] = tile
    for c in range(CH):
        for b in range(batches):
            ag_pass(c, b)
    round_got(dt.at[pl.ds(1, others)], dt_r.at[0])
    total = dt[0]
    for i in range(1, chips):
        total = total + dt[i]
    entries = float(full_rows) * float(full_rows)
    factor = 0.5 * lax.rsqrt(total[0:1, 0:1] / entries + 1e-06)
    loss_out[...] = total[1:2, 0:1] / total[2:3, 0:1]
    flag_out[...] = total[3:4, 0:1]

    blk_rows = width // per

    def finish(h, c, i, p):
        at = (h * chips + p) * blk_rows + c * part_rows
        r = pl.ds(pl.multiple_of(at, part_rows), part_rows)
        out[r, :] = (proj[r, :].astype(F32) - gfull[h, c, i].astype(F32) * factor).astype(BF16)

    for c in range(CH):
        starts(0, chips, lambda i: finish(core, c, i, from_chip(i)))
    for c in range(CH):
        for b in range(batches, -1, -1):
            forward(c, b, 1 - core).wait_recv()
        starts(0, chips, lambda i: finish(1 - core, c, i, from_chip(i, True)))

    for wait in sent:
        wait()


def fast_step(nd, nz, feats, parent, counts, accepted, cand_ids, target_probs, gain, embed, proj):
    nodes, width = feats.shape
    full_rows = proj.shape[0]
    share = nodes // nd
    vocab = embed.shape[0]
    slots = nodes // 2
    chips = nd // 2
    quarter = nz // 2
    per = chips // quarter
    vm = pltpu.VMEM
    scratch = [
        vm(feats.shape, BF16),
        vm(embed.shape, BF16),
        vm(proj.shape, BF16),
        pltpu.SemaphoreType.DMA((3,)),
        vm((2, -(-vocab // 256) * 256, width), BF16),
        vm((nodes, nodes), BF16),
        vm((nodes, 128), BF16),
        vm((nodes, 128), F32),
        vm((nd, share // 2, 128), BF16),
        vm((nd, share // 2, 128), BF16),
        vm((nd, share, width), BF16),
        vm((nd, share, width), BF16),
        vm((2, slots, slots), BF16),
        vm((64, slots), F32),
        vm((chips, 8, CAPL), F32),
        vm((chips, 8, 128), F32),
        vm((chips, 8, 128), F32),
        vm((chips, CAPL, width), BF16),
        vm((chips, CAPL, width), BF16),
        vm((nz, slots, width), BF16),
        vm((nz, width, slots), BF16),
        vm((slots, width), F32),
        vm((slots, width), BF16),
        vm((chips // WIDE, slots, WIDE * CAPL), BF16),
        vm((chips // WIDE, 8, WIDE * CAPL), F32),
        vm((chips // GROUP, GROUP * CAPL, width), BF16),
        vm((8, 128), F32),
        vm((nz, 8, 128), F32),
        vm((chips // GROUP, 1, GROUP * CAPL), F32),
        vm((chips // GROUP, nz, 1, GROUP * CAPL), F32),
        vm((slots, width), BF16),
        vm((quarter, width, width), BF16),
        vm((quarter, width, width), BF16),
        vm((quarter, width, width), F32),
        vm((CH, chips, width // per // CH, width), BF16),
        vm((CH, chips, width // per // CH, width), BF16),
        vm((2, CH, chips, width // per // CH, width), BF16),
        vm((8, 128), F32),
        vm((8, 128), F32),
        vm((8, 128), F32),
        vm((nz, 8, 128), F32),
        vm((8, 128), F32),
        vm((chips, 8, 128), F32),
    ]
    dma = pltpu.SemaphoreType.DMA
    for count in (
        2, 2, 1, 1, 1, 1, 1, chips, 1, chips // GROUP,
        nz, nz, nz, nz, chips // GROUP, chips // GROUP, 1, 1, quarter, quarter,
        CH, CH, CH, BATCHES * CH, (BATCHES + 1) * CH, (BATCHES + 1) * CH, 1, 1, 1, 1, 1, 1,
    ):
        scratch.append(dma((count,)))
    in_vmem = pl.BlockSpec(memory_space=pltpu.VMEM)
    return pl.pallas_call(
        functools.partial(step_kernel, nd, nz, full_rows),
        out_shape=(
            jax.ShapeDtypeStruct(proj.shape, BF16),
            jax.ShapeDtypeStruct((1, 1), F32),
            jax.ShapeDtypeStruct((1, 1), F32),
        ),
        in_specs=[pl.BlockSpec(memory_space=pltpu.SMEM)] + [in_vmem] * 5 + [pl.BlockSpec(memory_space=pl.ANY)] * 3,
        out_specs=(in_vmem, in_vmem, in_vmem),
        scratch_shapes=scratch,
        compiler_params=pltpu.CompilerParams(
            collective_id=0, has_side_effects=True, vmem_limit_bytes=60 * 1024 * 1024
        ),
        name="step",
    )(
        counts, cand_ids.T, target_probs.T, parent.reshape(8, nodes // 8), accepted.reshape(8, nodes // 8),
        gain.reshape(2, width // 2), feats, embed, proj,
    )


def every(x, axis):
    n = lax.axis_size(axis)
    return lax.all_to_all(jnp.broadcast_to(x[None], (n,) + x.shape), axis, 0, 0, tiled=True)


def total(x, axis):
    return jnp.sum(every(jnp.atleast_1d(x), axis), axis=0).reshape(x.shape)


def wide_step(feats, parent, counts, accepted, cand_ids, target_probs, gain, embed, proj):
    node_rows, width_part = feats.shape
    full_width = proj.shape[0]
    group = lax.axis_index("dp")
    groups = lax.axis_size("dp")
    shard_rows = embed.shape[0]
    cand_count = cand_ids.shape[1]
    scale_in = 1.0 / jnp.sqrt(jnp.float32(full_width))
    gain_f = gain.astype(jnp.float32)
    flat_ids = cand_ids.reshape(-1)
    requests = flat_ids.shape[0]
    capacity = 3 * requests // (2 * groups)
    owners = flat_ids // shard_rows
    local_ids = flat_ids - owners * shard_rows
    member = owners[:, None] == jnp.arange(groups, dtype=jnp.int32)[None, :]
    per_owner = jnp.sum(member.astype(jnp.int32), axis=0)
    starts = jnp.cumsum(per_owner) - per_owner
    my_start = jnp.sum(jnp.where(member, starts[None, :], 0), axis=1)
    order = jnp.argsort(owners, stable=True)
    ranks = jnp.arange(requests, dtype=jnp.int32) - my_start[order]
    slots = owners[order] * capacity + ranks
    outgoing = jnp.zeros((groups * capacity,), jnp.int32).at[slots].set(local_ids[order])
    placed = jnp.zeros((requests,), jnp.int32).at[order].set(slots)
    mixed = (feats.astype(jnp.float32) + feats[parent].astype(jnp.float32)).astype(jnp.bfloat16)
    piece = every(mixed, "mp").transpose(1, 0, 2).reshape(node_rows, full_width)
    partial_value = jnp.dot(piece, proj, preferred_element_type=jnp.float32)
    whole = piece
    partial_value, whole = (partial_value, whole)
    hidden = partial_value * scale_in
    squares = total(jnp.sum(hidden * hidden, axis=1), "mp")
    recip = lax.rsqrt(squares / full_width + 1e-05)
    normed = (hidden * recip[:, None] * gain_f).astype(jnp.bfloat16)
    found = embed[
        lax.all_to_all(
            outgoing.reshape(groups, capacity), "dp", split_axis=0, concat_axis=0, tiled=True
        )
    ]
    fetched = lax.all_to_all(found, "dp", split_axis=0, concat_axis=0, tiled=True)
    cand_rows = fetched.reshape(groups * capacity, width_part)[placed].reshape(
        node_rows, cand_count, width_part
    )
    part_scores = jnp.einsum("nkd,nd->nk", cand_rows, normed, preferred_element_type=jnp.float32)
    scores = total(part_scores, "mp")
    logp = scores - jnp.log(jnp.sum(jnp.exp(scores), axis=1, keepdims=True))
    prob = jnp.exp(logp)
    probs = target_probs.astype(jnp.float32)
    target = probs / jnp.sum(probs, axis=1, keepdims=True)
    kl_node = jnp.sum(target * (jnp.log(target) - logp), axis=1)
    live_count = lax.dynamic_index_in_dim(counts, group, 0, keepdims=False)
    live = jnp.arange(node_rows, dtype=jnp.int32) < live_count
    weight = jnp.where(live, 1 + accepted, 0).astype(jnp.float32)
    num, den = total(jnp.stack([jnp.sum(weight * kl_node), jnp.sum(weight)]), "dp")
    grad_scores = weight[:, None] * (prob - target)
    dnormed = jnp.einsum("nk,nkd->nd", grad_scores, cand_rows, preferred_element_type=jnp.float32)
    inner = total(jnp.sum(dnormed * gain_f * hidden, axis=1), "mp")
    dhidden = (
        recip[:, None] * gain_f * dnormed - hidden * (recip**3 * inner / full_width)[:, None]
    ).astype(jnp.bfloat16)
    grad_part = (
        lax.dot_general(
            whole, dhidden, (((0,), (0,)), ((), ())), preferred_element_type=jnp.float32
        )
        * scale_in
    )
    shares = lax.all_to_all(grad_part.reshape(groups, -1, width_part), "dp", 0, 0, tiled=True)
    grad = every(jnp.sum(shares, axis=0), "dp").reshape(full_width, width_part)
    energy = total(jnp.sum(grad * grad), "mp")
    factor = lax.rsqrt(energy / (full_width * full_width) + 1e-06)
    new_proj = (proj.astype(jnp.float32) - 0.5 * grad * factor).astype(jnp.bfloat16)
    return (new_proj, num / den)


def solution(mesh):
    nd = mesh.shape["dp"]
    nz = mesh.shape["mp"]

    def per_device(*args):
        out, loss, flag = fast_step(nd, nz, *args)
        return lax.cond(
            flag[0, 0] > 0.0,
            lambda: wide_step(*args),
            lambda: (out, loss[0, 0]),
        )

    placed = (
        P("dp", "mp"),
        P("dp"),
        P(),
        P("dp"),
        P("dp", None),
        P("dp", None),
        P("mp"),
        P("dp", "mp"),
        P(None, "mp"),
    )
    return jax.shard_map(
        per_device, mesh=mesh, in_specs=placed, out_specs=(P(None, "mp"), P()), check_vma=False
    )
```

```python
import functools
import jax
import jax.numpy as jnp
from jax import lax
from jax.experimental import pallas as pl
from jax.experimental.pallas import tpu as pltpu
from jax.sharding import PartitionSpec as P

MESH = pl.DeviceIdType.MESH
F32 = jnp.float32
BF16 = jnp.bfloat16
I32 = jnp.int32

GROUP = 2
WIDE = 4
CH = 1
BATCHES = 5
RING_AT = 2
CAP = 352
CAPL = 384
HALF = 224


def dot(a, b):
    return jnp.dot(a, b, preferred_element_type=F32)


def dot_nt(a, b):
    return lax.dot_general(a, b, (((1,), (1,)), ((), ())), preferred_element_type=F32)


def one_hot(hit):
    return jnp.where(hit, 1.0, 0.0).astype(BF16)


def iota(shape, axis):
    return lax.broadcasted_iota(I32, shape, axis)


def step_kernel(
    nd, nz, full_rows,
    counts, ids, odds, parent, accepted, gain2, feats_in, embed_in, proj_in,
    out, loss_out, flag_out,
    feats, embed, proj, in_s, emb, perm, meta, mixat, metap, metar, mixp, mixr, live, metat,
    lists, sendid, idr, rows_out, rows_in, whole, whole_t, hidden, ng,
    pick_t, ksel_t, asked, zq, zqr, zs, zsr, dh,
    pair_out, pair_in, gown, rs_out, rs_in, gfull, sb_out, sb, ez_out, ez, dt_out, dt,
    emb_s, emb_r, meta_s, meta_r, mix_s, mix_r, id_s, id_r, row_s, row_r,
    zr_s, zr_r, zl_s, zl_r, zx_s, zx_r, zq_s, zq_r, pair_s, pair_r,
    rs_s, rs_r, ag_s, ag_r, fw_s, fw_r, sb_s, sb_r, ez_s, ez_r, dt_s, dt_r,
):
    me = lax.axis_index("dp")
    z = lax.axis_index("mp")
    nodes = feats.shape[0]
    width = feats.shape[1]
    slots = live.shape[1]
    share = nodes // nd
    core = lax.rem(me, 2)
    chip = lax.div(me, 2)
    chips = nd // 2
    sibling = me + 1 - 2 * core
    vocab = embed.shape[0]

    sent = []

    fetch = [
        pltpu.make_async_copy(src, dst, in_s.at[i])
        for i, (src, dst) in enumerate(((feats_in, feats), (embed_in, embed), (proj_in, proj)))
    ]
    for f in fetch:
        f.start()

    def each(lo, hi, body):
        for i in range(lo, hi):
            body(i)

    def copy(src, dst, ss, rs, d, zz):
        return pltpu.make_async_remote_copy(
            src_ref=src, dst_ref=dst, send_sem=ss, recv_sem=rs,
            device_id=(d, zz), device_id_type=MESH,
        )

    def nxt(i):
        return lax.rem(me + i, nd)

    def prv(i):
        return lax.rem(me - i + nd, nd)

    def loop(lo, hi, body):
        def wrapped(i, carry):
            body(i)
            return carry
        lax.fori_loop(lo, hi, wrapped, 0)

    side = int(chips ** 0.5)
    chip_x = lax.rem(chip, side)
    chip_y = lax.div(chip, side)

    def offset(i):
        if isinstance(i, int):
            dx = i % side
            dy = (i // side + i) % side
        else:
            dx = lax.rem(i, side)
            dy = lax.rem(lax.div(i, side) + i, side)
        return dx + core * (dy - dx), dy + core * (dx - dy)

    def to_chip(i):
        dx, dy = offset(i)
        return lax.rem(chip_y + dy, side) * side + lax.rem(chip_x + dx, side)

    def from_chip(i, sibling_order=False):
        dx, dy = offset(i)
        if sibling_order:
            dx, dy = dy, dx
        return lax.rem(chip_y - dy + side, side) * side + lax.rem(chip_x - dx + side, side)

    others = chips - 1

    def round_got(dst, rs):
        copy(dst, dst, rs, rs, sibling, z).wait_recv()

    def round_sent(src, ss):
        copy(src, src, ss, ss, sibling, z).wait_send()

    def each_device(act):
        act(sibling)

        def both(i):
            act(to_chip(i) * 2 + core)
            act(to_chip(i) * 2 + 1 - core)

        loop(1, chips, both)

    def z_round(src, dst, ss, rs):
        def one(i):
            copy(src, dst.at[z], ss, rs, me, lax.rem(z + i, nz)).start()

        loop(1, nz, one)
        sent.append(lambda: round_sent(dst.at[pl.ds(0, nz - 1)], ss))

    def z_got(dst, rs):
        round_got(dst.at[pl.ds(0, nz - 1)], rs)

    def dp_round(src, dst, ss, rs):
        each_device(lambda d: copy(src.at[d], dst.at[me], ss.at[0], rs.at[0], d, z).start())
        sent.append(lambda: round_sent(src.at[pl.ds(0, nd - 1)], ss.at[0]))

    def dp_got(dst, rs):
        round_got(dst.at[pl.ds(0, nd - 1)], rs.at[0])

    barrier = pltpu.get_barrier_semaphore()
    loop(1, nd, lambda i: pl.semaphore_signal(barrier, inc=1, device_id=(nxt(i), z), device_id_type=MESH))
    loop(1, nz, lambda i: pl.semaphore_signal(barrier, inc=1, device_id=(me, lax.rem(z + i, nz)), device_id_type=MESH))

    pair_rows = share // 2
    node_lane = iota((1, nodes), 1)
    src_lane = iota((1, slots), 1)
    lane_h = lax.div(src_lane, pair_rows)
    lane_j = 2 * (src_lane - lane_h * pair_rows)

    def deal(h, state):
        off, mine, into0, into1 = state
        count = counts[h]
        first = (me - off) & (nd - 1)
        base = (off + first) // nd
        row0 = jnp.where(lane_j * nd + first < count, base + lane_j, -1)
        row1 = jnp.where((lane_j + 1) * nd + first < count, base + lane_j + 1, -1)
        here = lane_h == h
        return (
            off + count, jnp.where(h == me, off, mine),
            jnp.where(here, row0, into0), jnp.where(here, row1, into1),
        )

    none = jnp.full((1, slots), -1, I32)
    _, mine, into0, into1 = lax.fori_loop(0, nd, deal, (jnp.int32(0), jnp.int32(0), none, none))
    place_j = lax.div(node_lane, nd)
    dealt = (
        ((node_lane + mine) & (nd - 1)) * share
        + (place_j & 1) * pair_rows + lax.div(place_j, 2)
    )
    gain = jnp.concatenate([gain2[0:1, :], gain2[1:2, :]], axis=1).astype(F32)

    def in_row(ref):
        return jnp.concatenate([ref[r:r + 1, :] for r in range(ref.shape[0])], axis=1)

    idf = ids[...].astype(F32)
    own_f = jnp.floor((idf + 0.5) * (1.0 / float(vocab)))
    at_f = idf - own_f * float(vocab)
    hi_f = jnp.floor(at_f * (1.0 / 256.0))
    par = in_row(parent)
    extra = jnp.concatenate(
        [
            in_row(accepted).astype(F32),
            (par // 32).astype(F32),
            (par % 32).astype(F32),
            jnp.zeros((5, nodes), F32),
        ],
        axis=0,
    )
    table = jnp.concatenate(
        [own_f, hi_f + 1.0, at_f - 256.0 * hi_f, odds[...].astype(F32), extra, jnp.zeros((88, nodes), F32)],
        axis=0,
    )
    meta[...] = table.T.astype(BF16)

    step = 128

    def perm_block(b):
        rows = pl.ds(b * step, step)
        e = one_hot(iota((step, nodes), 0) + b * step == dealt)
        perm[rows, :] = e
        m = dot(e, meta[...])
        mixat[rows, :] = m
        m = m.astype(BF16).reshape(step // share, 2, pair_rows, 128)
        metap[pl.ds(b * (step // share), step // share)] = jnp.concatenate(
            [m[:, 0, :, 0:64], m[:, 1, :, 0:64]], axis=-1
        )

    loop(0, nodes // step, perm_block)

    fetch[1].wait()
    block = emb.shape[1]
    even = vocab // 32 * 32
    emb[core, 0:even, :] = embed[0:even, :]
    emb[core, even:block, :] = jnp.concatenate(
        [embed[even:vocab, :].astype(F32), jnp.zeros((block - vocab, width), F32)], axis=0
    ).astype(BF16)
    pl.semaphore_wait(barrier, nd - 1 + nz - 1)

    def emb_copy(c):
        return copy(emb.at[c], emb.at[c], emb_s.at[c], emb_r.at[c], sibling, z)

    emb_copy(core).start()
    sent.append(lambda: emb_copy(core).wait_send())
    dp_round(metap, metar, meta_s, meta_r)
    metar[me] = metap[me]

    def mixp_block(b):
        rows = pl.ds(b * step, step)
        at = mixat[rows, 33:34] * 32.0 + mixat[rows, 34:35]
        p = one_hot(iota((step, nodes), 1) == at.astype(I32))
        mixp[pl.ds(b * (step // share), step // share)] = (
            dot(perm[rows, :] + p, feats[...])
            .astype(BF16)
            .reshape(step // share, share, width)
        )

    fetch[0].wait()
    loop(0, nodes // step, mixp_block)
    dp_round(mixp, mixr, mix_s, mix_r)
    mixr[me] = mixp[me]

    def live_block(b):
        at = iota((step, slots), 0) + b * step
        live[0, pl.ds(b * step, step), :] = one_hot(at == into0)
        live[1, pl.ds(b * step, step), :] = one_hot(at == into1)

    loop(0, slots // step, live_block)

    dp_got(metar, meta_r)
    for b in range(slots // step):
        rows = slice(b * step, (b + 1) * step)
        got = metar[...].reshape(slots, metar.shape[2])
        part = dot(live[0, rows, :], got)[:, 0:64] + dot(live[1, rows, :], got)[:, 64:128]
        metat[:, rows] = part.T

    owner = metat[0:8, :].astype(I32)
    upper = one_hot(iota((slots, slots), 0) < iota((slots, slots), 1))
    own_iota = iota((nd, slots), 0)
    member = jnp.concatenate(
        [jnp.where(own_iota == owner[k:k + 1, :], 1.0, 0.0) for k in range(8)], axis=0
    )
    before = dot(member.astype(BF16), upper)
    carry = jnp.zeros((nd, 1), F32)
    found = jnp.zeros((chips * 8, CAPL), F32)
    asks = jnp.zeros((chips, 1), F32)
    at_chip = owner // 2
    odd_core = owner - 2 * at_chip
    chip_iota = iota((chips, slots), 0)
    node_row = iota((1, slots), 1)
    for k in range(8):
        mk = member[k * nd:(k + 1) * nd, :]
        rank = jnp.sum(mk * (before[k * nd:(k + 1) * nd, :] + carry), axis=0, keepdims=True)
        carry = carry + jnp.sum(mk, axis=1, keepdims=True)
        odd_k = odd_core[k:k + 1, :].astype(F32)
        place = rank + odd_k * (float(CAP - 1) - 2.0 * rank)
        asks = asks + jnp.sum(jnp.where(chip_iota == at_chip[k:k + 1, :], 1.0, 0.0), axis=1, keepdims=True)
        fields = jnp.concatenate(
            [
                metat[8 + k:9 + k, :] + float(block // 256) * odd_k,
                metat[16 + k:17 + k, :],
                (node_row // 2).astype(F32),
                ((node_row % 2) * 8 + (k + 1)).astype(F32),
                jnp.zeros((4, slots), F32),
            ],
            axis=0,
        )
        here = iota((chips, 8, slots), 0) == at_chip[k:k + 1, :][None]
        f = jnp.where(here, fields[None], 0.0).reshape(chips * 8, slots).astype(BF16)
        at = one_hot(iota((CAPL, slots), 0) == place.astype(I32))
        found = found + dot_nt(f, at)
    found = found.reshape(chips, 8, CAPL)
    lists[...] = found
    tiles = CAPL // 128
    sendid[...] = jnp.concatenate(
        [found[:, f:f + 1, t * 128:(t + 1) * 128] for f in range(2) for t in range(tiles)]
        + [jnp.zeros((chips, 8 - 2 * tiles, 128), F32)],
        axis=1,
    )
    over = jnp.maximum(
        jnp.max(jnp.where(carry > float(HALF), 1.0, 0.0), axis=0, keepdims=True),
        jnp.max(jnp.where(asks > float(CAP), 1.0, 0.0), axis=0, keepdims=True),
    )

    def ask(i):
        p = to_chip(i)
        copy(sendid.at[p], idr.at[chip], id_s.at[0], id_r.at[chip], p * 2 + core, z).start()

    loop(1, chips, ask)
    sent.append(lambda: round_sent(sendid.at[pl.ds(0, others)], id_s.at[0]))
    idr[chip] = sendid[chip]

    def owner_at(j, q):
        return from_chip(j * GROUP + q + 1)

    groups = chips // GROUP

    def lanes(j, lo, hi):
        first = j * GROUP % WIDE
        return slice((first + lo) * CAPL, (first + hi) * CAPL)

    def picked(ref, j):
        return ref[j * GROUP // WIDE, :, lanes(j, 0, GROUP)]

    def pick_group(j):
        for q in range(GROUP):
            a = lists[owner_at(j, q), 2:3, :]
            b = lists[owner_at(j, q), 3:4, :]
            odd = jnp.where(b - 1.0 >= 8.0, 1.0, 0.0)
            node = jnp.where(b > 0.0, 2.0 * a + odd, -1.0).astype(I32)
            k = jnp.where(b > 0.0, b - 1.0 - 8.0 * odd, -1.0).astype(I32)
            at = lanes(j, q, q + 1)
            pick_t[j * GROUP // WIDE, :, at] = one_hot(iota((slots, CAPL), 0) == node)
            ksel_t[j * GROUP // WIDE, :, at] = jnp.where(iota((8, CAPL), 0) == k, 1.0, 0.0)

    used = pl.ds(0, CAP)

    def ask_group(j):
        got = lax.dot_general(picked(pick_t, j), ng[...], (((0,), (0,)), ((), ())), preferred_element_type=F32)
        asked[j] = got.astype(BF16)

    def score(j, arrivals):
        round_got(rows_in.at[pl.ds(j * GROUP, arrivals), used], row_r.at[j])
        got = rows_in[j * GROUP:(j + 1) * GROUP].reshape(GROUP * CAPL, width).astype(F32)
        s = jnp.sum(got * asked[j].astype(F32), axis=1, keepdims=True)
        s = jnp.broadcast_to(s, (GROUP * CAPL, 128)).T[0:8, :]
        zs[j] = s[0:1, :]
        z_round(zs.at[j], zsr.at[j], zx_s.at[j], zx_r.at[j])
        zsr[j, z] = zs[j]

    def node_scores(j):
        z_got(zsr.at[j], zx_r.at[j])
        s = zsr[j, 0]
        for i in range(1, nz):
            s = s + zsr[j, i]
        s_hi = s.astype(BF16).astype(F32)
        mask = picked(ksel_t, j)
        by_k = jnp.concatenate([s_hi * mask, (s - s_hi) * mask], axis=0).astype(BF16)
        return dot_nt(by_k, picked(pick_t, j))

    def mix_in():
        dp_got(mixr, mix_r)
        for b in range(slots // step):
            rows = slice(b * step, (b + 1) * step)
            part = dot(live[0, rows, :], mixr[:, 0:pair_rows, :].reshape(slots, width)) + dot(
                live[1, rows, :], mixr[:, pair_rows:share, :].reshape(slots, width)
            )
            whole[z, rows, :] = part.astype(BF16)

    zright = lax.rem(z + 1, nz)
    zleft = lax.rem(z + nz - 1, nz)

    def ring_part(s, first):
        if s + 1 < nz // 2:
            return pl.ds(0, slots)
        return pl.ds(first * (slots // 2), slots // 2)

    def ring_copy(s, b, side_r):
        rows = ring_part(s, 0 if side_r else 1)
        ss, rs = (zr_s, zr_r) if side_r else (zl_s, zl_r)
        return copy(
            whole.at[b, rows], whole.at[b, rows], ss.at[s], rs.at[s], me, zright if side_r else zleft
        )

    def ring_right(s):
        return ring_copy(s, lax.rem(z - s + nz, nz), True)

    def ring_left(s):
        return ring_copy(s, lax.rem(z + s, nz), False)

    def got_right(s):
        b = lax.rem(z - s - 1 + nz, nz)
        ring_copy(s, b, True).wait_recv()
        return b

    def got_left(s):
        b = lax.rem(z + s + 1, nz)
        ring_copy(s, b, False).wait_recv()
        return b

    hops = nz // 2
    for j in range(groups):
        pick_group(j)
    scale = 1.0 / (float(full_rows) ** 0.5)

    def use_block(b, first=False):
        blk = whole[b]
        whole_t[b] = blk.T
        h = dot(blk, proj[pl.ds(pl.multiple_of(b * width, width), width), :])
        if first:
            hidden[...] = h
        else:
            hidden[...] += h

    chunk = 256

    low = CAP - HALF

    def serve(h):
        cols = idr[h].T
        hi = jnp.concatenate([cols[:, t:t + 1] for t in range(tiles)], axis=0)[:CAP]
        lo = jnp.concatenate([cols[:, tiles + t:tiles + t + 1] for t in range(tiles)], axis=0)[:CAP]
        hi = jnp.broadcast_to(hi, (CAP, chunk)).astype(BF16)
        lo = one_hot(iota((CAP, chunk), 1) == lo.astype(I32))
        halves = []
        for c in range(2):
            first = c * low
            parts = [
                jnp.where(
                    hi[first:first + HALF, :] == jnp.bfloat16(c * (block // chunk) + i + 1),
                    lo[first:first + HALF, :],
                    jnp.bfloat16(0),
                )
                for i in range(block // chunk)
            ]
            halves.append(dot(jnp.concatenate(parts, axis=1), emb[c]))
        front, rear = halves
        rows_out[h, 0:low, :] = front[0:low, :].astype(BF16)
        rows_out[h, low:HALF, :] = (front[low:, :] + rear[:HALF - low, :]).astype(BF16)
        rows_out[h, HALF:CAP, :] = rear[HALF - low:, :].astype(BF16)

    def row_send(i):
        p = to_chip(i)
        copy(
            rows_out.at[p, used], rows_in.at[i - 1, used],
            row_s.at[0], row_r.at[lax.div(i - 1, GROUP)], p * 2 + core, z,
        ).start()

    def serve_far(i):
        h = to_chip(i)
        round_got(idr.at[h], id_r.at[h])
        serve(h)
        row_send(i)

    emb_copy(1 - core).wait_recv()
    fetch[2].wait()
    done = 1
    loop(done, 1 + RING_AT, serve_far)
    done = 1 + RING_AT
    mix_in()
    ring_right(0).start()
    ring_left(0).start()
    use_block(z, True)
    for s in range(hops):
        upto = min(done + 5, chips)
        loop(done, upto, serve_far)
        done = upto
        if s + 2 == hops:
            loop(done, chips, serve_far)
            done = chips
            serve(chip)
        b = got_right(s)
        if s + 1 < hops:
            ring_right(s + 1).start()
            use_block(b)
        b = got_left(s)
        if s + 1 < hops:
            ring_left(s + 1).start()
        use_block(b)
    rows_in[chips - 1, 0:CAP, :] = rows_out[chip, 0:CAP, :]
    rows_in[:, CAP:CAPL, :] = jnp.zeros((chips, CAPL - CAP, width), BF16)
    sent.append(lambda: round_sent(rows_out.at[pl.ds(0, others), used], row_s.at[0]))
    for s in range(hops):
        sent.append(functools.partial(lambda s: ring_right(s).wait_send(), s))
        sent.append(functools.partial(lambda s: ring_left(s).wait_send(), s))

    hid = hidden[...] * scale
    hidden[...] = hid
    square = jnp.sum(hid * hid, axis=1, keepdims=True)
    ng[...] = (hid * gain).astype(BF16)
    square = jnp.broadcast_to(square, (slots, 128)).T[0:1, :]
    folds = slots // 128
    zq[...] = jnp.concatenate(
        [square[:, f * 128:(f + 1) * 128] for f in range(folds)] + [jnp.zeros((8 - folds, 128), F32)], axis=0
    )
    z_round(zq, zqr, zq_s.at[0], zq_r.at[0])
    zqr[z] = zq[...]
    for j in range(groups):
        ask_group(j)
    for j in range(groups):
        score(j, GROUP - (j + 1) // groups)

    z_got(zqr, zq_r.at[0])
    tot = zqr[0]
    for i in range(1, nz):
        tot = tot + zqr[i]
    squares = jnp.concatenate([tot[f:f + 1, :] for f in range(folds)], axis=1)
    recip = lax.rsqrt(squares / float(full_rows) + 1e-05)
    got = node_scores(0)
    for j in range(1, groups):
        got = got + node_scores(j)
    raw = got[0:8, :] + got[8:16, :]
    scores = raw * recip
    logp = scores - jnp.log(jnp.sum(jnp.exp(scores), axis=0, keepdims=True))
    prob = jnp.exp(logp)
    probs = metat[24:32, :]
    target = probs / jnp.sum(probs, axis=0, keepdims=True)
    kl = jnp.sum(target * (jnp.log(target) - logp), axis=0, keepdims=True)
    weight = 1.0 + metat[32:33, :]
    num = jnp.sum(weight * kl, axis=1, keepdims=True)
    den = jnp.sum(weight, axis=1, keepdims=True)
    gs = weight * (prob - target)
    inner = jnp.sum(gs * raw, axis=0, keepdims=True)
    back = recip * recip * recip * inner * (1.0 / float(full_rows))
    gs_hi = gs.astype(BF16).astype(F32)
    gs16 = jnp.concatenate([gs_hi, gs - gs_hi], axis=0).astype(BF16)
    coef = jnp.concatenate([recip, back, jnp.zeros((6, slots), F32)], axis=0).T

    for j in range(chips // WIDE):
        g16 = dot(gs16, pick_t[j])
        g = jnp.sum((g16[0:8, :] + g16[8:16, :]) * ksel_t[j], axis=0, keepdims=True)
        scaled = pick_t[j] * g.astype(BF16)
        part = dot(scaled, rows_in[j * WIDE:(j + 1) * WIDE].reshape(WIDE * CAPL, width))
        dnormed = part if j == 0 else dnormed + part
    dh[...] = (coef[:, 0:1] * gain * dnormed - hidden[...] * coef[:, 1:2]).astype(BF16)

    quarter = nz // 2

    def pair(q):
        return copy(pair_out.at[q], pair_in.at[q], pair_s.at[q], pair_r.at[q], sibling, z)

    def turn(q, c):
        return lax.rem(chip_y + (1 - 2 * c) * q + quarter, quarter)

    for q in range(quarter):
        pair_out[q] = (dot(whole_t[(1 - core) * quarter + turn(q, 1 - core)], dh[...]) * scale).astype(BF16)
        pair(q).start()
    for q in range(quarter):
        gown[q] = dot(whole_t[core * quarter + turn(q, core)], dh[...]) * scale
    per = chips // quarter

    part_rows = width // per

    def rs_send(c, i, p):
        copy(rs_out.at[c, p], rs_in.at[c, i], rs_s.at[c], rs_r.at[c], p * 2 + core, z).start()

    batches = BATCHES
    batch = others // batches

    def ag_send(c, i):
        p = to_chip(i)
        copy(
            gfull.at[core, c, 0], gfull.at[core, c, i],
            ag_s.at[c], ag_r.at[c * batches + lax.div(i - 1, batch)], p * 2 + core, z,
        ).start()

    def forward(c, b, side_core):
        at = pl.ds(0, 1) if b == batches else pl.ds(1 + b * batch, batch)
        ref = gfull.at[side_core, c, at]
        n = c * (batches + 1) + b
        return copy(ref, ref, fw_s.at[n], fw_r.at[n], sibling, z)

    for q in range(quarter):
        pair(q).wait_recv()
        both = (gown[q] + pair_in[q].astype(F32)).astype(BF16).reshape(per, CH, part_rows, width)
        first = turn(q, core) * per
        for c in range(CH):
            rs_out[c, pl.ds(first, per)] = both[:, c]
        for i in range(1 if q == 0 else 0, per):
            rs_send(0, q * per + i, first + lax.rem(chip_x + (1 - 2 * core) * i + per, per))
    for c in range(1, CH):
        loop(1, chips, lambda i: rs_send(c, i, to_chip(i)))
    for q in range(quarter):
        sent.append(functools.partial(lambda q: pair(q).wait_send(), q))
    for c in range(CH):
        sent.append(functools.partial(lambda c: round_sent(rs_out.at[c, pl.ds(0, others)], rs_s.at[c]), c))
        sent.append(functools.partial(lambda c: round_sent(gfull.at[core, c, pl.ds(0, others)], ag_s.at[c]), c))
        for b in range(batches + 1):
            sent.append(functools.partial(lambda c, b: forward(c, b, core).wait_send(), c, b))
    def spread_shard(c):
        loop(1, chips, lambda i: ag_send(c, i))
        forward(c, batches, core).start()

    energy = jnp.zeros((1, 1), F32)
    for c in range(CH):
        rs_in[c, 0] = rs_out[c, chip]
        round_got(rs_in.at[c, pl.ds(1, others)], rs_r.at[c])
        shard = rs_in[c, 0].astype(F32)
        for p in range(1, chips):
            shard = shard + rs_in[c, p].astype(F32)
        gfull[core, c, 0] = shard.astype(BF16)
        energy = energy + jnp.sum(jnp.sum(shard * shard, axis=1, keepdims=True), axis=0, keepdims=True)
        if c + 1 < CH:
            spread_shard(c)
    row = iota((8, 128), 0)
    tile = jnp.where(row == 0, energy, jnp.where(row == 1, num, jnp.where(row == 2, den, over)))

    sb_out[...] = tile
    both_cores = copy(sb_out, sb, sb_s.at[0], sb_r.at[0], sibling, z)
    both_cores.start()
    spread_shard(CH - 1)

    sent.append(both_cores.wait_send)

    def ag_pass(c, b):
        round_got(gfull.at[core, c, pl.ds(1 + b * batch, batch)], ag_r.at[c * batches + b])
        forward(c, b, core).start()

    both_cores.wait_recv()
    tile = tile + sb[...]
    ez_out[...] = tile
    z_round(ez_out, ez, ez_s.at[0], ez_r.at[0])
    ez[z] = tile
    z_got(ez, ez_r.at[0])
    etot = ez[0]
    for i in range(1, nz):
        etot = etot + ez[i]
    tile = jnp.where(row == 0, etot, tile)
    dt_out[...] = tile

    def tell(i):
        copy(dt_out, dt.at[i], dt_s.at[0], dt_r.at[0], to_chip(i) * 2 + core, z).start()

    loop(1, chips, tell)
    sent.append(lambda: round_sent(dt.at[pl.ds(1, others)], dt_s.at[0]))
    dt[0] = tile
    for c in range(CH):
        for b in range(batches):
            ag_pass(c, b)
    round_got(dt.at[pl.ds(1, others)], dt_r.at[0])
    total = dt[0]
    for i in range(1, chips):
        total = total + dt[i]
    entries = float(full_rows) * float(full_rows)
    factor = 0.5 * lax.rsqrt(total[0:1, 0:1] / entries + 1e-06)
    loss_out[...] = total[1:2, 0:1] / total[2:3, 0:1]
    flag_out[...] = total[3:4, 0:1]

    blk_rows = width // per

    def finish(h, c, i, p):
        at = (h * chips + p) * blk_rows + c * part_rows
        r = pl.ds(pl.multiple_of(at, part_rows), part_rows)
        out[r, :] = (proj[r, :].astype(F32) - gfull[h, c, i].astype(F32) * factor).astype(BF16)

    for c in range(CH):
        each(0, chips, lambda i: finish(core, c, i, from_chip(i)))
    for c in range(CH):
        for b in range(batches, -1, -1):
            forward(c, b, 1 - core).wait_recv()
        each(0, chips, lambda i: finish(1 - core, c, i, from_chip(i, True)))

    for wait in sent:
        wait()


def fast_step(nd, nz, feats, parent, counts, accepted, cand_ids, target_probs, gain, embed, proj):
    nodes, width = feats.shape
    full_rows = proj.shape[0]
    share = nodes // nd
    vocab = embed.shape[0]
    slots = nodes // 2
    chips = nd // 2
    quarter = nz // 2
    per = chips // quarter
    vm = pltpu.VMEM
    scratch = [
        vm(feats.shape, BF16),
        vm(embed.shape, BF16),
        vm(proj.shape, BF16),
        pltpu.SemaphoreType.DMA((3,)),
        vm((2, -(-vocab // 256) * 256, width), BF16),
        vm((nodes, nodes), BF16),
        vm((nodes, 128), BF16),
        vm((nodes, 128), F32),
        vm((nd, share // 2, 128), BF16),
        vm((nd, share // 2, 128), BF16),
        vm((nd, share, width), BF16),
        vm((nd, share, width), BF16),
        vm((2, slots, slots), BF16),
        vm((64, slots), F32),
        vm((chips, 8, CAPL), F32),
        vm((chips, 8, 128), F32),
        vm((chips, 8, 128), F32),
        vm((chips, CAPL, width), BF16),
        vm((chips, CAPL, width), BF16),
        vm((nz, slots, width), BF16),
        vm((nz, width, slots), BF16),
        vm((slots, width), F32),
        vm((slots, width), BF16),
        vm((chips // WIDE, slots, WIDE * CAPL), BF16),
        vm((chips // WIDE, 8, WIDE * CAPL), F32),
        vm((chips // GROUP, GROUP * CAPL, width), BF16),
        vm((8, 128), F32),
        vm((nz, 8, 128), F32),
        vm((chips // GROUP, 1, GROUP * CAPL), F32),
        vm((chips // GROUP, nz, 1, GROUP * CAPL), F32),
        vm((slots, width), BF16),
        vm((quarter, width, width), BF16),
        vm((quarter, width, width), BF16),
        vm((quarter, width, width), F32),
        vm((CH, chips, width // per // CH, width), BF16),
        vm((CH, chips, width // per // CH, width), BF16),
        vm((2, CH, chips, width // per // CH, width), BF16),
        vm((8, 128), F32),
        vm((8, 128), F32),
        vm((8, 128), F32),
        vm((nz, 8, 128), F32),
        vm((8, 128), F32),
        vm((chips, 8, 128), F32),
    ]
    dma = pltpu.SemaphoreType.DMA
    for count in (
        2, 2, 1, 1, 1, 1, 1, chips, 1, chips // GROUP,
        nz, nz, nz, nz, chips // GROUP, chips // GROUP, 1, 1, quarter, quarter,
        CH, CH, CH, BATCHES * CH, (BATCHES + 1) * CH, (BATCHES + 1) * CH, 1, 1, 1, 1, 1, 1,
    ):
        scratch.append(dma((count,)))
    in_vmem = pl.BlockSpec(memory_space=pltpu.VMEM)
    return pl.pallas_call(
        functools.partial(step_kernel, nd, nz, full_rows),
        out_shape=(
            jax.ShapeDtypeStruct(proj.shape, BF16),
            jax.ShapeDtypeStruct((1, 1), F32),
            jax.ShapeDtypeStruct((1, 1), F32),
        ),
        in_specs=[pl.BlockSpec(memory_space=pltpu.SMEM)] + [in_vmem] * 5 + [pl.BlockSpec(memory_space=pl.ANY)] * 3,
        out_specs=(in_vmem, in_vmem, in_vmem),
        scratch_shapes=scratch,
        compiler_params=pltpu.CompilerParams(
            collective_id=0, has_side_effects=True, vmem_limit_bytes=60 * 1024 * 1024
        ),
        name="step",
    )(
        counts, cand_ids.T, target_probs.T, parent.reshape(8, nodes // 8), accepted.reshape(8, nodes // 8),
        gain.reshape(2, width // 2), feats, embed, proj,
    )


def every(x, axis):
    n = lax.axis_size(axis)
    return lax.all_to_all(jnp.broadcast_to(x[None], (n,) + x.shape), axis, 0, 0, tiled=True)


def total(x, axis):
    return jnp.sum(every(jnp.atleast_1d(x), axis), axis=0).reshape(x.shape)


def wide_step(feats, parent, counts, accepted, cand_ids, target_probs, gain, embed, proj):
    node_rows, width_part = feats.shape
    full_width = proj.shape[0]
    group = lax.axis_index("dp")
    groups = lax.axis_size("dp")
    shard_rows = embed.shape[0]
    cand_count = cand_ids.shape[1]
    scale_in = 1.0 / jnp.sqrt(jnp.float32(full_width))
    gain_f = gain.astype(jnp.float32)
    flat_ids = cand_ids.reshape(-1)
    requests = flat_ids.shape[0]
    capacity = 3 * requests // (2 * groups)
    owners = flat_ids // shard_rows
    local_ids = flat_ids - owners * shard_rows
    member = owners[:, None] == jnp.arange(groups, dtype=jnp.int32)[None, :]
    per_owner = jnp.sum(member.astype(jnp.int32), axis=0)
    starts = jnp.cumsum(per_owner) - per_owner
    my_start = jnp.sum(jnp.where(member, starts[None, :], 0), axis=1)
    order = jnp.argsort(owners, stable=True)
    ranks = jnp.arange(requests, dtype=jnp.int32) - my_start[order]
    slots = owners[order] * capacity + ranks
    outgoing = jnp.zeros((groups * capacity,), jnp.int32).at[slots].set(local_ids[order])
    placed = jnp.zeros((requests,), jnp.int32).at[order].set(slots)
    mixed = (feats.astype(jnp.float32) + feats[parent].astype(jnp.float32)).astype(jnp.bfloat16)
    piece = every(mixed, "mp").transpose(1, 0, 2).reshape(node_rows, full_width)
    partial_value = jnp.dot(piece, proj, preferred_element_type=jnp.float32)
    whole = piece
    partial_value, whole = (partial_value, whole)
    hidden = partial_value * scale_in
    squares = total(jnp.sum(hidden * hidden, axis=1), "mp")
    recip = lax.rsqrt(squares / full_width + 1e-05)
    normed = (hidden * recip[:, None] * gain_f).astype(jnp.bfloat16)
    found = embed[
        lax.all_to_all(
            outgoing.reshape(groups, capacity), "dp", split_axis=0, concat_axis=0, tiled=True
        )
    ]
    fetched = lax.all_to_all(found, "dp", split_axis=0, concat_axis=0, tiled=True)
    cand_rows = fetched.reshape(groups * capacity, width_part)[placed].reshape(
        node_rows, cand_count, width_part
    )
    part_scores = jnp.einsum("nkd,nd->nk", cand_rows, normed, preferred_element_type=jnp.float32)
    scores = total(part_scores, "mp")
    logp = scores - jnp.log(jnp.sum(jnp.exp(scores), axis=1, keepdims=True))
    prob = jnp.exp(logp)
    probs = target_probs.astype(jnp.float32)
    target = probs / jnp.sum(probs, axis=1, keepdims=True)
    kl_node = jnp.sum(target * (jnp.log(target) - logp), axis=1)
    live_count = lax.dynamic_index_in_dim(counts, group, 0, keepdims=False)
    live = jnp.arange(node_rows, dtype=jnp.int32) < live_count
    weight = jnp.where(live, 1 + accepted, 0).astype(jnp.float32)
    num, den = total(jnp.stack([jnp.sum(weight * kl_node), jnp.sum(weight)]), "dp")
    grad_scores = weight[:, None] * (prob - target)
    dnormed = jnp.einsum("nk,nkd->nd", grad_scores, cand_rows, preferred_element_type=jnp.float32)
    inner = total(jnp.sum(dnormed * gain_f * hidden, axis=1), "mp")
    dhidden = (
        recip[:, None] * gain_f * dnormed - hidden * (recip**3 * inner / full_width)[:, None]
    ).astype(jnp.bfloat16)
    grad_part = (
        lax.dot_general(
            whole, dhidden, (((0,), (0,)), ((), ())), preferred_element_type=jnp.float32
        )
        * scale_in
    )
    shares = lax.all_to_all(grad_part.reshape(groups, -1, width_part), "dp", 0, 0, tiled=True)
    grad = every(jnp.sum(shares, axis=0), "dp").reshape(full_width, width_part)
    energy = total(jnp.sum(grad * grad), "mp")
    factor = lax.rsqrt(energy / (full_width * full_width) + 1e-06)
    new_proj = (proj.astype(jnp.float32) - 0.5 * grad * factor).astype(jnp.bfloat16)
    return (new_proj, num / den)


def solution(mesh):
    nd = mesh.shape["dp"]
    nz = mesh.shape["mp"]

    def per_device(*args):
        out, loss, flag = fast_step(nd, nz, *args)
        return lax.cond(
            flag[0, 0] > 0.0,
            lambda: wide_step(*args),
            lambda: (out, loss[0, 0]),
        )

    placed = (
        P("dp", "mp"),
        P("dp"),
        P(),
        P("dp"),
        P("dp", None),
        P("dp", None),
        P("mp"),
        P("dp", "mp"),
        P(None, "mp"),
    )
    return jax.shard_map(
        per_device, mesh=mesh, in_specs=placed, out_specs=(P(None, "mp"), P()), check_vma=False
    )
```
